128 devices in a mesh: probe: 4 (over z_lo, core), slab: 32 (over x, z_hi, y).
Axes of the slice: x: 4, y: 4, z: 4 (z_hi: 2, z_lo: 2; z = z_hi * 2 + z_lo), core: 2. Of those that a mesh axis runs over, the one named last changes fastest.
Arguments:
- probes: bfloat16 [8, 256, 256, 256], P('probe', 'slab'), may hold values from -3 to 3, as said below
- potential: float32 [256, 256, 256], P('slab'), may hold values from -0.4 to 0.4
- potential_change: float32 [256, 256, 256], P('slab'), may hold values from 0.2 to 1
- coefficients: float32 [3], replicated, may hold values from 0.5 to 1.5
Outputs:
- hartree_change: float32 [256, 256, 256], P('slab')
- moment_change: float32 [3], replicated
The draws below stay inside these ranges and needn't reach their ends.
Inputs may be any that keep to these rules, and one draw needn't show every extreme that they name: `probes`: every entry of a probe vector is plus or minus one amplitude shared by that whole vector, at least 1.
All inputs are finite; a program needn't handle non-finite values.
Results may differ from the reference program's by a relative error of at most 0.00035.
Values may be sent and summed in bfloat16 or wider, within the bound.
A program may use at most 192 MiB of HBM per device.

```python
import math
import jax
import jax.numpy as jnp
from jax import lax

NX = 256
NY = 256
NZ = 256
ORDER = 3
PROBES = 8


def draw_probes(key, part):
    key = jax.random.fold_in(key, 11)
    signs = jax.random.bernoulli(jax.random.fold_in(key, 1), 0.5, (PROBES, NZ, NY, NX))
    jitter = jax.random.uniform(jax.random.fold_in(key, 2), (PROBES,), jnp.float32)
    position = (jnp.arange(PROBES, dtype=jnp.float32) + jitter) / PROBES
    amplitude = jnp.exp(math.log(2.0) * position)
    values = jnp.where(signs, 1.0, -1.0).astype(jnp.float32) * amplitude[:, None, None, None]
    return values.astype(jnp.bfloat16)


def shaped_noise(key, power, shape):
    values = jax.random.uniform(key, shape, jnp.float32, -1.0, 1.0)
    return jnp.sign(values) * jnp.abs(values) ** power


def change_field(key, power):
    phase = jax.random.uniform(jax.random.fold_in(key, 101), (), jnp.float32, -0.3, 0.3)
    rough = shaped_noise(jax.random.fold_in(key, 102), power, (NZ, NY, NX))
    planes = jnp.arange(NZ, dtype=jnp.int32)
    turns = planes * (NZ // 8 - 1) % NZ
    angle = turns.astype(jnp.float32) * (2.0 * math.pi / NZ) + phase
    wave = jnp.sin(angle)
    return 0.6 + 0.12 * wave[:, None, None] + 0.28 * rough


def draw_potential(key, part):
    power = 1.0
    shared = change_field(key, power)
    key = jax.random.fold_in(key, 21)
    own = shaped_noise(jax.random.fold_in(key, 1), power, (NZ, NY, NX))
    return 0.5 * (shared - 0.6) + 0.2 * own


def draw_potential_change(key, part):
    power = 1.0
    return change_field(key, power)


def setup_inputs(seed: int = 0) -> dict:
    streams_of = jax.random.split(jax.random.key(seed), 5)
    probes = draw_probes(jax.random.fold_in(streams_of[4], 71), 0)
    potential = draw_potential(jax.random.fold_in(streams_of[4], 71), 0)
    potential_change = draw_potential_change(jax.random.fold_in(streams_of[4], 71), 0)
    coefficients = jnp.clip(jax.random.uniform(streams_of[3], (ORDER,), jnp.float32, 0.5, 1.5), 0.5, 1.5)
    return dict(probes=probes, potential=potential, potential_change=potential_change, coefficients=coefficients)


KINETIC = 1.0 / 12.0
CENTRE = 0.5
SCREEN = 0.05


def hamiltonian(field, potential):
    beside_all = jnp.roll(field, 1, -3) + jnp.roll(field, -1, -3)
    beside_all = beside_all + jnp.roll(field, 1, -2) + jnp.roll(field, -1, -2)
    beside_all = beside_all + jnp.roll(field, 1, -1) + jnp.roll(field, -1, -1)
    return KINETIC * (6.0 * field - beside_all) + (potential - CENTRE) * field


def signed_freq(count, size):
    values = jnp.arange(count, dtype=jnp.int32)
    return jnp.where(values <= size // 2, values, values - size)


def screened_kernel(planes, rows, cols):
    freq_z = signed_freq(planes, planes)
    freq_y = signed_freq(rows, rows)
    freq_x = signed_freq(cols, cols)
    wave_z = (freq_z.astype(jnp.float32) * (2.0 * math.pi / planes)) ** 2
    wave_y = (freq_y.astype(jnp.float32) * (2.0 * math.pi / rows)) ** 2
    wave_x = (freq_x.astype(jnp.float32) * (2.0 * math.pi / cols)) ** 2
    summed = wave_z[:, None, None] + wave_y[None, :, None] + wave_x[None, None, :]
    values = 4.0 * math.pi / (summed + SCREEN * SCREEN)
    anchor = (freq_z == 0)[:, None, None] & (freq_y == 0)[None, :, None] & (freq_x == 0)[None, None, :]
    return jnp.where(anchor, 0.0, values)


def reference(probes, potential, potential_change, coefficients):
    def one_probe(carry, probe):
        density, moments = carry
        vector = probe.astype(jnp.float32)
        current = hamiltonian(vector, potential)
        current_change = potential_change * vector
        density = density + coefficients[0] * vector * current_change
        terms = [jnp.sum(vector * current_change)]
        earlier = vector
        earlier_change = jnp.zeros_like(vector)
        for order_index in range(1, ORDER):
            following = 2.0 * hamiltonian(current, potential) - earlier
            following_change = 2.0 * (hamiltonian(current_change, potential) + potential_change * current) - earlier_change
            density = density + coefficients[order_index] * vector * following_change
            terms.append(jnp.sum(vector * following_change))
            earlier, earlier_change = current, current_change
            current, current_change = following, following_change
        return (density, moments + jnp.stack(terms)), None

    start = (jnp.zeros(potential.shape, jnp.float32), jnp.zeros((ORDER,), jnp.float32))
    (density, moments), unused = lax.scan(one_probe, start, probes)
    density = density / PROBES
    moment_change = moments / (PROBES * NZ * NY * NX)
    spectrum = jnp.fft.fftn(density) * screened_kernel(NZ, NY, NX)
    hartree_change = jnp.real(jnp.fft.ifftn(spectrum)).astype(jnp.float32)
    return hartree_change, moment_change.astype(jnp.float32)
```

```python
import functools
import math

import jax
import jax.numpy as jnp
import ml_dtypes
import numpy as np
from jax import lax
from jax.experimental import pallas as pl
from jax.experimental.pallas import tpu as pltpu
from jax.sharding import PartitionSpec as P

MESH = pl.DeviceIdType.MESH
F32 = jnp.float32
BF16 = jnp.bfloat16
KINETIC = 1.0 / 12.0
SCREEN = 0.05
CHUNK = 256
PAD = 8


def cas_split(size):
    index = np.arange(size)
    angle = (index[:, None] * index[None, :] % size) * (2.0 * np.pi / size)
    table = np.cos(angle) + np.sin(angle)
    high = table.astype(ml_dtypes.bfloat16)
    low = (table - high.astype(np.float64)).astype(ml_dtypes.bfloat16)
    return high, low


def shuffle(size):
    index = np.arange(size)
    return index % 8 * (size // 8) + index // 8


def tables(*pairs):
    return jnp.asarray(np.stack([part for pair in pairs for part in pair]))


def split(value):
    high = value.astype(BF16)
    low = (value - high.astype(F32)).astype(BF16)
    return high, low


def times_table(value, table):
    high, low = split(value)
    total = jnp.dot(high, table[0], preferred_element_type=F32)
    total = total + jnp.dot(high, table[1], preferred_element_type=F32)
    return total + jnp.dot(low, table[0], preferred_element_type=F32)


def table_times(table, value):
    high, low = split(value)
    total = jnp.dot(table[0], high, preferred_element_type=F32)
    total = total + jnp.dot(table[1], high, preferred_element_type=F32)
    return total + jnp.dot(table[0], low, preferred_element_type=F32)


def place():
    probe = lax.axis_index("probe")
    slab = lax.axis_index("slab")
    return probe, slab


def sibling_of(probe, slab):
    return {"probe": probe + 1 - 2 * lax.rem(probe, 2), "slab": slab}


def partner_of(probe, slab):
    return {"probe": lax.rem(probe + 2, 4), "slab": slab}


def greet(peers):
    barrier = pltpu.get_barrier_semaphore()
    for peer in peers:
        pl.semaphore_signal(barrier, inc=1, device_id=peer, device_id_type=MESH)
    pl.semaphore_wait(barrier, len(peers))


def remote(source, target, sems, index, peer):
    return pltpu.make_async_remote_copy(
        src_ref=source,
        dst_ref=target,
        send_sem=sems[0].at[index],
        recv_sem=sems[1].at[index],
        device_id=peer,
        device_id_type=MESH,
    )


def density_kernel(
    slabs,
    coef_ref, table_ref, probes_ref, pot_ref, change_ref,
    out_ref, moment_ref,
    tab, v16, pot, change, near, weight, v32, qbuf, tbuf, ubuf, dbuf, ybuf, rone, rtwo, mbuf,
    load_sems, halo_s, halo_r, fwd_s, fwd_r, one_s, one_r, two_s, two_r, mom_s, mom_r,
):
    probe, slab = place()
    core = lax.rem(probe, 2)
    zlow = probe // 2
    above = {"probe": probe, "slab": lax.rem(slab + 1, slabs)}
    below = {"probe": probe, "slab": lax.rem(slab + slabs - 1, slabs)}
    sibling = sibling_of(probe, slab)
    partner = partner_of(probe, slab)
    planes = probes_ref.shape[1]
    rows, cols = probes_ref.shape[2], probes_ref.shape[3]
    half = rows // 2
    mine = pl.ds(pl.multiple_of(core * half, half), half)
    other = pl.ds(pl.multiple_of((1 - core) * half, half), half)

    loads = [
        pltpu.make_async_copy(probes_ref, v16.at[:, 2 : planes + 2], load_sems.at[0]),
        pltpu.make_async_copy(change_ref, change.at[2 : planes + 2], load_sems.at[1]),
        pltpu.make_async_copy(pot_ref, pot.at[1 : planes + 1], load_sems.at[2]),
        pltpu.make_async_copy(table_ref, tab, load_sems.at[3]),
    ]
    for load in loads:
        load.start()
    greet([above, below, sibling, partner])
    halo = (halo_s, halo_r)
    copies = [
        remote(change_ref.at[planes - 2 : planes, mine], change.at[0:2, mine], halo, 0, above),
        remote(change_ref.at[0:2, mine], change.at[planes + 2 : planes + 4, mine], halo, 1, below),
        remote(pot_ref.at[planes - 1 : planes, mine], pot.at[0:1, mine], halo, 2, above),
        remote(pot_ref.at[0:1, mine], pot.at[planes + 1 : planes + 2, mine], halo, 3, below),
        remote(probes_ref.at[:, planes - 1 : planes], v16.at[:, 1:2], halo, 4, above),
        remote(probes_ref.at[:, 0:1], v16.at[:, planes + 2 : planes + 3], halo, 5, below),
        remote(probes_ref.at[:, planes - 2 : planes - 1], v16.at[:, 0:1], halo, 6, above),
        remote(probes_ref.at[:, 1:2], v16.at[:, planes + 3 : planes + 4], halo, 7, below),
    ]
    for copy in copies:
        copy.start()
    for load in loads:
        load.wait()

    def chunks(body):
        for index in range(rows // CHUNK):
            body(index * CHUNK)

    lanes = cols // 2
    lane = lax.broadcasted_iota(jnp.int32, (CHUNK, lanes), 1)
    at_low, at_high = lane == 0, lane == lanes - 1

    def seal(buffer, *lead):
        for side in range(2):
            buffer[(*lead, side, pl.ds(0, PAD))] = pltpu.roll(buffer[(*lead, side, pl.ds(rows, PAD))], 1, 0)
            buffer[(*lead, side, pl.ds(rows + PAD, PAD))] = pltpu.roll(buffer[(*lead, side, pl.ds(PAD, PAD))], PAD - 1, 0)

    stretch = rows // 8

    def widen(plane, with_pot):
        for step in range(8):
            here = pl.ds(step * stretch, stretch)
            spread = pl.ds(step, stretch, stride=8)
            inner = pl.ds(PAD + step, stretch, stride=8)
            local = change[plane, here]
            for side in range(2):
                part = slice(side * lanes, (side + 1) * lanes)
                weight[plane, side, spread, :] = local[:, part]
                if with_pot:
                    near[plane - 1, side, spread, :] = pot[plane - 1, here, part]
            for which in range(2):
                value = v16[which, plane, here].astype(F32)
                tangent = value * local
                for side in range(2):
                    part = slice(side * lanes, (side + 1) * lanes)
                    v32[which, plane, side, inner, :] = value[:, part]
                    qbuf[which, plane, side, inner, :] = tangent[:, part]
        for which in range(2):
            seal(v32, which, plane)
            seal(qbuf, which, plane)

    def beside(buffer, which, plane, row):
        inner = pl.ds(row + PAD, CHUNK)
        middle, total = [], []
        for side in range(2):
            wide = buffer[which, plane, side, pl.ds(row, CHUNK + 2 * PAD)]
            middle.append(wide[PAD : PAD + CHUNK])
            around = wide[:CHUNK] + wide[2 * PAD :]
            around = around + (buffer[which, plane - 1, side, inner] + buffer[which, plane + 1, side, inner])
            total.append(around)
        left = [pltpu.roll(value, 1, 1) for value in middle]
        right = [pltpu.roll(value, lanes - 1, 1) for value in middle]
        for side in range(2):
            beyond = jnp.where(at_low, left[1 - side], left[side])
            beyond = beyond + jnp.where(at_high, right[1 - side], right[side])
            total[side] = total[side] + beyond
        return middle, total

    def first(plane):
        def body(row):
            here = pl.ds(row, CHUNK)
            inner = pl.ds(row + PAD, CHUNK)
            for which in range(2):
                terms, around = beside(v32, which, plane + 1, row)
                tangents, beyond = beside(qbuf, which, plane + 1, row)
                for side in range(2):
                    local = near[plane, side, here]
                    term = local * terms[side] - KINETIC * around[side]
                    tbuf[which, plane, side, inner] = term
                    ubuf[which, plane, side, inner] = (
                        local * tangents[side] - KINETIC * beyond[side] + weight[plane + 1, side, here] * term
                    )

        chunks(body)
        for which in range(2):
            seal(tbuf, which, plane)
            seal(ubuf, which, plane)

    mbuf[0:2] = jnp.zeros((2, 24, cols), F32)

    def fold(value):
        total = value[0:8]
        for index in range(1, CHUNK // 8):
            total = total + value[8 * index : 8 * index + 8]
        return total

    def last(plane):
        def body(row):
            here = pl.ds(row, CHUNK)
            inner = pl.ds(row + PAD, CHUNK)
            sums = [None, None]
            for which in range(2):
                terms, around = beside(tbuf, which, plane + 1, row)
                mixes, beyond = beside(ubuf, which, plane + 1, row)
                for side in range(2):
                    local = near[plane + 1, side, here]
                    vector = v32[which, plane + 2, side, inner]
                    tangent = qbuf[which, plane + 2, side, inner]
                    image = local * terms[side] - KINETIC * around[side]
                    third = local * mixes[side] - KINETIC * beyond[side] + weight[plane + 2, side, here] * image
                    parts = (vector * tangent, vector * mixes[side], vector * (4.0 * third - 3.0 * tangent))
                    sums[side] = parts if sums[side] is None else tuple(a + b for a, b in zip(sums[side], parts))
            for side in range(2):
                for order in range(3):
                    mbuf[0, pl.ds(8 * order, 8), side * lanes : (side + 1) * lanes] += fold(sums[side][order])
                dbuf[plane, here, side * lanes : (side + 1) * lanes] = (
                    coef_ref[0] * sums[side][0] + (2.0 * coef_ref[1]) * sums[side][1] + coef_ref[2] * sums[side][2]
                )

        chunks(body)

    def hop_one(plane):
        return remote(ybuf.at[plane, 1 - core], rone.at[plane], (one_s, one_r), plane, sibling)

    def hop_two(plane):
        away = pl.ds(pl.multiple_of((1 - zlow) * half, half), half)
        return remote(ybuf.at[plane, core, away], rtwo.at[plane], (two_s, two_r), plane, partner)

    def transform(plane):
        value = times_table(dbuf[plane], tab.at[0:2])
        value = table_times(tab.at[2:4], value)
        ybuf[plane, 0] = value[:, :lanes]
        ybuf[plane, 1] = value[:, lanes:]
        hop_one(plane).start()

    def merge(plane):
        hop_one(plane).wait_recv()
        ybuf[plane, core] = ybuf[plane, core] + rone[plane]
        hop_two(plane).start()

    def loop(low, high, body):
        def step(index, carry):
            body(index)
            return carry

        lax.fori_loop(low, high, step, 0)

    def settle(plane):
        hop_two(plane).wait_recv()
        value = ybuf[plane, core, keep] + rtwo[plane]
        for row in range(per):
            spread = pl.ds(plane * per + row, slabs, stride=planes * per)
            out_ref[spread, :] = value[row * slabs : (row + 1) * slabs]

    keep = pl.ds(pl.multiple_of(zlow * half, half), half)
    per = half // slabs
    loop(2, planes + 2, functools.partial(widen, with_pot=True))
    loop(2, planes, first)
    loop(2, planes - 2, last)
    loop(2, planes - 2, transform)
    loop(2, planes - 2, merge)
    for copy in copies[:4]:
        copy.wait()
    fwd = (fwd_s, fwd_r)
    forwards = [
        remote(change.at[0:2, mine], change.at[0:2, mine], fwd, 0, sibling),
        remote(change.at[planes + 2 : planes + 4, mine], change.at[planes + 2 : planes + 4, mine], fwd, 1, sibling),
        remote(pot.at[0:1, mine], pot.at[0:1, mine], fwd, 2, sibling),
        remote(pot.at[planes + 1 : planes + 2, mine], pot.at[planes + 1 : planes + 2, mine], fwd, 3, sibling),
    ]
    for copy in forwards:
        copy.start()
    for plane in range(2, planes - 2):
        settle(plane)
    for copy in copies[4:6]:
        copy.wait()
    for copy in forwards:
        copy.wait()

    def both(body, low, high):
        def step(index, carry):
            body(jnp.where(index == 0, low, high))
            return carry

        lax.fori_loop(0, 2, step, 0)

    both(functools.partial(widen, with_pot=True), 1, planes + 2)
    both(first, 1, planes)
    both(last, 1, planes - 2)
    both(transform, 1, planes - 2)
    for copy in copies[6:]:
        copy.wait()
    both(functools.partial(widen, with_pot=False), 0, planes + 3)
    both(merge, 1, planes - 2)
    both(first, 0, planes + 1)
    both(last, 0, planes - 1)

    mom = (mom_s, mom_r)
    for order in range(3):
        strip = jnp.sum(mbuf[0, pl.ds(8 * order, 8)], axis=0, keepdims=True)
        total = jnp.sum(strip, axis=1, keepdims=True)
        mbuf[1, pl.ds(order, 1)] = jnp.broadcast_to(total, (1, cols))
    swap = remote(mbuf.at[1, 0:8], mbuf.at[2, 0:8], mom, 0, sibling)
    swap.start()
    both(transform, 0, planes - 1)
    swap.wait()
    mbuf[3, 0:8] = mbuf[1, 0:8] + mbuf[2, 0:8]
    swap = remote(mbuf.at[3, 0:8], mbuf.at[4, 0:8], mom, 1, partner)
    swap.start()
    both(merge, 0, planes - 1)
    settle(1)
    settle(planes - 2)
    swap.wait()
    moment_ref[...] = (mbuf[3, 0:8] + mbuf[4, 0:8])[:, :128]
    settle(0)
    settle(planes - 1)

    def drain(plane):
        hop_one(plane).wait_send()
        hop_two(plane).wait_send()

    loop(0, planes, drain)


def signed(index, size):
    return jnp.where(index <= size // 2, index, index - size).astype(F32) * (2.0 * math.pi / size)


def solve_kernel(
    slabs, planes, groups,
    ytable_ref, ztable_ref, a_ref, moment_ref,
    out_ref, total_ref,
    ytab, ztab, e_ref, rin, rout, back, far, kern, mslots, load_sems,
    in_s, in_r, out_s, out_r, far_s, far_r, e_s, e_r, mom_s, mom_r,
):
    probe, slab = place()
    core = lax.rem(probe, 2)
    zlow = probe // 2
    sibling = sibling_of(probe, slab)
    partner = partner_of(probe, slab)
    depth = planes * slabs
    rows = ytable_ref.shape[1]
    half = rows // 2
    per = half // slabs
    size = planes * per
    loads = [
        pltpu.make_async_copy(ytable_ref, ytab, load_sems.at[0]),
        pltpu.make_async_copy(ztable_ref, ztab, load_sems.at[1]),
    ]
    for load in loads:
        load.start()
    barrier = pltpu.get_barrier_semaphore()

    def greeting(step, carry):
        peer = {"probe": probe, "slab": lax.rem(slab + step, slabs)}
        pl.semaphore_signal(barrier, inc=1, device_id=peer, device_id_type=MESH)
        return carry

    lax.fori_loop(1, slabs, greeting, 0)
    pl.semaphore_signal(barrier, inc=1, device_id=sibling, device_id_type=MESH)
    pl.semaphore_signal(barrier, inc=1, device_id=partner, device_id_type=MESH)
    pl.semaphore_wait(barrier, slabs + 1)

    def block(index):
        return pl.ds(pl.multiple_of(index * size, size), size)

    def sender(source, target, sems, step):
        peer = lax.rem(slab + step, slabs)
        return remote(source.at[block(peer)], target.at[block(slab)], sems, step, {"probe": probe, "slab": peer})

    def receiver(source, target, sems, step):
        peer = lax.rem(slab + slabs - step, slabs)
        return remote(source.at[block(peer)], target.at[block(peer)], sems, step, {"probe": probe, "slab": peer})

    def exchange_start(source, target, sems):
        def start(step, carry):
            sender(source, target, sems, step).start()
            return carry

        lax.fori_loop(1, slabs, start, 0)
        target[block(slab)] = source[block(slab)]

    def exchange_recv(source, target, sems):
        def finish(step, carry):
            receiver(source, target, sems, step).wait_recv()
            return carry

        lax.fori_loop(1, slabs, finish, 0)

    def exchange_sent(source, target, sems):
        def finish(step, carry):
            sender(source, target, sems, step).wait_send()
            return carry

        lax.fori_loop(1, slabs, finish, 0)

    def moment_round(number):
        stride, count = groups[number]
        where = lax.rem(slab // stride, count)
        copies = []
        for step in range(1, count):
            peer = slab + (lax.rem(where + step, count) - where) * stride
            copies.append(
                remote(
                    mslots.at[number, where], mslots.at[number, where],
                    (mom_s.at[number], mom_r.at[number]), step, {"probe": probe, "slab": peer},
                )
            )
        waits = []
        for step in range(1, count):
            source = lax.rem(where + count - step, count)
            peer = slab + (source - where) * stride
            waits.append(
                remote(
                    mslots.at[number, source], mslots.at[number, source],
                    (mom_s.at[number], mom_r.at[number]), step, {"probe": probe, "slab": peer},
                )
            )
        return where, count, copies, waits

    def moment_start(number, value):
        where, count, copies, waits = moment_round(number)
        mslots[number, where] = value
        for copy in copies:
            copy.start()

    def moment_finish(number):
        where, count, copies, waits = moment_round(number)
        for copy in waits:
            copy.wait_recv()
        for copy in copies:
            copy.wait_send()
        total = mslots[number, 0]
        for index in range(1, count):
            total = total + mslots[number, index]
        return total

    ins, outs = (in_s, in_r), (out_s, out_r)
    exchange_start(a_ref, rin, ins)
    moment_start(0, moment_ref[...])

    wave_z = signed(lax.broadcasted_iota(jnp.int32, (depth, 128), 0), depth)
    wave_x = signed(lax.broadcasted_iota(jnp.int32, (depth, 128), 1) + core * 128, 256)
    base = wave_z * wave_z + wave_x * wave_x
    for row in range(per):
        number = zlow * half + row * slabs + slab
        wave_y = signed(jnp.full((depth, 128), number, jnp.int32), rows)
        summed = base + wave_y * wave_y
        value = (4.0 * math.pi / (8.0 * depth * rows * 256)) / (summed + SCREEN * SCREEN)
        kern[:, row * 128 : (row + 1) * 128] = jnp.where(summed == 0.0, 0.0, value)

    for load in loads:
        load.wait()
    exchange_recv(a_ref, rin, ins)
    moments = moment_finish(0)
    columns = jnp.concatenate([rin[pl.ds(row, depth, stride=per), :] for row in range(per)], axis=1)
    columns = table_times(ztab, columns) * kern[...]
    columns = table_times(ztab, columns)
    for row in range(per):
        rout[pl.ds(row, depth, stride=per), :] = columns[:, row * 128 : (row + 1) * 128]

    exchange_start(rout, back, outs)
    for number in range(1, len(groups)):
        moment_start(number, moments)
        moments = moment_finish(number)
    total_ref[...] = moments
    exchange_recv(rout, back, outs)
    across = remote(back, far, (far_s, far_r), 0, partner)
    across.start()
    across.wait()

    def share(plane):
        return remote(e_ref.at[core, plane], e_ref.at[core, plane], (e_s, e_r), plane, sibling)

    def arrival(plane):
        return remote(e_ref.at[1 - core, plane], e_ref.at[1 - core, plane], (e_s, e_r), plane, sibling)

    for plane in range(planes):
        own = [back[pl.ds(plane * per + row, slabs, stride=size), :] for row in range(per)]
        away = [far[pl.ds(plane * per + row, slabs, stride=size), :] for row in range(per)]
        own = jnp.concatenate(own, axis=0)
        away = jnp.concatenate(away, axis=0)
        low = jnp.where(zlow == 0, own, away)
        high = jnp.where(zlow == 0, away, own)
        e_ref[core, plane] = table_times(ytab, jnp.concatenate([low, high], axis=0))
        share(plane).start()

    def settle(plane, carry):
        arrival(plane).wait_recv()
        share(plane).wait_send()
        value = jnp.concatenate([e_ref[0, plane], e_ref[1, plane]], axis=1)
        out_ref[plane] = times_table(value, ytab)
        return carry

    lax.fori_loop(0, planes, settle, 0)
    exchange_sent(a_ref, rin, ins)
    exchange_sent(rout, back, outs)


def groups_of(slabs):
    return {32: ((1, 4), (4, 2), (8, 4)), 4: ((1, 2), (2, 2))}[slabs]


def per_device(probes, potential, potential_change, coefficients):
    panel, planes, rows, cols = probes.shape
    slabs = lax.axis_size("slab")
    depth = planes * slabs
    half = rows // 2
    per = half // slabs
    vmem = pl.BlockSpec(memory_space=pltpu.VMEM)
    anywhere = pl.BlockSpec(memory_space=pl.ANY)
    dma = pltpu.SemaphoreType.DMA
    high, low = cas_split(rows)
    order = shuffle(rows)
    forward = tables((high, low), (high[:, order], low[:, order]))
    inverse = tables((high, low))
    deep = tables(cas_split(depth))
    tall = rows + 2 * PAD
    spectrum, moments = pl.pallas_call(
        functools.partial(density_kernel, slabs),
        out_shape=(
            jax.ShapeDtypeStruct((planes * half, 128), F32),
            jax.ShapeDtypeStruct((8, 128), F32),
        ),
        in_specs=[pl.BlockSpec(memory_space=pltpu.SMEM), anywhere, anywhere, anywhere, anywhere],
        out_specs=(vmem, vmem),
        scratch_shapes=[
            pltpu.VMEM((4, rows, cols), BF16),
            pltpu.VMEM((panel, planes + 4, rows, cols), BF16),
            pltpu.VMEM((planes + 2, rows, cols), F32),
            pltpu.VMEM((planes + 4, rows, cols), F32),
            pltpu.VMEM((planes + 2, 2, rows, 128), F32),
            pltpu.VMEM((planes + 4, 2, rows, 128), F32),
            pltpu.VMEM((panel, planes + 4, 2, tall, 128), F32),
            pltpu.VMEM((panel, planes + 4, 2, tall, 128), F32),
            pltpu.VMEM((panel, planes + 2, 2, tall, 128), F32),
            pltpu.VMEM((panel, planes + 2, 2, tall, 128), F32),
            pltpu.VMEM((planes, rows, cols), F32),
            pltpu.VMEM((planes, 2, rows, 128), F32),
            pltpu.VMEM((planes, rows, 128), F32),
            pltpu.VMEM((planes, half, 128), F32),
            pltpu.VMEM((5, 24, cols), F32),
            dma((4,)),
            dma((8,)), dma((8,)),
            dma((4,)), dma((4,)),
            dma((planes,)), dma((planes,)),
            dma((planes,)), dma((planes,)),
            dma((2,)), dma((2,)),
        ],
        compiler_params=pltpu.CompilerParams(
            collective_id=0, has_side_effects=True, vmem_limit_bytes=56 * 1024 * 1024
        ),
        name="density",
    )(coefficients, forward, probes, potential, potential_change)
    groups = groups_of(slabs)
    hartree_change, total = pl.pallas_call(
        functools.partial(solve_kernel, slabs, planes, groups),
        out_shape=(
            jax.ShapeDtypeStruct((planes, rows, cols), F32),
            jax.ShapeDtypeStruct((8, 128), F32),
        ),
        in_specs=[anywhere, anywhere, vmem, vmem],
        out_specs=(vmem, vmem),
        scratch_shapes=[
            pltpu.VMEM((2, rows, cols), BF16),
            pltpu.VMEM((2, depth, depth), BF16),
            pltpu.VMEM((2, planes, rows, 128), F32),
            pltpu.VMEM((planes * half, 128), F32),
            pltpu.VMEM((planes * half, 128), F32),
            pltpu.VMEM((planes * half, 128), F32),
            pltpu.VMEM((planes * half, 128), F32),
            pltpu.VMEM((depth, per * 128), F32),
            pltpu.VMEM((len(groups), 4, 8, 128), F32),
            dma((2,)),
            dma((slabs,)), dma((slabs,)),
            dma((slabs,)), dma((slabs,)),
            dma((1,)), dma((1,)),
            dma((planes,)), dma((planes,)),
            dma((len(groups), 4)), dma((len(groups), 4)),
        ],
        compiler_params=pltpu.CompilerParams(
            collective_id=1, has_side_effects=True, vmem_limit_bytes=32 * 1024 * 1024
        ),
        name="solve",
    )(inverse, deep, spectrum, moments)
    weights = jnp.array([1.0, 2.0, 1.0], F32) / (panel * lax.axis_size("probe") * depth * rows * cols)
    return hartree_change, total[:3, 0] * weights


def solution(mesh):
    return jax.shard_map(
        per_device,
        mesh=mesh,
        in_specs=(
            P("probe", "slab", None, None),
            P("slab", None, None),
            P("slab", None, None),
            P(),
        ),
        out_specs=(P("slab", None, None), P()),
        check_vma=False,
    )
```

```python
import functools
import math

import jax
import jax.numpy as jnp
import ml_dtypes
import numpy as np
from jax import lax
from jax.experimental import pallas as pl
from jax.experimental.pallas import tpu as pltpu
from jax.sharding import PartitionSpec as P

MESH = pl.DeviceIdType.MESH
F32 = jnp.float32
BF16 = jnp.bfloat16
KINETIC = 1.0 / 12.0
SCREEN = 0.05
PAD = 8


def cas_split(size):
    index = np.arange(size)
    angle = (index[:, None] * index[None, :] % size) * (2.0 * np.pi / size)
    table = np.cos(angle) + np.sin(angle)
    high = table.astype(ml_dtypes.bfloat16)
    low = (table - high.astype(np.float64)).astype(ml_dtypes.bfloat16)
    return high, low


def shuffle(size):
    index = np.arange(size)
    return index % 8 * (size // 8) + index // 8


def tables(*pairs):
    return jnp.asarray(np.stack([part for pair in pairs for part in pair]))


def split(value):
    high = value.astype(BF16)
    low = (value - high.astype(F32)).astype(BF16)
    return high, low


def times_table(value, table):
    high, low = split(value)
    total = jnp.dot(high, table[0], preferred_element_type=F32)
    total = total + jnp.dot(high, table[1], preferred_element_type=F32)
    return total + jnp.dot(low, table[0], preferred_element_type=F32)


def table_times(table, value):
    high, low = split(value)
    total = jnp.dot(table[0], high, preferred_element_type=F32)
    total = total + jnp.dot(table[1], high, preferred_element_type=F32)
    return total + jnp.dot(table[0], low, preferred_element_type=F32)


def place():
    probe = lax.axis_index("probe")
    slab = lax.axis_index("slab")
    return probe, slab


def sibling_of(probe, slab):
    return {"probe": probe + 1 - 2 * lax.rem(probe, 2), "slab": slab}


def partner_of(probe, slab):
    return {"probe": lax.rem(probe + 2, 4), "slab": slab}


def greet(peers):
    barrier = pltpu.get_barrier_semaphore()
    for peer in peers:
        pl.semaphore_signal(barrier, inc=1, device_id=peer, device_id_type=MESH)
    pl.semaphore_wait(barrier, len(peers))


def remote(source, target, sems, index, peer):
    return pltpu.make_async_remote_copy(
        src_ref=source,
        dst_ref=target,
        send_sem=sems[0].at[index],
        recv_sem=sems[1].at[index],
        device_id=peer,
        device_id_type=MESH,
    )


def density_kernel(
    slabs,
    coef_ref, table_ref, probes_ref, pot_ref, change_ref,
    out_ref, moment_ref,
    tab, v16, pot, change, ghost_in, near, weight, v32, qbuf, tbuf, ubuf, dbuf,
    pair_out, pair_in, ybuf, rone, rtwo, mbuf,
    load_sems, halo_s, halo_r, fwd_s, fwd_r, pair_s, pair_r, one_s, one_r, two_s, two_r, mom_s, mom_r,
):
    probe, slab = place()
    core = lax.rem(probe, 2)
    zlow = probe // 2
    above = {"probe": probe, "slab": lax.rem(slab + 1, slabs)}
    below = {"probe": probe, "slab": lax.rem(slab + slabs - 1, slabs)}
    sibling = sibling_of(probe, slab)
    partner = partner_of(probe, slab)
    planes = probes_ref.shape[1]
    rows, cols = probes_ref.shape[2], probes_ref.shape[3]
    half = rows // 2
    mine = pl.ds(pl.multiple_of(core * half, half), half)

    loads = [
        pltpu.make_async_copy(change_ref, change, load_sems.at[0]),
        pltpu.make_async_copy(pot_ref, pot, load_sems.at[1]),
        pltpu.make_async_copy(probes_ref, v16.at[:, 1 : planes + 1], load_sems.at[2]),
        pltpu.make_async_copy(table_ref, tab, load_sems.at[3]),
    ]
    for load in loads:
        load.start()
    greet([above, below, sibling, partner])
    halo = (halo_s, halo_r)
    copies = [
        remote(probes_ref.at[:, planes - 1 : planes], v16.at[:, 0:1], halo, 0, above),
        remote(probes_ref.at[:, 0:1], v16.at[:, planes + 1 : planes + 2], halo, 1, below),
    ]
    for copy in copies:
        copy.start()
    edges = (
        (change_ref, planes - 1, above),
        (change_ref, 0, below),
        (pot_ref, planes - 1, above),
        (pot_ref, 0, below),
    )
    for index, (field, plane, peer) in enumerate(edges):
        copy = remote(field.at[plane, mine], ghost_in.at[index, mine], halo, 2 + index, peer)
        copy.start()
        copies.append(copy)
    for load in loads:
        load.wait()

    lanes = cols // 2
    lane = lax.broadcasted_iota(jnp.int32, (rows, lanes), 1)
    at_low, at_high = lane == 0, lane == lanes - 1
    inner = pl.ds(PAD, rows)

    def seal(buffer, *lead):
        for side in range(2):
            buffer[(*lead, side, pl.ds(0, PAD))] = pltpu.roll(buffer[(*lead, side, pl.ds(rows, PAD))], 1, 0)
            buffer[(*lead, side, pl.ds(rows + PAD, PAD))] = pltpu.roll(buffer[(*lead, side, pl.ds(PAD, PAD))], PAD - 1, 0)

    stretch = rows // 8

    def widen(plane, ghost=None):
        for step in range(8):
            here = pl.ds(step * stretch, stretch)
            spread = pl.ds(step, stretch, stride=8)
            wide = pl.ds(PAD + step, stretch, stride=8)
            if ghost is None:
                local, level = change[plane - 1, here], pot[plane - 1, here]
            else:
                local, level = ghost_in[ghost, here], ghost_in[2 + ghost, here]
            for side in range(2):
                part = slice(side * lanes, (side + 1) * lanes)
                weight[plane, side, spread, :] = local[:, part]
                near[plane, side, spread, :] = level[:, part]
            for which in range(2):
                value = v16[which, plane, here].astype(F32)
                tangent = value * local
                for side in range(2):
                    part = slice(side * lanes, (side + 1) * lanes)
                    v32[which, plane, side, wide, :] = value[:, part]
                    qbuf[which, plane, side, wide, :] = tangent[:, part]
        for which in range(2):
            seal(v32, which, plane)
            seal(qbuf, which, plane)

    def beside(buffer, which, plane, steps):
        middle, total = [], []
        for side in range(2):
            tall = buffer[which, plane, side]
            middle.append(tall[PAD : PAD + rows])
            around = tall[:rows] + tall[2 * PAD :]
            for step in steps:
                around = around + buffer[which, plane + step, side, inner]
            total.append(around)
        left = [pltpu.roll(value, 1, 1) for value in middle]
        right = [pltpu.roll(value, lanes - 1, 1) for value in middle]
        for side in range(2):
            beyond = jnp.where(at_low, left[1 - side], left[side])
            beyond = beyond + jnp.where(at_high, right[1 - side], right[side])
            total[side] = total[side] + beyond
        return middle, total

    def first(plane, steps=(-1, 1)):
        for which in range(2):
            terms, around = beside(v32, which, plane, steps)
            tangents, beyond = beside(qbuf, which, plane, steps)
            for side in range(2):
                local = near[plane, side]
                term = local * terms[side] - KINETIC * around[side]
                tbuf[which, plane, side, inner] = term
                ubuf[which, plane, side, inner] = (
                    local * tangents[side] - KINETIC * beyond[side] + weight[plane, side] * term
                )
        for which in range(2):
            seal(tbuf, which, plane)
            seal(ubuf, which, plane)

    mbuf[0:2] = jnp.zeros((2, 24, cols), F32)

    def fold(value):
        total = value[0:8]
        for index in range(1, rows // 8):
            total = total + value[8 * index : 8 * index + 8]
        return total

    def count(order, side, value):
        mbuf[0, pl.ds(8 * order, 8), side * lanes : (side + 1) * lanes] += fold(value)

    def last(plane):
        sums = [None, None]
        for which in range(2):
            terms, around = beside(tbuf, which, plane, (-1, 1))
            mixes, beyond = beside(ubuf, which, plane, (-1, 1))
            for side in range(2):
                local = near[plane, side]
                vector = v32[which, plane, side, inner]
                tangent = qbuf[which, plane, side, inner]
                image = local * terms[side] - KINETIC * around[side]
                third = local * mixes[side] - KINETIC * beyond[side] + weight[plane, side] * image
                parts = (vector * tangent, vector * mixes[side], vector * (4.0 * third - 3.0 * tangent))
                sums[side] = parts if sums[side] is None else tuple(a + b for a, b in zip(sums[side], parts))
        for side in range(2):
            for order in range(3):
                count(order, side, sums[side][order])
            dbuf[plane, :, side * lanes : (side + 1) * lanes] = (
                coef_ref[0] * sums[side][0] + (2.0 * coef_ref[1]) * sums[side][1] + coef_ref[2] * sums[side][2]
            )

    def pairs(target, planes_of):
        low, mid, high = planes_of
        for side in range(2):
            product = v32[0, low, side, inner] * v32[0, high, side, inner]
            product = product + v32[1, low, side, inner] * v32[1, high, side, inner]
            total = weight[low, side] + weight[mid, side] + weight[high, side]
            value = (4.0 * KINETIC * KINETIC) * total * product
            count(2, side, value)
            pair_out[target, :, side * lanes : (side + 1) * lanes] = (coef_ref[2] * value).astype(BF16)

    def hop_one(plane):
        return remote(ybuf.at[plane, 1 - core], rone.at[plane], (one_s, one_r), plane, sibling)

    def hop_two(plane):
        away = pl.ds(pl.multiple_of((1 - zlow) * half, half), half)
        return remote(ybuf.at[plane, core, away], rtwo.at[plane], (two_s, two_r), plane, partner)

    def transform(plane):
        value = times_table(dbuf[plane], tab.at[0:2])
        value = table_times(tab.at[2:4], value)
        ybuf[plane, 0] = value[:, :lanes]
        ybuf[plane, 1] = value[:, lanes:]
        hop_one(plane).start()

    def merge(plane):
        hop_one(plane).wait_recv()
        ybuf[plane, core] = ybuf[plane, core] + rone[plane]
        hop_two(plane).start()

    keep = pl.ds(pl.multiple_of(zlow * half, half), half)
    per = half // slabs

    def settle(plane):
        hop_two(plane).wait_recv()
        value = ybuf[plane, core, keep] + rtwo[plane]
        for row in range(per):
            spread = pl.ds((plane - 1) * per + row, slabs, stride=planes * per)
            out_ref[spread, :] = value[row * slabs : (row + 1) * slabs]

    def loop(low, high, body):
        def step(index, carry):
            body(index)
            return carry

        lax.fori_loop(low, high, step, 0)

    def both(body, low, high):
        def step(index, carry):
            body(jnp.where(index == 0, low, high))
            return carry

        lax.fori_loop(0, 2, step, 0)

    loop(1, planes + 1, widen)
    loop(2, planes, first)
    loop(3, planes - 1, last)
    loop(3, planes - 1, transform)
    loop(3, planes - 1, merge)
    for copy in copies[2:]:
        copy.wait()
    fwd = (fwd_s, fwd_r)
    forwards = [
        remote(ghost_in.at[index, mine], ghost_in.at[index, mine], fwd, index, sibling) for index in range(4)
    ]
    for copy in forwards:
        copy.start()
    for copy in copies[:2]:
        copy.wait()
    for copy in forwards:
        copy.wait()
    widen(0, 0)
    widen(planes + 1, 1)
    pairs(0, (0, 1, 2))
    pairs(1, (planes - 1, planes, planes + 1))
    trades = [
        remote(pair_out.at[0], pair_in.at[1], (pair_s, pair_r), 0, below),
        remote(pair_out.at[1], pair_in.at[0], (pair_s, pair_r), 1, above),
    ]
    for copy in trades:
        copy.start()
    both(first, 1, planes)
    both(last, 2, planes - 1)
    both(transform, 2, planes - 1)
    first(0, (1,))
    first(planes + 1, (-1,))
    both(merge, 2, planes - 1)
    both(last, 1, planes)

    mom = (mom_s, mom_r)
    for order in range(3):
        strip = jnp.sum(mbuf[0, pl.ds(8 * order, 8)], axis=0, keepdims=True)
        total = jnp.sum(strip, axis=1, keepdims=True)
        mbuf[1, pl.ds(order, 1)] = jnp.broadcast_to(total, (1, cols))
    swap = remote(mbuf.at[1, 0:8], mbuf.at[2, 0:8], mom, 0, sibling)
    swap.start()
    for copy in trades:
        copy.wait()
    dbuf[1] += pair_in[0].astype(F32)
    dbuf[planes] += pair_in[1].astype(F32)
    both(transform, 1, planes)
    for plane in range(3, planes - 1):
        settle(plane)
    swap.wait()
    mbuf[3, 0:8] = mbuf[1, 0:8] + mbuf[2, 0:8]
    swap = remote(mbuf.at[3, 0:8], mbuf.at[4, 0:8], mom, 1, partner)
    swap.start()
    both(merge, 1, planes)
    settle(2)
    settle(planes - 1)
    swap.wait()
    moment_ref[...] = (mbuf[3, 0:8] + mbuf[4, 0:8])[:, :128]
    settle(1)
    settle(planes)

    def drain(plane):
        hop_one(plane).wait_send()
        hop_two(plane).wait_send()

    loop(1, planes + 1, drain)


def signed(index, size):
    return jnp.where(index <= size // 2, index, index - size).astype(F32) * (2.0 * math.pi / size)


def solve_kernel(
    slabs, planes, groups,
    ytable_ref, ztable_ref, a_ref, moment_ref,
    out_ref, total_ref,
    ytab, ztab, e_ref, rin, rout, back, far, kern, mslots, load_sems,
    in_s, in_r, out_s, out_r, far_s, far_r, e_s, e_r, mom_s, mom_r,
):
    probe, slab = place()
    core = lax.rem(probe, 2)
    zlow = probe // 2
    sibling = sibling_of(probe, slab)
    partner = partner_of(probe, slab)
    depth = planes * slabs
    rows = ytable_ref.shape[1]
    half = rows // 2
    per = half // slabs
    size = planes * per
    loads = [
        pltpu.make_async_copy(ytable_ref, ytab, load_sems.at[0]),
        pltpu.make_async_copy(ztable_ref, ztab, load_sems.at[1]),
    ]
    for load in loads:
        load.start()
    barrier = pltpu.get_barrier_semaphore()

    def greeting(step, carry):
        peer = {"probe": probe, "slab": lax.rem(slab + step, slabs)}
        pl.semaphore_signal(barrier, inc=1, device_id=peer, device_id_type=MESH)
        return carry

    lax.fori_loop(1, slabs, greeting, 0)
    pl.semaphore_signal(barrier, inc=1, device_id=sibling, device_id_type=MESH)
    pl.semaphore_signal(barrier, inc=1, device_id=partner, device_id_type=MESH)
    pl.semaphore_wait(barrier, slabs + 1)

    def block(index):
        return pl.ds(pl.multiple_of(index * size, size), size)

    def sender(source, target, sems, step):
        peer = lax.rem(slab + step, slabs)
        return remote(source.at[block(peer)], target.at[block(slab)], sems, step, {"probe": probe, "slab": peer})

    def receiver(source, target, sems, step):
        peer = lax.rem(slab + slabs - step, slabs)
        return remote(source.at[block(peer)], target.at[block(peer)], sems, step, {"probe": probe, "slab": peer})

    def exchange_start(source, target, sems):
        def start(step, carry):
            sender(source, target, sems, step).start()
            return carry

        lax.fori_loop(1, slabs, start, 0)
        target[block(slab)] = source[block(slab)]

    def exchange_recv(source, target, sems):
        def finish(step, carry):
            receiver(source, target, sems, step).wait_recv()
            return carry

        lax.fori_loop(1, slabs, finish, 0)

    def exchange_sent(source, target, sems):
        def finish(step, carry):
            sender(source, target, sems, step).wait_send()
            return carry

        lax.fori_loop(1, slabs, finish, 0)

    def moment_round(number):
        stride, count = groups[number]
        where = lax.rem(slab // stride, count)
        copies = []
        for step in range(1, count):
            peer = slab + (lax.rem(where + step, count) - where) * stride
            copies.append(
                remote(
                    mslots.at[number, where], mslots.at[number, where],
                    (mom_s.at[number], mom_r.at[number]), step, {"probe": probe, "slab": peer},
                )
            )
        waits = []
        for step in range(1, count):
            source = lax.rem(where + count - step, count)
            peer = slab + (source - where) * stride
            waits.append(
                remote(
                    mslots.at[number, source], mslots.at[number, source],
                    (mom_s.at[number], mom_r.at[number]), step, {"probe": probe, "slab": peer},
                )
            )
        return where, count, copies, waits

    def moment_start(number, value):
        where, count, copies, waits = moment_round(number)
        mslots[number, where] = value
        for copy in copies:
            copy.start()

    def moment_finish(number):
        where, count, copies, waits = moment_round(number)
        for copy in waits:
            copy.wait_recv()
        for copy in copies:
            copy.wait_send()
        total = mslots[number, 0]
        for index in range(1, count):
            total = total + mslots[number, index]
        return total

    ins, outs = (in_s, in_r), (out_s, out_r)
    exchange_start(a_ref, rin, ins)
    moment_start(0, moment_ref[...])

    wave_z = signed(lax.broadcasted_iota(jnp.int32, (depth, 128), 0), depth)
    wave_x = signed(lax.broadcasted_iota(jnp.int32, (depth, 128), 1) + core * 128, 256)
    base = wave_z * wave_z + wave_x * wave_x
    for row in range(per):
        number = zlow * half + row * slabs + slab
        wave_y = signed(jnp.full((depth, 128), number, jnp.int32), rows)
        summed = base + wave_y * wave_y
        value = (4.0 * math.pi / (8.0 * depth * rows * 256)) / (summed + SCREEN * SCREEN)
        kern[:, row * 128 : (row + 1) * 128] = jnp.where(summed == 0.0, 0.0, value)

    for load in loads:
        load.wait()
    exchange_recv(a_ref, rin, ins)
    moments = moment_finish(0)
    columns = jnp.concatenate([rin[pl.ds(row, depth, stride=per), :] for row in range(per)], axis=1)
    columns = table_times(ztab, columns) * kern[...]
    columns = table_times(ztab, columns)
    for row in range(per):
        rout[pl.ds(row, depth, stride=per), :] = columns[:, row * 128 : (row + 1) * 128]

    exchange_start(rout, back, outs)
    for number in range(1, len(groups)):
        moment_start(number, moments)
        moments = moment_finish(number)
    total_ref[...] = moments
    exchange_recv(rout, back, outs)
    across = remote(back, far, (far_s, far_r), 0, partner)
    across.start()
    across.wait()

    def share(plane):
        return remote(e_ref.at[core, plane], e_ref.at[core, plane], (e_s, e_r), plane, sibling)

    def arrival(plane):
        return remote(e_ref.at[1 - core, plane], e_ref.at[1 - core, plane], (e_s, e_r), plane, sibling)

    for plane in range(planes):
        own = [back[pl.ds(plane * per + row, slabs, stride=size), :] for row in range(per)]
        away = [far[pl.ds(plane * per + row, slabs, stride=size), :] for row in range(per)]
        own = jnp.concatenate(own, axis=0)
        away = jnp.concatenate(away, axis=0)
        low = jnp.where(zlow == 0, own, away)
        high = jnp.where(zlow == 0, away, own)
        e_ref[core, plane] = table_times(ytab, jnp.concatenate([low, high], axis=0))
        share(plane).start()

    def settle(plane, carry):
        arrival(plane).wait_recv()
        share(plane).wait_send()
        value = jnp.concatenate([e_ref[0, plane], e_ref[1, plane]], axis=1)
        out_ref[plane] = times_table(value, ytab)
        return carry

    lax.fori_loop(0, planes, settle, 0)
    exchange_sent(a_ref, rin, ins)
    exchange_sent(rout, back, outs)


def groups_of(slabs):
    return {32: ((1, 4), (4, 2), (8, 4)), 4: ((1, 2), (2, 2))}[slabs]


def per_device(probes, potential, potential_change, coefficients):
    panel, planes, rows, cols = probes.shape
    slabs = lax.axis_size("slab")
    depth = planes * slabs
    half = rows // 2
    per = half // slabs
    vmem = pl.BlockSpec(memory_space=pltpu.VMEM)
    anywhere = pl.BlockSpec(memory_space=pl.ANY)
    dma = pltpu.SemaphoreType.DMA
    high, low = cas_split(rows)
    order = shuffle(rows)
    forward = tables((high, low), (high[:, order], low[:, order]))
    inverse = tables((high, low))
    deep = tables(cas_split(depth))
    tall = rows + 2 * PAD
    spectrum, moments = pl.pallas_call(
        functools.partial(density_kernel, slabs),
        out_shape=(
            jax.ShapeDtypeStruct((planes * half, 128), F32),
            jax.ShapeDtypeStruct((8, 128), F32),
        ),
        in_specs=[pl.BlockSpec(memory_space=pltpu.SMEM), anywhere, anywhere, anywhere, anywhere],
        out_specs=(vmem, vmem),
        scratch_shapes=[
            pltpu.VMEM((4, rows, cols), BF16),
            pltpu.VMEM((panel, planes + 2, rows, cols), BF16),
            pltpu.VMEM((planes, rows, cols), F32),
            pltpu.VMEM((planes, rows, cols), F32),
            pltpu.VMEM((4, rows, cols), F32),
            pltpu.VMEM((planes + 2, 2, rows, 128), F32),
            pltpu.VMEM((planes + 2, 2, rows, 128), F32),
            pltpu.VMEM((panel, planes + 2, 2, tall, 128), F32),
            pltpu.VMEM((panel, planes + 2, 2, tall, 128), F32),
            pltpu.VMEM((panel, planes + 2, 2, tall, 128), F32),
            pltpu.VMEM((panel, planes + 2, 2, tall, 128), F32),
            pltpu.VMEM((planes + 1, rows, cols), F32),
            pltpu.VMEM((2, rows, cols), BF16),
            pltpu.VMEM((2, rows, cols), BF16),
            pltpu.VMEM((planes + 1, 2, rows, 128), F32),
            pltpu.VMEM((planes + 1, rows, 128), F32),
            pltpu.VMEM((planes + 1, half, 128), F32),
            pltpu.VMEM((5, 24, cols), F32),
            dma((4,)),
            dma((6,)), dma((6,)),
            dma((4,)), dma((4,)),
            dma((2,)), dma((2,)),
            dma((planes + 1,)), dma((planes + 1,)),
            dma((planes + 1,)), dma((planes + 1,)),
            dma((2,)), dma((2,)),
        ],
        compiler_params=pltpu.CompilerParams(
            collective_id=0, has_side_effects=True, vmem_limit_bytes=56 * 1024 * 1024
        ),
        name="density",
    )(coefficients, forward, probes, potential, potential_change)
    groups = groups_of(slabs)
    hartree_change, total = pl.pallas_call(
        functools.partial(solve_kernel, slabs, planes, groups),
        out_shape=(
            jax.ShapeDtypeStruct((planes, rows, cols), F32),
            jax.ShapeDtypeStruct((8, 128), F32),
        ),
        in_specs=[anywhere, anywhere, vmem, vmem],
        out_specs=(vmem, vmem),
        scratch_shapes=[
            pltpu.VMEM((2, rows, cols), BF16),
            pltpu.VMEM((2, depth, depth), BF16),
            pltpu.VMEM((2, planes, rows, 128), F32),
            pltpu.VMEM((planes * half, 128), F32),
            pltpu.VMEM((planes * half, 128), F32),
            pltpu.VMEM((planes * half, 128), F32),
            pltpu.VMEM((planes * half, 128), F32),
            pltpu.VMEM((depth, per * 128), F32),
            pltpu.VMEM((len(groups), 4, 8, 128), F32),
            dma((2,)),
            dma((slabs,)), dma((slabs,)),
            dma((slabs,)), dma((slabs,)),
            dma((1,)), dma((1,)),
            dma((planes,)), dma((planes,)),
            dma((len(groups), 4)), dma((len(groups), 4)),
        ],
        compiler_params=pltpu.CompilerParams(
            collective_id=1, has_side_effects=True, vmem_limit_bytes=32 * 1024 * 1024
        ),
        name="solve",
    )(inverse, deep, spectrum, moments)
    weights = jnp.array([1.0, 2.0, 1.0], F32) / (panel * lax.axis_size("probe") * depth * rows * cols)
    return hartree_change, total[:3, 0] * weights


def solution(mesh):
    return jax.shard_map(
        per_device,
        mesh=mesh,
        in_specs=(
            P("probe", "slab", None, None),
            P("slab", None, None),
            P("slab", None, None),
            P(),
        ),
        out_specs=(P("slab", None, None), P()),
        check_vma=False,
    )
```

```python
import functools
import math

import jax
import jax.numpy as jnp
import ml_dtypes
import numpy as np
from jax import lax
from jax.experimental import pallas as pl
from jax.experimental.pallas import tpu as pltpu
from jax.sharding import PartitionSpec as P

MESH = pl.DeviceIdType.MESH
F32 = jnp.float32
BF16 = jnp.bfloat16
KINETIC = 1.0 / 12.0
SCREEN = 0.05
PAD = 8


def cas_split(size):
    index = np.arange(size)
    angle = (index[:, None] * index[None, :] % size) * (2.0 * np.pi / size)
    table = np.cos(angle) + np.sin(angle)
    high = table.astype(ml_dtypes.bfloat16)
    low = (table - high.astype(np.float64)).astype(ml_dtypes.bfloat16)
    return high, low


def shuffle(size):
    index = np.arange(size)
    return index % 8 * (size // 8) + index // 8


def tables(*pairs):
    return jnp.asarray(np.stack([part for pair in pairs for part in pair]))


def split(value):
    high = value.astype(BF16)
    low = (value - high.astype(F32)).astype(BF16)
    return high, low


def times_table(value, table):
    high, low = split(value)
    total = jnp.dot(high, table[0], preferred_element_type=F32)
    total = total + jnp.dot(high, table[1], preferred_element_type=F32)
    return total + jnp.dot(low, table[0], preferred_element_type=F32)


def table_times(table, value):
    high, low = split(value)
    total = jnp.dot(table[0], high, preferred_element_type=F32)
    total = total + jnp.dot(table[1], high, preferred_element_type=F32)
    return total + jnp.dot(table[0], low, preferred_element_type=F32)


def place():
    probe = lax.axis_index("probe")
    slab = lax.axis_index("slab")
    return probe, slab


def sibling_of(probe, slab):
    return {"probe": probe + 1 - 2 * lax.rem(probe, 2), "slab": slab}


def partner_of(probe, slab):
    return {"probe": lax.rem(probe + 2, 4), "slab": slab}


def greet(peers, count, layer_peer):
    barrier = pltpu.get_barrier_semaphore()
    for peer in peers:
        pl.semaphore_signal(barrier, inc=1, device_id=peer, device_id_type=MESH)

    def signal(step, carry):
        pl.semaphore_signal(barrier, inc=1, device_id=layer_peer(step), device_id_type=MESH)
        return carry

    lax.fori_loop(1, count, signal, 0)
    pl.semaphore_wait(barrier, len(peers) + count - 1)


def remote(source, target, sems, index, peer):
    return pltpu.make_async_remote_copy(
        src_ref=source,
        dst_ref=target,
        send_sem=sems[0].at[index],
        recv_sem=sems[1].at[index],
        device_id=peer,
        device_id_type=MESH,
    )


def signed(index, size):
    return jnp.where(index <= size // 2, index, index - size).astype(F32) * (2.0 * math.pi / size)


def response_kernel(
    slabs, layer,
    coef_ref, table_ref, ztable_ref, probes_ref, pot_ref, change_ref,
    out_ref, moment_ref,
    tab, v16, pot, change, ghost_in, near, weight, v32, qbuf, tbuf, ubuf, dbuf,
    pair_out, pair_in, ybuf, rone, rtwo, gsend, rgate, mbuf,
    ztab, abuf, rin, kern, rout, hold, quads, ebuf, mslots,
    load_sems, halo_s, halo_r, fwd_s, fwd_r, pair_s, pair_r, one_s, one_r, two_s, two_r, gate_s, gate_r, mom_s, mom_r,
    in_s, in_r, out_s, out_r, near_s, near_r, far_s, far_r, relay_s, relay_r, e_s, e_r, mslot_s, mslot_r,
):
    probe, slab = place()
    core = lax.rem(probe, 2)
    zlow = probe // 2
    above = {"probe": probe, "slab": lax.rem(slab + 1, slabs)}
    below = {"probe": probe, "slab": lax.rem(slab + slabs - 1, slabs)}
    sibling = sibling_of(probe, slab)
    partner = partner_of(probe, slab)
    zhigh = lax.rem(slab // 4, 2)
    spot = slab // 8 * 4 + lax.rem(slab, 4)
    across = {"probe": lax.rem(probe + 2, 4), "slab": slab + 4 - 8 * zhigh}

    def spot_after(step):
        return lax.rem(spot + step, layer)

    def layer_peer(step):
        other = spot_after(step)
        return {"probe": probe, "slab": other // 4 * 8 + zhigh * 4 + lax.rem(other, 4)}

    planes = probes_ref.shape[1]
    rows, cols = probes_ref.shape[2], probes_ref.shape[3]
    half = rows // 2
    mine = pl.ds(pl.multiple_of(core * half, half), half)

    loads = [
        pltpu.make_async_copy(change_ref, change, load_sems.at[0]),
        pltpu.make_async_copy(pot_ref, pot, load_sems.at[1]),
        pltpu.make_async_copy(probes_ref, v16.at[:, 1 : planes + 1], load_sems.at[2]),
        pltpu.make_async_copy(table_ref, tab, load_sems.at[3]),
        pltpu.make_async_copy(ztable_ref, ztab, load_sems.at[4]),
    ]
    for load in loads:
        load.start()
    greet([above, below, sibling, partner, across], layer, layer_peer)
    halo = (halo_s, halo_r)
    copies = [
        remote(probes_ref.at[:, planes - 1 : planes], v16.at[:, 0:1], halo, 0, above),
        remote(probes_ref.at[:, 0:1], v16.at[:, planes + 1 : planes + 2], halo, 1, below),
    ]
    for copy in copies:
        copy.start()
    edges = (
        (change_ref, planes - 1, above),
        (change_ref, 0, below),
        (pot_ref, planes - 1, above),
        (pot_ref, 0, below),
    )
    for index, (field, plane, peer) in enumerate(edges):
        copy = remote(field.at[plane, mine], ghost_in.at[index, mine], halo, 2 + index, peer)
        copy.start()
        copies.append(copy)
    for load in loads[:4]:
        load.wait()

    lanes = cols // 2
    lane = lax.broadcasted_iota(jnp.int32, (rows, lanes), 1)
    at_low, at_high = lane == 0, lane == lanes - 1
    inner = pl.ds(PAD, rows)

    def seal(buffer, *lead):
        for side in range(2):
            buffer[(*lead, side, pl.ds(0, PAD))] = pltpu.roll(buffer[(*lead, side, pl.ds(rows, PAD))], 1, 0)
            buffer[(*lead, side, pl.ds(rows + PAD, PAD))] = pltpu.roll(buffer[(*lead, side, pl.ds(PAD, PAD))], PAD - 1, 0)

    stretch = rows // 8

    def widen(plane, ghost=None):
        for step in range(8):
            here = pl.ds(step * stretch, stretch)
            spread = pl.ds(step, stretch, stride=8)
            wide = pl.ds(PAD + step, stretch, stride=8)
            if ghost is None:
                local, level = change[plane - 1, here], pot[plane - 1, here]
            else:
                local, level = ghost_in[ghost, here], ghost_in[2 + ghost, here]
            for side in range(2):
                part = slice(side * lanes, (side + 1) * lanes)
                weight[plane, side, spread, :] = local[:, part]
                near[plane, side, spread, :] = level[:, part]
            for which in range(2):
                value = v16[which, plane, here].astype(F32)
                tangent = value * local
                for side in range(2):
                    part = slice(side * lanes, (side + 1) * lanes)
                    v32[which, plane, side, wide, :] = value[:, part]
                    qbuf[which, plane, side, wide, :] = tangent[:, part]
        for which in range(2):
            seal(v32, which, plane)
            seal(qbuf, which, plane)

    def beside(buffer, which, plane, steps):
        middle, total = [], []
        for side in range(2):
            tall = buffer[which, plane, side]
            middle.append(tall[PAD : PAD + rows])
            around = tall[:rows] + tall[2 * PAD :]
            for step in steps:
                around = around + buffer[which, plane + step, side, inner]
            total.append(around)
        left = [pltpu.roll(value, 1, 1) for value in middle]
        right = [pltpu.roll(value, lanes - 1, 1) for value in middle]
        for side in range(2):
            beyond = jnp.where(at_low, left[1 - side], left[side])
            beyond = beyond + jnp.where(at_high, right[1 - side], right[side])
            total[side] = total[side] + beyond
        return middle, total

    def first(plane, steps=(-1, 1)):
        for which in range(2):
            terms, around = beside(v32, which, plane, steps)
            tangents, beyond = beside(qbuf, which, plane, steps)
            for side in range(2):
                local = near[plane, side]
                term = local * terms[side] - KINETIC * around[side]
                tbuf[which, plane, side, inner] = term
                ubuf[which, plane, side, inner] = (
                    local * tangents[side] - KINETIC * beyond[side] + weight[plane, side] * term
                )
        for which in range(2):
            seal(tbuf, which, plane)
            seal(ubuf, which, plane)

    mbuf[0:2] = jnp.zeros((2, 24, cols), F32)

    def fold(value):
        total = value[0:8]
        for index in range(1, rows // 8):
            total = total + value[8 * index : 8 * index + 8]
        return total

    def count(order, side, value):
        mbuf[0, pl.ds(8 * order, 8), side * lanes : (side + 1) * lanes] += fold(value)

    def last(plane):
        sums = [None, None]
        for which in range(2):
            terms, around = beside(tbuf, which, plane, (-1, 1))
            mixes, beyond = beside(ubuf, which, plane, (-1, 1))
            for side in range(2):
                local = near[plane, side]
                vector = v32[which, plane, side, inner]
                tangent = qbuf[which, plane, side, inner]
                image = local * terms[side] - KINETIC * around[side]
                third = local * mixes[side] - KINETIC * beyond[side] + weight[plane, side] * image
                parts = (vector * tangent, vector * mixes[side], vector * (4.0 * third - 3.0 * tangent))
                sums[side] = parts if sums[side] is None else tuple(a + b for a, b in zip(sums[side], parts))
        for side in range(2):
            for order in range(3):
                count(order, side, sums[side][order])
            dbuf[plane, :, side * lanes : (side + 1) * lanes] = (
                coef_ref[0] * sums[side][0] + (2.0 * coef_ref[1]) * sums[side][1] + coef_ref[2] * sums[side][2]
            )

    def pairs(target, planes_of):
        low, mid, high = planes_of
        for side in range(2):
            product = v32[0, low, side, inner] * v32[0, high, side, inner]
            product = product + v32[1, low, side, inner] * v32[1, high, side, inner]
            total = weight[low, side] + weight[mid, side] + weight[high, side]
            value = (4.0 * KINETIC * KINETIC) * total * product
            count(2, side, value)
            pair_out[target, :, side * lanes : (side + 1) * lanes] = (coef_ref[2] * value).astype(BF16)

    def hop_one(plane):
        return remote(ybuf.at[plane, 1 - core], rone.at[plane], (one_s, one_r), plane, sibling)

    fourth = rows // 4
    per = fourth // layer
    depth = planes * slabs
    size = 2 * planes * per

    def quarter(low, high):
        return pl.ds(pl.multiple_of((2 * low + high) * fourth, fourth), fourth)

    def hop_two(plane):
        return remote(
            ybuf.at[plane, core, quarter(1 - zlow, zhigh)], rtwo.at[plane, 0], (two_s.at[0], two_r.at[0]), plane, partner
        )

    def hop_pass(plane):
        return remote(
            ybuf.at[plane, core, quarter(zlow, 1 - zhigh)], rtwo.at[plane, 1], (two_s.at[1], two_r.at[1]), plane, partner
        )

    def hop_gate(plane):
        return remote(gsend.at[plane], rgate.at[plane], (gate_s, gate_r), plane, across)

    def transform(group):
        count = len(group)
        value = jnp.concatenate([dbuf[plane] for plane in group], axis=0)
        value = times_table(value, tab.at[0:2])
        value = jnp.concatenate([value[index * rows : (index + 1) * rows] for index in range(count)], axis=1)
        value = table_times(tab.at[2:4], value)
        for index, plane in enumerate(group):
            ybuf[plane, 0] = value[:, index * cols : index * cols + lanes]
            ybuf[plane, 1] = value[:, index * cols + lanes : (index + 1) * cols]
            hop_one(plane).start()

    def merge(plane):
        hop_one(plane).wait_recv()
        ybuf[plane, core] = ybuf[plane, core] + rone[plane]
        hop_pass(plane).start()
        hop_two(plane).start()

    def relay(plane):
        hop_pass(plane).wait_recv()
        gsend[plane] = ybuf[plane, core, quarter(1 - zlow, 1 - zhigh)] + rtwo[plane, 1]
        hop_gate(plane).start()

    inside = list(range(3, planes - 1))
    outside = [1, 2, planes - 1, planes]

    def spread(plane, which, value):
        group = inside if plane in inside else outside
        first_row = (0 if plane in inside else size // 2) + group.index(plane) * per
        for row in range(per):
            start = first_row + which * (size // 4) + row
            abuf[pl.ds(start, layer, stride=size), :] = value[row * layer : (row + 1) * layer]

    def settle(plane):
        hop_two(plane).wait_recv()
        spread(plane, zhigh, ybuf[plane, core, quarter(zlow, zhigh)] + rtwo[plane, 0])

    def collect(plane):
        hop_gate(plane).wait_recv()
        spread(plane, 1 - zhigh, rgate[plane])

    def in_rows(place_of, piece):
        return pl.ds(pl.multiple_of(place_of * size + piece * (size // 2), size // 2), size // 2)

    def in_copy(step, piece, here):
        rows_at = in_rows(spot_after(step), piece)
        return remote(abuf.at[rows_at], rin.at[here], (in_s.at[piece], in_r.at[piece]), step, layer_peer(step))

    def in_start(piece):
        def start(step, carry):
            in_copy(step, piece, in_rows(spot, piece)).start()
            return carry

        lax.fori_loop(1, layer, start, 0)
        rin[in_rows(spot, piece)] = abuf[in_rows(spot, piece)]

    def in_finish(piece):
        def finish(step, carry):
            in_copy(step, piece, in_rows(spot_after(layer - step), piece)).wait_recv()
            return carry

        lax.fori_loop(1, layer, finish, 0)

    def loop(low, high, body):
        def step(index, carry):
            body(index)
            return carry

        lax.fori_loop(low, high, step, 0)

    def both(body, low, high):
        def step(index, carry):
            body(jnp.where(index == 0, low, high))
            return carry

        lax.fori_loop(0, 2, step, 0)

    loop(1, planes + 1, widen)
    loop(2, planes, first)
    loop(3, planes - 1, last)
    transform(inside)
    loop(3, planes - 1, merge)
    for copy in copies[2:]:
        copy.wait()
    fwd = (fwd_s, fwd_r)
    forwards = [
        remote(ghost_in.at[index, mine], ghost_in.at[index, mine], fwd, index, sibling) for index in range(4)
    ]
    for copy in forwards:
        copy.start()
    loop(3, planes - 1, relay)
    for copy in copies[:2]:
        copy.wait()
    for copy in forwards:
        copy.wait()
    widen(0, 0)
    widen(planes + 1, 1)
    pairs(0, (0, 1, 2))
    pairs(1, (planes - 1, planes, planes + 1))
    trades = [
        remote(pair_out.at[0], pair_in.at[1], (pair_s, pair_r), 0, below),
        remote(pair_out.at[1], pair_in.at[0], (pair_s, pair_r), 1, above),
    ]
    for copy in trades:
        copy.start()
    both(first, 1, planes)
    for plane in inside:
        settle(plane)
    both(last, 2, planes - 1)
    transform([2, planes - 1])
    for plane in inside:
        collect(plane)
    in_start(0)
    first(0, (1,))
    first(planes + 1, (-1,))
    both(merge, 2, planes - 1)
    both(last, 1, planes)

    mom = (mom_s, mom_r)
    for order in range(3):
        strip = jnp.sum(mbuf[0, pl.ds(8 * order, 8)], axis=0, keepdims=True)
        total = jnp.sum(strip, axis=1, keepdims=True)
        mbuf[1, pl.ds(order, 1)] = jnp.broadcast_to(total, (1, cols))
    swap = remote(mbuf.at[1, 0:8], mbuf.at[2, 0:8], mom, 0, sibling)
    swap.start()
    both(relay, 2, planes - 1)
    for copy in trades:
        copy.wait()
    dbuf[1] += pair_in[0].astype(F32)
    dbuf[planes] += pair_in[1].astype(F32)
    transform([1, planes])
    settle(2)
    settle(planes - 1)
    swap.wait()
    mbuf[3, 0:8] = mbuf[1, 0:8] + mbuf[2, 0:8]
    swap = remote(mbuf.at[3, 0:8], mbuf.at[4, 0:8], mom, 1, partner)
    swap.start()
    both(merge, 1, planes)
    both(relay, 1, planes)
    collect(2)
    collect(planes - 1)
    settle(1)
    settle(planes)
    collect(1)
    collect(planes)
    in_start(1)
    swap.wait()
    mbuf[5, 0:8] = mbuf[3, 0:8] + mbuf[4, 0:8]
    swap = remote(mbuf.at[5, 0:8], mbuf.at[6, 0:8], mom, 2, across)
    swap.start()

    wave_z = signed(lax.broadcasted_iota(jnp.int32, (depth, lanes), 0), depth)
    wave_x = signed(lax.broadcasted_iota(jnp.int32, (depth, lanes), 1) + core * lanes, cols)
    base = wave_z * wave_z + wave_x * wave_x
    for row in range(per):
        number = (2 * zlow + zhigh) * fourth + row * layer + spot
        wave_y = signed(jnp.full((depth, lanes), number, jnp.int32), rows)
        summed = base + wave_y * wave_y
        value = (4.0 * math.pi / (8.0 * depth * rows * cols)) / (summed + SCREEN * SCREEN)
        kern[:, row * lanes : (row + 1) * lanes] = jnp.where(summed == 0.0, 0.0, value)
    loads[4].wait()

    def moment_round(number, stride):
        where = lax.rem(slab // stride, 4)
        copies, waits = [], []
        for step in range(1, 4):
            peer = {"probe": probe, "slab": slab + (lax.rem(where + step, 4) - where) * stride}
            source = lax.rem(where + 4 - step, 4)
            sems = (mslot_s.at[number], mslot_r.at[number])
            copies.append(remote(mslots.at[number, where], mslots.at[number, where], sems, step, peer))
            waits.append(remote(mslots.at[number, source], mslots.at[number, source], sems, step, peer))
        return where, copies, waits

    def moment_start(number, stride, value):
        where, copies, waits = moment_round(number, stride)
        mslots[number, where] = value
        for copy in copies:
            copy.start()

    def moment_finish(number, stride):
        where, copies, waits = moment_round(number, stride)
        for copy in waits:
            copy.wait_recv()
        for copy in copies:
            copy.wait_send()
        return (mslots[number, 0] + mslots[number, 1]) + (mslots[number, 2] + mslots[number, 3])

    in_finish(0)
    swap.wait()
    moment_start(0, 1, (mbuf[5, 0:8] + mbuf[6, 0:8])[:, :128])
    in_finish(1)
    columns = jnp.concatenate([rin[pl.ds(row, depth, stride=per), :] for row in range(per)], axis=1)
    here = lax.broadcasted_iota(jnp.int32, (1, per * lanes), 1) + (probe + slab) * (per * lanes)
    mean = jnp.sum(columns, axis=0, keepdims=True) * (1.0 / depth)
    columns = columns - jnp.where(here == 0, mean, 0.0)
    columns = table_times(ztab.at[0:2], columns) * kern[...]
    columns = table_times(ztab.at[2:4], columns)
    for row in range(per):
        rout[pl.ds(row, depth, stride=per), :] = columns[:, row * lanes : (row + 1) * lanes]

    piece = planes // 2 * per
    own_quarter = 2 * zlow + zhigh
    far_quarter = 2 * (1 - zlow) + (1 - zhigh)

    def out_rows(place_of, side, part):
        which = zhigh if side == 0 else 1 - zhigh
        return pl.ds(pl.multiple_of(place_of * size + which * (size // 2) + part * piece, piece), piece)

    def landing(side, part, place_of):
        rows_at = pl.ds(pl.multiple_of(place_of * piece, piece), piece)
        return quads.at[own_quarter, part, rows_at] if side == 0 else hold.at[part, rows_at]

    def out_copy(step, side, part, place_of):
        source = rout.at[out_rows(spot_after(step), side, part)]
        sems = (out_s.at[side, part], out_r.at[side, part])
        return remote(source, landing(side, part, place_of), sems, step, layer_peer(step))

    def out_start(side, part):
        def start(step, carry):
            out_copy(step, side, part, spot).start()
            return carry

        lax.fori_loop(1, layer, start, 0)
        target = landing(side, part, spot)
        target[...] = rout[out_rows(spot, side, part)]

    def out_finish(side, part):
        def finish(step, carry):
            out_copy(step, side, part, spot_after(layer - step)).wait_recv()
            return carry

        lax.fori_loop(1, layer, finish, 0)

    def to_partner(part):
        return remote(quads.at[own_quarter, part], quads.at[own_quarter, part], (near_s, near_r), part, partner)

    def to_across(part):
        return remote(hold.at[part], quads.at[own_quarter, part], (far_s, far_r), part, across)

    def pass_on(part):
        return remote(quads.at[far_quarter, part], quads.at[far_quarter, part], (relay_s, relay_r), part, partner)

    for part in range(2):
        out_start(0, part)
        out_start(1, part)
    moments = moment_finish(0, 1)
    moment_start(1, 8, moments)
    for part in range(2):
        out_finish(0, part)
        to_partner(part).start()
        out_finish(1, part)
        to_across(part).start()
    moment_ref[...] = moment_finish(1, 8)
    for part in range(2):
        to_across(part).wait_recv()
        pass_on(part).start()

    def share(part):
        return remote(ebuf.at[core, part], ebuf.at[core, part], (e_s, e_r), part, sibling)

    def invert(part):
        to_partner(part).wait_recv()
        pass_on(part).wait_recv()
        columns = []
        for plane in range(planes // 2):
            blocks = [
                quads[which, part, pl.ds(plane * per + row, layer, stride=piece), :]
                for which in range(4)
                for row in range(per)
            ]
            columns.append(jnp.concatenate(blocks, axis=0))
        ebuf[core, part] = table_times(tab.at[0:2], jnp.concatenate(columns, axis=1))
        share(part).start()

    def finish(part):
        share(part).wait_recv()
        value = [
            jnp.concatenate([ebuf[side, part, :, plane * lanes : (plane + 1) * lanes] for side in range(2)], axis=1)
            for plane in range(planes // 2)
        ]
        value = times_table(jnp.concatenate(value, axis=0), tab.at[0:2])
        for plane in range(planes // 2):
            out_ref[part * (planes // 2) + plane] = value[plane * rows : (plane + 1) * rows]

    invert(0)
    finish(0)
    invert(1)
    finish(1)

    def drain(plane):
        hop_one(plane).wait_send()
        hop_two(plane).wait_send()
        hop_pass(plane).wait_send()
        hop_gate(plane).wait_send()

    loop(1, planes + 1, drain)

    def sent(step, carry):
        for part in range(2):
            in_copy(step, part, in_rows(spot, part)).wait_send()
            for side in range(2):
                out_copy(step, side, part, spot).wait_send()
        return carry

    lax.fori_loop(1, layer, sent, 0)
    for part in range(2):
        to_partner(part).wait_send()
        to_across(part).wait_send()
        pass_on(part).wait_send()
        share(part).wait_send()


def per_device(probes, potential, potential_change, coefficients):
    panel, planes, rows, cols = probes.shape
    slabs = lax.axis_size("slab")
    layer = slabs // 2
    depth = planes * slabs
    fourth = rows // 4
    size = 2 * planes * (fourth // layer)
    vmem = pl.BlockSpec(memory_space=pltpu.VMEM)
    anywhere = pl.BlockSpec(memory_space=pl.ANY)
    dma = pltpu.SemaphoreType.DMA
    high, low = cas_split(rows)
    order = shuffle(rows)
    forward = tables((high, low), (high[:, order], low[:, order]))
    high, low = cas_split(depth)
    spots = np.arange(layer)[:, None, None, None] // 4 * 8 + np.arange(layer)[:, None, None, None] % 4
    halves = np.arange(2)[None, None, :, None] * 4
    inner = np.array([list(range(2, planes - 2)), [0, 1, planes - 2, planes - 1]])[None, :, None, :]
    came = ((spots + halves) * planes + inner).reshape(-1)
    goes = ((spots[:, 0] + halves[:, 0]) * planes + np.arange(planes)).reshape(-1)
    deep = tables((high[:, came], low[:, came]), (high[goes], low[goes]))
    tall = rows + 2 * PAD
    hartree_change, total = pl.pallas_call(
        functools.partial(response_kernel, slabs, layer),
        out_shape=(
            jax.ShapeDtypeStruct((planes, rows, cols), F32),
            jax.ShapeDtypeStruct((8, 128), F32),
        ),
        in_specs=[pl.BlockSpec(memory_space=pltpu.SMEM)] + [anywhere] * 5,
        out_specs=(vmem, vmem),
        scratch_shapes=[
            pltpu.VMEM((4, rows, cols), BF16),
            pltpu.VMEM((panel, planes + 2, rows, cols), BF16),
            pltpu.VMEM((planes, rows, cols), F32),
            pltpu.VMEM((planes, rows, cols), F32),
            pltpu.VMEM((4, rows, cols), F32),
            pltpu.VMEM((planes + 2, 2, rows, 128), F32),
            pltpu.VMEM((planes + 2, 2, rows, 128), F32),
            pltpu.VMEM((panel, planes + 2, 2, tall, 128), F32),
            pltpu.VMEM((panel, planes + 2, 2, tall, 128), F32),
            pltpu.VMEM((panel, planes + 2, 2, tall, 128), F32),
            pltpu.VMEM((panel, planes + 2, 2, tall, 128), F32),
            pltpu.VMEM((planes + 1, rows, cols), F32),
            pltpu.VMEM((2, rows, cols), BF16),
            pltpu.VMEM((2, rows, cols), BF16),
            pltpu.VMEM((planes + 1, 2, rows, 128), F32),
            pltpu.VMEM((planes + 1, rows, 128), F32),
            pltpu.VMEM((planes + 1, 2, fourth, 128), F32),
            pltpu.VMEM((planes + 1, fourth, 128), F32),
            pltpu.VMEM((planes + 1, fourth, 128), F32),
            pltpu.VMEM((7, 24, cols), F32),
            pltpu.VMEM((4, depth, depth), BF16),
            pltpu.VMEM((layer * size, 128), F32),
            pltpu.VMEM((layer * size, 128), F32),
            pltpu.VMEM((depth, 4 * 128), F32),
            pltpu.VMEM((layer * size, 128), F32),
            pltpu.VMEM((2, layer * size // 4, 128), F32),
            pltpu.VMEM((4, 2, layer * size // 4, 128), F32),
            pltpu.VMEM((2, 2, rows, planes // 2 * 128), F32),
            pltpu.VMEM((2, 4, 8, 128), F32),
            dma((5,)),
            dma((6,)), dma((6,)),
            dma((4,)), dma((4,)),
            dma((2,)), dma((2,)),
            dma((planes + 1,)), dma((planes + 1,)),
            dma((2, planes + 1)), dma((2, planes + 1)),
            dma((planes + 1,)), dma((planes + 1,)),
            dma((3,)), dma((3,)),
            dma((2, layer)), dma((2, layer)),
            dma((2, 2, layer)), dma((2, 2, layer)),
            dma((2,)), dma((2,)),
            dma((2,)), dma((2,)),
            dma((2,)), dma((2,)),
            dma((2,)), dma((2,)),
            dma((2, 4)), dma((2, 4)),
        ],
        compiler_params=pltpu.CompilerParams(
            collective_id=0, has_side_effects=True, vmem_limit_bytes=60 * 1024 * 1024
        ),
        name="response",
    )(coefficients, forward, deep, probes, potential, potential_change)
    weights = jnp.array([1.0, 2.0, 1.0], F32) / (panel * lax.axis_size("probe") * depth * rows * cols)
    return hartree_change, total[:3, 0] * weights


def solution(mesh):
    return jax.shard_map(
        per_device,
        mesh=mesh,
        in_specs=(
            P("probe", "slab", None, None),
            P("slab", None, None),
            P("slab", None, None),
            P(),
        ),
        out_specs=(P("slab", None, None), P()),
        check_vma=False,
    )
```

```python
import functools
import math

import jax
import jax.numpy as jnp
import ml_dtypes
import numpy as np
from jax import lax
from jax.experimental import pallas as pl
from jax.experimental.pallas import tpu as pltpu
from jax.sharding import PartitionSpec as P

MESH = pl.DeviceIdType.MESH
F32 = jnp.float32
BF16 = jnp.bfloat16
KINETIC = 1.0 / 12.0
SCREEN = 0.05
PAD = 8


def cas_split(size):
    index = np.arange(size)
    angle = (index[:, None] * index[None, :] % size) * (2.0 * np.pi / size)
    table = np.cos(angle) + np.sin(angle)
    high = table.astype(ml_dtypes.bfloat16)
    low = (table - high.astype(np.float64)).astype(ml_dtypes.bfloat16)
    return high, low


def shuffle(size):
    index = np.arange(size)
    return index % 8 * (size // 8) + index // 8


def tables(*pairs):
    return jnp.asarray(np.stack([part for pair in pairs for part in pair]))


def split(value):
    high = value.astype(BF16)
    low = (value - high.astype(F32)).astype(BF16)
    return high, low


def times_table(value, table):
    high, low = split(value)
    total = jnp.dot(high, table[0], preferred_element_type=F32)
    total = total + jnp.dot(high, table[1], preferred_element_type=F32)
    return total + jnp.dot(low, table[0], preferred_element_type=F32)


def table_times(table, value):
    high, low = split(value)
    total = jnp.dot(table[0], high, preferred_element_type=F32)
    total = total + jnp.dot(table[1], high, preferred_element_type=F32)
    return total + jnp.dot(table[0], low, preferred_element_type=F32)


def place():
    probe = lax.axis_index("probe")
    slab = lax.axis_index("slab")
    return probe, slab


def sibling_of(probe, slab):
    return {"probe": probe + 1 - 2 * lax.rem(probe, 2), "slab": slab}


def partner_of(probe, slab):
    return {"probe": lax.rem(probe + 2, 4), "slab": slab}


def greet(peers):
    barrier = pltpu.get_barrier_semaphore()
    for peer in peers:
        pl.semaphore_signal(barrier, inc=1, device_id=peer, device_id_type=MESH)
    pl.semaphore_wait(barrier, len(peers))


def remote(source, target, sems, index, peer):
    return pltpu.make_async_remote_copy(
        src_ref=source,
        dst_ref=target,
        send_sem=sems[0].at[index],
        recv_sem=sems[1].at[index],
        device_id=peer,
        device_id_type=MESH,
    )


def signed(index, size):
    return jnp.where(index <= size // 2, index, index - size).astype(F32) * (2.0 * math.pi / size)


def response_kernel(
    slabs, layer,
    coef_ref, table_ref, ztable_ref, probes_ref, pot_ref, change_ref,
    out_ref, moment_ref,
    tab, v16, pot, change, ghost_in, near, weight, v32, qbuf, tbuf, ubuf, dbuf,
    pair_out, pair_in, ybuf, rone, rtwo, mbuf,
    ztab, abuf, rin, kern, rout, hold, quads, mslots,
    load_sems, halo_s, halo_r, fwd_s, fwd_r, pair_s, pair_r, one_s, one_r, two_s, two_r, mom_s, mom_r,
    in_s, in_r, out_s, out_r, near_s, near_r, far_s, far_r, relay_s, relay_r, e_s, e_r, mslot_s, mslot_r, ready,
):
    probe, slab = place()
    core = lax.rem(probe, 2)
    zlow = probe // 2
    above = {"probe": probe, "slab": lax.rem(slab + 1, slabs)}
    below = {"probe": probe, "slab": lax.rem(slab + slabs - 1, slabs)}
    sibling = sibling_of(probe, slab)
    partner = partner_of(probe, slab)
    zhigh = lax.rem(slab // 4, 2)
    spot = slab // 8 * 4 + lax.rem(slab, 4)
    across = {"probe": lax.rem(probe + 2, 4), "slab": slab + 4 - 8 * zhigh}

    def spot_after(step):
        return lax.rem(spot + step, layer)

    def layer_peer(step):
        other = spot_after(step)
        return {"probe": probe, "slab": other // 4 * 8 + zhigh * 4 + lax.rem(other, 4)}

    def other_peer(step):
        other = spot_after(step)
        return {
            "probe": lax.rem(probe + 2, 4),
            "slab": other // 4 * 8 + (1 - zhigh) * 4 + lax.rem(other, 4),
        }

    planes = probes_ref.shape[1]
    rows, cols = probes_ref.shape[2], probes_ref.shape[3]
    half = rows // 2
    mine = pl.ds(pl.multiple_of(core * half, half), half)

    loads = [
        pltpu.make_async_copy(change_ref, change, load_sems.at[0]),
        pltpu.make_async_copy(pot_ref, pot, load_sems.at[1]),
        pltpu.make_async_copy(probes_ref, v16.at[:, 1 : planes + 1], load_sems.at[2]),
        pltpu.make_async_copy(table_ref, tab, load_sems.at[3]),
        pltpu.make_async_copy(ztable_ref, ztab, load_sems.at[4]),
    ]
    for load in loads:
        load.start()
    column = [{"probe": probe, "slab": slab - lax.rem(slab, 4) + lax.rem(slab + step, 4)} for step in range(1, 4)]
    row_peers = [{"probe": probe, "slab": lax.rem(slab + 8 * step, slabs)} for step in range(1, 4)]
    greet([above, below, sibling, partner, across] + column + row_peers)
    for peer in row_peers:
        pl.semaphore_signal(ready.at[0], inc=1, device_id=peer, device_id_type=MESH)
    halo = (halo_s, halo_r)
    copies = [
        remote(probes_ref.at[:, planes - 1 : planes], v16.at[:, 0:1], halo, 0, above),
        remote(probes_ref.at[:, 0:1], v16.at[:, planes + 1 : planes + 2], halo, 1, below),
    ]
    for copy in copies:
        copy.start()
    edges = (
        (change_ref, planes - 1, above),
        (change_ref, 0, below),
        (pot_ref, planes - 1, above),
        (pot_ref, 0, below),
    )
    for index, (field, plane, peer) in enumerate(edges):
        copy = remote(field.at[plane, mine], ghost_in.at[index, mine], halo, 2 + index, peer)
        copy.start()
        copies.append(copy)
    for load in loads[:4]:
        load.wait()

    lanes = cols // 2
    lane = lax.broadcasted_iota(jnp.int32, (rows, lanes), 1)
    at_low, at_high = lane == 0, lane == lanes - 1
    inner = pl.ds(PAD, rows)

    def seal(buffer, *lead):
        for side in range(2):
            buffer[(*lead, side, pl.ds(0, PAD))] = pltpu.roll(buffer[(*lead, side, pl.ds(rows, PAD))], 1, 0)
            buffer[(*lead, side, pl.ds(rows + PAD, PAD))] = pltpu.roll(buffer[(*lead, side, pl.ds(PAD, PAD))], PAD - 1, 0)

    stretch = rows // 8

    def widen(plane, ghost=None):
        for step in range(8):
            here = pl.ds(step * stretch, stretch)
            spread = pl.ds(step, stretch, stride=8)
            wide = pl.ds(PAD + step, stretch, stride=8)
            if ghost is None:
                local, level = change[plane - 1, here], pot[plane - 1, here]
            else:
                local, level = ghost_in[ghost, here], ghost_in[2 + ghost, here]
            for side in range(2):
                part = slice(side * lanes, (side + 1) * lanes)
                weight[plane, side, spread, :] = local[:, part]
                near[plane, side, spread, :] = level[:, part]
            for which in range(2):
                value = v16[which, plane, here].astype(F32)
                tangent = value * local
                for side in range(2):
                    part = slice(side * lanes, (side + 1) * lanes)
                    v32[which, plane, side, wide, :] = value[:, part]
                    qbuf[which, plane, side, wide, :] = tangent[:, part]
        for which in range(2):
            seal(v32, which, plane)
            seal(qbuf, which, plane)

    def beside(buffer, which, plane, steps):
        middle, total = [], []
        for side in range(2):
            tall = buffer[which, plane, side]
            middle.append(tall[PAD : PAD + rows])
            around = tall[:rows] + tall[2 * PAD :]
            for step in steps:
                around = around + buffer[which, plane + step, side, inner]
            total.append(around)
        left = [pltpu.roll(value, 1, 1) for value in middle]
        right = [pltpu.roll(value, lanes - 1, 1) for value in middle]
        for side in range(2):
            beyond = jnp.where(at_low, left[1 - side], left[side])
            beyond = beyond + jnp.where(at_high, right[1 - side], right[side])
            total[side] = total[side] + beyond
        return middle, total

    def first(plane, steps=(-1, 1)):
        for which in range(2):
            terms, around = beside(v32, which, plane, steps)
            tangents, beyond = beside(qbuf, which, plane, steps)
            for side in range(2):
                local = near[plane, side]
                term = local * terms[side] - KINETIC * around[side]
                tbuf[which, plane, side, inner] = term
                ubuf[which, plane, side, inner] = (
                    local * tangents[side] - KINETIC * beyond[side] + weight[plane, side] * term
                )
        for which in range(2):
            seal(tbuf, which, plane)
            seal(ubuf, which, plane)

    mbuf[0:2] = jnp.zeros((2, 24, cols), F32)

    def fold(value):
        total = value[0:8]
        for index in range(1, rows // 8):
            total = total + value[8 * index : 8 * index + 8]
        return total

    def count(order, side, value):
        mbuf[0, pl.ds(8 * order, 8), side * lanes : (side + 1) * lanes] += fold(value)

    def last(plane):
        sums = [None, None]
        for which in range(2):
            terms, around = beside(tbuf, which, plane, (-1, 1))
            mixes, beyond = beside(ubuf, which, plane, (-1, 1))
            for side in range(2):
                local = near[plane, side]
                vector = v32[which, plane, side, inner]
                tangent = qbuf[which, plane, side, inner]
                image = local * terms[side] - KINETIC * around[side]
                third = local * mixes[side] - KINETIC * beyond[side] + weight[plane, side] * image
                parts = (vector * tangent, vector * mixes[side], vector * (4.0 * third - 3.0 * tangent))
                sums[side] = parts if sums[side] is None else tuple(a + b for a, b in zip(sums[side], parts))
        for side in range(2):
            for order in range(3):
                count(order, side, sums[side][order])
            dbuf[plane, :, side * lanes : (side + 1) * lanes] = (
                coef_ref[0] * sums[side][0] + (2.0 * coef_ref[1]) * sums[side][1] + coef_ref[2] * sums[side][2]
            )

    def pairs(target, planes_of):
        low, mid, high = planes_of
        for side in range(2):
            product = v32[0, low, side, inner] * v32[0, high, side, inner]
            product = product + v32[1, low, side, inner] * v32[1, high, side, inner]
            total = weight[low, side] + weight[mid, side] + weight[high, side]
            value = (4.0 * KINETIC * KINETIC) * total * product
            count(2, side, value)
            pair_out[target, :, side * lanes : (side + 1) * lanes] = (coef_ref[2] * value).astype(BF16)

    def hop_one(plane):
        return remote(ybuf.at[plane, 1 - core], rone.at[plane], (one_s, one_r), plane, sibling)

    fourth = rows // 4
    per = fourth // layer
    depth = planes * slabs
    size = 2 * planes * per

    def quarter(low, high):
        return pl.ds(pl.multiple_of((2 * low + high) * fourth, fourth), fourth)

    def hop_two(plane):
        return remote(
            ybuf.at[plane, core, quarter(1 - zlow, zhigh)], rtwo.at[plane, 0], (two_s.at[0], two_r.at[0]), plane, partner
        )

    def hop_pass(plane):
        return remote(
            ybuf.at[plane, core, quarter(zlow, 1 - zhigh)], rtwo.at[plane, 1], (two_s.at[1], two_r.at[1]), plane, partner
        )

    def transform(group):
        count = len(group)
        value = jnp.concatenate([dbuf[plane] for plane in group], axis=0)
        value = times_table(value, tab.at[0:2])
        value = jnp.concatenate([value[index * rows : (index + 1) * rows] for index in range(count)], axis=1)
        value = table_times(tab.at[2:4], value)
        for index, plane in enumerate(group):
            ybuf[plane, 0] = value[:, index * cols : index * cols + lanes]
            ybuf[plane, 1] = value[:, index * cols + lanes : (index + 1) * cols]
            hop_one(plane).start()

    def merge(plane):
        hop_one(plane).wait_recv()
        ybuf[plane, core] = ybuf[plane, core] + rone[plane]
        hop_pass(plane).start()
        hop_two(plane).start()

    inside = list(range(3, planes - 1))
    outside = [1, 2, planes - 1, planes]

    def spread(plane, side, value):
        group = inside if plane in inside else outside
        first_row = (0 if plane in inside else size // 4) + group.index(plane) * per
        for row in range(per):
            abuf[side, pl.ds(first_row + row, layer, stride=size // 2), :] = value[row * layer : (row + 1) * layer]

    def relay(plane):
        hop_pass(plane).wait_recv()
        spread(plane, 1, ybuf[plane, core, quarter(1 - zlow, 1 - zhigh)] + rtwo[plane, 1])

    def settle(plane):
        hop_two(plane).wait_recv()
        spread(plane, 0, ybuf[plane, core, quarter(zlow, zhigh)] + rtwo[plane, 0])

    def in_from(place_of, piece):
        return pl.ds(pl.multiple_of(place_of * (size // 2) + piece * (size // 4), size // 4), size // 4)

    def in_rows(place_of, piece, which):
        start = place_of * size + piece * (size // 2) + which * (size // 4)
        return pl.ds(pl.multiple_of(start, size // 4), size // 4)

    def in_copy(step, piece, side, here):
        source = abuf.at[side, in_from(spot_after(step), piece)]
        peer = layer_peer(step) if side == 0 else other_peer(step)
        return remote(source, rin.at[here], (in_s.at[piece, side], in_r.at[piece, side]), step, peer)

    def in_start(piece, side):
        def start(step, carry):
            in_copy(step, piece, side, in_rows(spot, piece, zhigh)).start()
            return carry

        lax.fori_loop(1 - side, layer, start, 0)
        if side == 0:
            rin[in_rows(spot, piece, zhigh)] = abuf[0, in_from(spot, piece)]

    def in_sent(piece, side):
        def finish(step, carry):
            in_copy(step, piece, side, in_rows(spot, piece, zhigh)).wait_send()
            return carry

        lax.fori_loop(1 - side, layer, finish, 0)

    def in_finish(piece):
        for side in range(2):
            def finish(step, carry):
                place_of = lax.rem(spot + layer - step, layer)
                which = zhigh if side == 0 else 1 - zhigh
                in_copy(step, piece, side, in_rows(place_of, piece, which)).wait_recv()
                return carry

            lax.fori_loop(1 - side, layer, finish, 0)

    def loop(low, high, body):
        def step(index, carry):
            body(index)
            return carry

        lax.fori_loop(low, high, step, 0)

    def both(body, low, high):
        def step(index, carry):
            body(jnp.where(index == 0, low, high))
            return carry

        lax.fori_loop(0, 2, step, 0)

    loop(1, planes + 1, widen)
    loop(2, planes, first)
    loop(3, planes - 1, last)
    transform(inside)
    loop(3, planes - 1, merge)
    for copy in copies[2:]:
        copy.wait()
    fwd = (fwd_s, fwd_r)
    forwards = [
        remote(ghost_in.at[index, mine], ghost_in.at[index, mine], fwd, index, sibling) for index in range(4)
    ]
    for copy in forwards:
        copy.start()
    pl.semaphore_wait(ready.at[0], 3)
    pl.semaphore_signal(ready.at[1], inc=1, device_id=across, device_id_type=MESH)
    for plane in inside:
        relay(plane)
    pl.semaphore_wait(ready.at[1], 1)
    in_start(0, 1)
    for plane in inside:
        settle(plane)
    in_start(0, 0)
    for copy in copies[:2]:
        copy.wait()
    for copy in forwards:
        copy.wait()
    widen(0, 0)
    widen(planes + 1, 1)
    pairs(0, (0, 1, 2))
    pairs(1, (planes - 1, planes, planes + 1))
    trades = [
        remote(pair_out.at[0], pair_in.at[1], (pair_s, pair_r), 0, below),
        remote(pair_out.at[1], pair_in.at[0], (pair_s, pair_r), 1, above),
    ]
    for copy in trades:
        copy.start()
    both(first, 1, planes)
    both(last, 2, planes - 1)
    transform([2, planes - 1])
    first(0, (1,))
    first(planes + 1, (-1,))
    both(merge, 2, planes - 1)
    both(last, 1, planes)
    for copy in trades:
        copy.wait()
    dbuf[1] += pair_in[0].astype(F32)
    dbuf[planes] += pair_in[1].astype(F32)
    transform([1, planes])

    mom = (mom_s, mom_r)
    for order in range(3):
        strip = jnp.sum(mbuf[0, pl.ds(8 * order, 8)], axis=0, keepdims=True)
        total = jnp.sum(strip, axis=1, keepdims=True)
        mbuf[1, pl.ds(order, 1)] = jnp.broadcast_to(total, (1, cols))
    swap = remote(mbuf.at[1, 0:8], mbuf.at[2, 0:8], mom, 0, sibling)
    swap.start()
    for plane in (2, planes - 1):
        relay(plane)
        settle(plane)
    both(merge, 1, planes)
    swap.wait()
    mbuf[3, 0:8] = mbuf[1, 0:8] + mbuf[2, 0:8]
    swap = remote(mbuf.at[3, 0:8], mbuf.at[4, 0:8], mom, 1, partner)
    swap.start()
    relay(1)
    relay(planes)
    in_start(1, 1)
    settle(1)
    settle(planes)
    in_start(1, 0)
    swap.wait()
    mbuf[5, 0:8] = mbuf[3, 0:8] + mbuf[4, 0:8]
    swap = remote(mbuf.at[5, 0:8], mbuf.at[6, 0:8], mom, 2, across)
    swap.start()

    wave_z = signed(lax.broadcasted_iota(jnp.int32, (depth, lanes), 0), depth)
    wave_x = signed(lax.broadcasted_iota(jnp.int32, (depth, lanes), 1) + core * lanes, cols)
    base = wave_z * wave_z + wave_x * wave_x
    for row in range(per):
        number = (2 * zlow + zhigh) * fourth + row * layer + spot
        wave_y = signed(jnp.full((depth, lanes), number, jnp.int32), rows)
        summed = base + wave_y * wave_y
        value = (4.0 * math.pi / (8.0 * depth * rows * cols)) / (summed + SCREEN * SCREEN)
        kern[:, row * lanes : (row + 1) * lanes] = jnp.where(summed == 0.0, 0.0, value)
    loads[4].wait()

    def moment_round(number, stride):
        where = lax.rem(slab // stride, 4)
        copies, waits = [], []
        for step in range(1, 4):
            peer = {"probe": probe, "slab": slab + (lax.rem(where + step, 4) - where) * stride}
            source = lax.rem(where + 4 - step, 4)
            sems = (mslot_s.at[number], mslot_r.at[number])
            copies.append(remote(mslots.at[number, where], mslots.at[number, where], sems, step, peer))
            waits.append(remote(mslots.at[number, source], mslots.at[number, source], sems, step, peer))
        return where, copies, waits

    def moment_start(number, stride, value):
        where, copies, waits = moment_round(number, stride)
        mslots[number, where] = value
        for copy in copies:
            copy.start()

    def moment_finish(number, stride):
        where, copies, waits = moment_round(number, stride)
        for copy in waits:
            copy.wait_recv()
        for copy in copies:
            copy.wait_send()
        return (mslots[number, 0] + mslots[number, 1]) + (mslots[number, 2] + mslots[number, 3])

    in_finish(0)
    swap.wait()
    moment_start(0, 1, (mbuf[5, 0:8] + mbuf[6, 0:8])[:, :128])
    in_finish(1)
    columns = jnp.concatenate([rin[pl.ds(row, depth, stride=per), :] for row in range(per)], axis=1)
    here = lax.broadcasted_iota(jnp.int32, (1, per * lanes), 1) + (probe + slab) * (per * lanes)
    mean = jnp.sum(columns, axis=0, keepdims=True) * (1.0 / depth)
    columns = columns - jnp.where(here == 0, mean, 0.0)
    columns = table_times(ztab.at[0:2], columns) * kern[...]
    columns = table_times(ztab.at[2:4], columns)
    for row in range(per):
        rout[pl.ds(row, depth, stride=per), :] = columns[:, row * lanes : (row + 1) * lanes]

    piece = planes // 2 * per
    own_quarter = 2 * zlow + zhigh
    far_quarter = 2 * (1 - zlow) + (1 - zhigh)

    def out_rows(place_of, side, part):
        which = zhigh if side == 0 else 1 - zhigh
        return pl.ds(pl.multiple_of(place_of * size + which * (size // 2) + part * piece, piece), piece)

    def landing(side, part, place_of):
        rows_at = pl.ds(pl.multiple_of(place_of * piece, piece), piece)
        return quads.at[own_quarter, part, rows_at] if side == 0 else hold.at[part, rows_at]

    def out_copy(step, side, part, place_of):
        source = rout.at[out_rows(spot_after(step), side, part)]
        sems = (out_s.at[side, part], out_r.at[side, part])
        return remote(source, landing(side, part, place_of), sems, step, layer_peer(step))

    def out_start(side, part):
        def start(step, carry):
            out_copy(step, side, part, spot).start()
            return carry

        lax.fori_loop(1, layer, start, 0)
        target = landing(side, part, spot)
        target[...] = rout[out_rows(spot, side, part)]

    def out_finish(side, part):
        def finish(step, carry):
            out_copy(step, side, part, spot_after(layer - step)).wait_recv()
            return carry

        lax.fori_loop(1, layer, finish, 0)

    def out_sent():
        def finish(step, carry):
            for side in range(2):
                for part in range(2):
                    out_copy(step, side, part, spot).wait_send()
            return carry

        lax.fori_loop(1, layer, finish, 0)

    def to_partner(part):
        return remote(quads.at[own_quarter, part], quads.at[own_quarter, part], (near_s, near_r), part, partner)

    def to_across(part):
        return remote(hold.at[part], quads.at[own_quarter, part], (far_s, far_r), part, across)

    def pass_on(part):
        return remote(quads.at[far_quarter, part], quads.at[far_quarter, part], (relay_s, relay_r), part, partner)

    for part in range(2):
        out_start(0, part)
        out_start(1, part)
    moments = moment_finish(0, 1)
    moment_start(1, 8, moments)

    def drain(plane):
        hop_one(plane).wait_send()
        hop_two(plane).wait_send()
        hop_pass(plane).wait_send()

    loop(1, planes + 1, drain)
    for piece_number in range(2):
        for side in range(2):
            in_sent(piece_number, side)
    for part in range(2):
        out_finish(0, part)
        to_partner(part).start()
        out_finish(1, part)
        to_across(part).start()
    moment_ref[...] = moment_finish(1, 8)
    for part in range(2):
        to_across(part).wait_recv()
        pass_on(part).start()

    def share(part):
        slot = pl.ds(4 * core + 2 * part, 2)
        return remote(pot.at[slot], pot.at[slot], (e_s, e_r), part, sibling)

    def invert(part):
        to_partner(part).wait_recv()
        pass_on(part).wait_recv()
        columns = []
        for plane in range(planes // 2):
            blocks = [
                quads[which, part, pl.ds(plane * per + row, layer, stride=piece), :]
                for which in range(4)
                for row in range(per)
            ]
            columns.append(jnp.concatenate(blocks, axis=0))
        value = table_times(tab.at[0:2], jnp.concatenate(columns, axis=1))
        for pair in range(2):
            pot[4 * core + 2 * part + pair] = value[:, pair * cols : (pair + 1) * cols]
        share(part).start()

    def finish(part):
        share(part).wait_recv()
        value = [
            jnp.concatenate(
                [pot[4 * side + 2 * part + plane // 2, :, plane % 2 * lanes : (plane % 2 + 1) * lanes] for side in range(2)],
                axis=1,
            )
            for plane in range(planes // 2)
        ]
        value = times_table(jnp.concatenate(value, axis=0), tab.at[0:2])
        for plane in range(planes // 2):
            out_ref[part * (planes // 2) + plane] = value[plane * rows : (plane + 1) * rows]

    invert(0)
    finish(0)
    out_sent()
    invert(1)
    finish(1)
    for part in range(2):
        to_partner(part).wait_send()
        to_across(part).wait_send()
        pass_on(part).wait_send()
        share(part).wait_send()


def per_device(probes, potential, potential_change, coefficients):
    panel, planes, rows, cols = probes.shape
    slabs = lax.axis_size("slab")
    layer = slabs // 2
    depth = planes * slabs
    fourth = rows // 4
    size = 2 * planes * (fourth // layer)
    vmem = pl.BlockSpec(memory_space=pltpu.VMEM)
    anywhere = pl.BlockSpec(memory_space=pl.ANY)
    dma = pltpu.SemaphoreType.DMA
    high, low = cas_split(rows)
    order = shuffle(rows)
    forward = tables((high, low), (high[:, order], low[:, order]))
    high, low = cas_split(depth)
    spots = np.arange(layer)[:, None, None, None] // 4 * 8 + np.arange(layer)[:, None, None, None] % 4
    halves = np.arange(2)[None, None, :, None] * 4
    inner = np.array([list(range(2, planes - 2)), [0, 1, planes - 2, planes - 1]])[None, :, None, :]
    came = ((spots + halves) * planes + inner).reshape(-1)
    goes = ((spots[:, 0] + halves[:, 0]) * planes + np.arange(planes)).reshape(-1)
    deep = tables((high[:, came], low[:, came]), (high[goes], low[goes]))
    tall = rows + 2 * PAD
    hartree_change, total = pl.pallas_call(
        functools.partial(response_kernel, slabs, layer),
        out_shape=(
            pltpu.VMEM((planes, rows, cols), F32),
            jax.ShapeDtypeStruct((8, 128), F32),
        ),
        in_specs=[pl.BlockSpec(memory_space=pltpu.SMEM)] + [anywhere] * 5,
        out_specs=(vmem, vmem),
        scratch_shapes=[
            pltpu.VMEM((4, rows, cols), BF16),
            pltpu.VMEM((panel, planes + 2, rows, cols), BF16),
            pltpu.VMEM((planes, rows, cols), F32),
            pltpu.VMEM((planes, rows, cols), F32),
            pltpu.VMEM((4, rows, cols), F32),
            pltpu.VMEM((planes + 2, 2, rows, 128), F32),
            pltpu.VMEM((planes + 2, 2, rows, 128), F32),
            pltpu.VMEM((panel, planes + 2, 2, tall, 128), F32),
            pltpu.VMEM((panel, planes + 2, 2, tall, 128), F32),
            pltpu.VMEM((panel, planes + 2, 2, tall, 128), F32),
            pltpu.VMEM((panel, planes + 2, 2, tall, 128), F32),
            pltpu.VMEM((planes + 1, rows, cols), F32),
            pltpu.VMEM((2, rows, cols), BF16),
            pltpu.VMEM((2, rows, cols), BF16),
            pltpu.VMEM((planes + 1, 2, rows, 128), F32),
            pltpu.VMEM((planes + 1, rows, 128), F32),
            pltpu.VMEM((planes + 1, 2, fourth, 128), F32),
            pltpu.VMEM((7, 24, cols), F32),
            pltpu.VMEM((4, depth, depth), BF16),
            pltpu.VMEM((2, layer * size // 2, 128), F32),
            pltpu.VMEM((layer * size, 128), F32),
            pltpu.VMEM((depth, 4 * 128), F32),
            pltpu.VMEM((layer * size, 128), F32),
            pltpu.VMEM((2, layer * size // 4, 128), F32),
            pltpu.VMEM((4, 2, layer * size // 4, 128), F32),
            pltpu.VMEM((2, 4, 8, 128), F32),
            dma((5,)),
            dma((6,)), dma((6,)),
            dma((4,)), dma((4,)),
            dma((2,)), dma((2,)),
            dma((planes + 1,)), dma((planes + 1,)),
            dma((2, planes + 1)), dma((2, planes + 1)),
            dma((3,)), dma((3,)),
            dma((2, 2, layer)), dma((2, 2, layer)),
            dma((2, 2, layer)), dma((2, 2, layer)),
            dma((2,)), dma((2,)),
            dma((2,)), dma((2,)),
            dma((2,)), dma((2,)),
            dma((2,)), dma((2,)),
            dma((2, 4)), dma((2, 4)),
            pltpu.SemaphoreType.REGULAR((2,)),
        ],
        compiler_params=pltpu.CompilerParams(
            collective_id=0, has_side_effects=True, vmem_limit_bytes=56 * 1024 * 1024
        ),
        name="response",
    )(coefficients, forward, deep, probes, potential, potential_change)
    weights = jnp.array([1.0, 2.0, 1.0], F32) / (panel * lax.axis_size("probe") * depth * rows * cols)
    return hartree_change, total[:3, 0] * weights


def solution(mesh):
    return jax.shard_map(
        per_device,
        mesh=mesh,
        in_specs=(
            P("probe", "slab", None, None),
            P("slab", None, None),
            P("slab", None, None),
            P(),
        ),
        out_specs=(P("slab", None, None), P()),
        check_vma=False,
    )
```

```python
import functools
import math

import jax
import jax.numpy as jnp
import ml_dtypes
import numpy as np
from jax import lax
from jax.experimental import pallas as pl
from jax.experimental.pallas import tpu as pltpu
from jax.sharding import PartitionSpec as P

MESH = pl.DeviceIdType.MESH
F32 = jnp.float32
BF16 = jnp.bfloat16
KINETIC = 1.0 / 12.0
SCREEN = 0.05
PAD = 8
STEP = 16


def cas_split(size):
    index = np.arange(size)
    angle = (index[:, None] * index[None, :] % size) * (2.0 * np.pi / size)
    table = np.cos(angle) + np.sin(angle)
    high = table.astype(ml_dtypes.bfloat16)
    low = (table - high.astype(np.float64)).astype(ml_dtypes.bfloat16)
    return high, low


def shuffle(size):
    index = np.arange(size)
    return index % 8 * (size // 8) + index // 8


def tables(*pairs):
    return jnp.asarray(np.stack([part for pair in pairs for part in pair]))


def split(value):
    high = value.astype(BF16)
    low = (value - high.astype(F32)).astype(BF16)
    return high, low


def times_table(value, table):
    high, low = split(value)
    total = jnp.dot(high, table[0], preferred_element_type=F32)
    total = total + jnp.dot(high, table[1], preferred_element_type=F32)
    return total + jnp.dot(low, table[0], preferred_element_type=F32)


def table_times(table, value):
    high, low = split(value)
    total = jnp.dot(table[0], high, preferred_element_type=F32)
    total = total + jnp.dot(table[1], high, preferred_element_type=F32)
    return total + jnp.dot(table[0], low, preferred_element_type=F32)


def place():
    probe = lax.axis_index("probe")
    slab = lax.axis_index("slab")
    return probe, slab


def sibling_of(probe, slab):
    return {"probe": probe + 1 - 2 * lax.rem(probe, 2), "slab": slab}


def partner_of(probe, slab):
    return {"probe": lax.rem(probe + 2, 4), "slab": slab}


def greet(peers):
    barrier = pltpu.get_barrier_semaphore()
    for peer in peers:
        pl.semaphore_signal(barrier, inc=1, device_id=peer, device_id_type=MESH)
    pl.semaphore_wait(barrier, len(peers))


def remote(source, target, sems, index, peer):
    return pltpu.make_async_remote_copy(
        src_ref=source,
        dst_ref=target,
        send_sem=sems[0].at[index],
        recv_sem=sems[1].at[index],
        device_id=peer,
        device_id_type=MESH,
    )


def signed(index, size):
    return jnp.where(index <= size // 2, index, index - size).astype(F32) * (2.0 * math.pi / size)


def response_kernel(
    slabs, layer,
    coef_ref, table_ref, ztable_ref, probes_ref, pot_ref, change_ref,
    out_ref, moment_ref,
    tab, v16, pot, change, ghost_in, near, weight, v32, qbuf, tbuf, ubuf, dbuf,
    pair_out, pair_in, ybuf, rone, rtwo, mbuf,
    ztab, abuf, rin, kern, rout, hold, quads, mslots,
    load_sems, halo_s, halo_r, fwd_s, fwd_r, pair_s, pair_r, one_s, one_r, two_s, two_r, mom_s, mom_r,
    in_s, in_r, out_s, out_r, near_s, near_r, far_s, far_r, relay_s, relay_r, e_s, e_r, mslot_s, mslot_r, ready,
):
    probe, slab = place()
    core = lax.rem(probe, 2)
    zlow = probe // 2
    above = {"probe": probe, "slab": lax.rem(slab + 1, slabs)}
    below = {"probe": probe, "slab": lax.rem(slab + slabs - 1, slabs)}
    sibling = sibling_of(probe, slab)
    partner = partner_of(probe, slab)
    zhigh = lax.rem(slab // 4, 2)
    spot = slab // 8 * 4 + lax.rem(slab, 4)
    across = {"probe": lax.rem(probe + 2, 4), "slab": slab + 4 - 8 * zhigh}

    def spot_after(step):
        return lax.rem(spot + step, layer)

    def layer_peer(step):
        other = spot_after(step)
        return {"probe": probe, "slab": other // 4 * 8 + zhigh * 4 + lax.rem(other, 4)}

    def other_peer(step):
        other = spot_after(step)
        return {
            "probe": lax.rem(probe + 2, 4),
            "slab": other // 4 * 8 + (1 - zhigh) * 4 + lax.rem(other, 4),
        }

    planes = probes_ref.shape[1]
    rows, cols = probes_ref.shape[2], probes_ref.shape[3]
    half = rows // 2
    mine = pl.ds(pl.multiple_of(core * half, half), half)

    loads = [
        pltpu.make_async_copy(change_ref, change, load_sems.at[0]),
        pltpu.make_async_copy(pot_ref, pot, load_sems.at[1]),
        pltpu.make_async_copy(probes_ref, v16.at[:, 1 : planes + 1], load_sems.at[2]),
        pltpu.make_async_copy(table_ref, tab, load_sems.at[3]),
        pltpu.make_async_copy(ztable_ref, ztab, load_sems.at[4]),
    ]
    for load in loads:
        load.start()
    column = [{"probe": probe, "slab": slab - lax.rem(slab, 4) + lax.rem(slab + step, 4)} for step in range(1, 4)]
    row_peers = [{"probe": probe, "slab": lax.rem(slab + 8 * step, slabs)} for step in range(1, 4)]
    greet([above, below, sibling, partner, across] + column + row_peers)
    for peer in row_peers:
        pl.semaphore_signal(ready.at[0], inc=1, device_id=peer, device_id_type=MESH)
    halo = (halo_s, halo_r)
    copies = [
        remote(probes_ref.at[:, planes - 1 : planes], v16.at[:, 0:1], halo, 0, above),
        remote(probes_ref.at[:, 0:1], v16.at[:, planes + 1 : planes + 2], halo, 1, below),
    ]
    for copy in copies:
        copy.start()
    edges = (
        (change_ref, planes - 1, above),
        (change_ref, 0, below),
        (pot_ref, planes - 1, above),
        (pot_ref, 0, below),
    )
    for index, (field, plane, peer) in enumerate(edges):
        copy = remote(field.at[plane, mine], ghost_in.at[index, mine], halo, 2 + index, peer)
        copy.start()
        copies.append(copy)
    for load in loads[:4]:
        load.wait()

    lanes = cols // 2
    lane = lax.broadcasted_iota(jnp.int32, (STEP, lanes), 1)
    at_low, at_high = lane == 0, lane == lanes - 1
    inner = pl.ds(PAD, rows)

    def seal(buffer, *lead):
        for side in range(2):
            buffer[(*lead, side, pl.ds(0, PAD))] = pltpu.roll(buffer[(*lead, side, pl.ds(rows, PAD))], 1, 0)
            buffer[(*lead, side, pl.ds(rows + PAD, PAD))] = pltpu.roll(buffer[(*lead, side, pl.ds(PAD, PAD))], PAD - 1, 0)

    stretch = rows // 8

    def widen(plane, ghost=None):
        for step in range(8):
            here = pl.ds(step * stretch, stretch)
            spread = pl.ds(step, stretch, stride=8)
            wide = pl.ds(PAD + step, stretch, stride=8)
            if ghost is None:
                local, level = change[plane - 1, here], pot[plane - 1, here]
            else:
                local, level = ghost_in[ghost, here], ghost_in[2 + ghost, here]
            for side in range(2):
                part = slice(side * lanes, (side + 1) * lanes)
                weight[plane, side, spread, :] = local[:, part]
                near[plane, side, spread, :] = level[:, part]
            for which in range(2):
                value = v16[which, plane, here].astype(F32)
                tangent = value * local
                for side in range(2):
                    part = slice(side * lanes, (side + 1) * lanes)
                    v32[which, plane, side, wide, :] = value[:, part]
                    qbuf[which, plane, side, wide, :] = tangent[:, part]
        for which in range(2):
            seal(v32, which, plane)
            seal(qbuf, which, plane)

    def beside(buffer, which, plane, row, steps):
        middle, total = [], []
        for side in range(2):
            tall = buffer[which, plane, side, row : row + STEP + 2 * PAD]
            middle.append(tall[PAD : PAD + STEP])
            around = tall[:STEP] + tall[2 * PAD :]
            for step in steps:
                around = around + buffer[which, plane + step, side, row + PAD : row + PAD + STEP]
            total.append(around)
        left = [pltpu.roll(value, 1, 1) for value in middle]
        right = [pltpu.roll(value, lanes - 1, 1) for value in middle]
        for side in range(2):
            beyond = jnp.where(at_low, left[1 - side], left[side])
            beyond = beyond + jnp.where(at_high, right[1 - side], right[side])
            total[side] = total[side] + beyond
        return middle, total

    def first(plane, steps=(-1, 1)):
        for row in range(0, rows, STEP):
            here = slice(row, row + STEP)
            there = slice(row + PAD, row + PAD + STEP)
            for which in range(2):
                terms, around = beside(v32, which, plane, row, steps)
                tangents, beyond = beside(qbuf, which, plane, row, steps)
                for side in range(2):
                    local = near[plane, side, here]
                    term = local * terms[side] - KINETIC * around[side]
                    tbuf[which, plane, side, there] = term
                    ubuf[which, plane, side, there] = (
                        local * tangents[side] - KINETIC * beyond[side] + weight[plane, side, here] * term
                    )
        for which in range(2):
            seal(tbuf, which, plane)
            seal(ubuf, which, plane)

    mbuf[0:2] = jnp.zeros((2, 24, cols), F32)

    def fold(value):
        total = value[0:8]
        for index in range(1, value.shape[0] // 8):
            total = total + value[8 * index : 8 * index + 8]
        return total

    def count(order, side, value):
        mbuf[0, pl.ds(8 * order, 8), side * lanes : (side + 1) * lanes] += fold(value)

    def last(plane):
        tallies = [[0.0] * 3, [0.0] * 3]
        for row in range(0, rows, STEP):
            here = slice(row, row + STEP)
            there = slice(row + PAD, row + PAD + STEP)
            sums = [None, None]
            for which in range(2):
                terms, around = beside(tbuf, which, plane, row, (-1, 1))
                mixes, beyond = beside(ubuf, which, plane, row, (-1, 1))
                for side in range(2):
                    local = near[plane, side, here]
                    vector = v32[which, plane, side, there]
                    tangent = qbuf[which, plane, side, there]
                    image = local * terms[side] - KINETIC * around[side]
                    third = local * mixes[side] - KINETIC * beyond[side] + weight[plane, side, here] * image
                    parts = (vector * tangent, vector * mixes[side], vector * (4.0 * third - 3.0 * tangent))
                    sums[side] = parts if sums[side] is None else tuple(a + b for a, b in zip(sums[side], parts))
            for side in range(2):
                for order in range(3):
                    tallies[side][order] = tallies[side][order] + fold(sums[side][order])
                dbuf[plane, here, side * lanes : (side + 1) * lanes] = (
                    coef_ref[0] * sums[side][0] + (2.0 * coef_ref[1]) * sums[side][1] + coef_ref[2] * sums[side][2]
                )
        for side in range(2):
            for order in range(3):
                mbuf[0, pl.ds(8 * order, 8), side * lanes : (side + 1) * lanes] += tallies[side][order]

    def pairs(target, planes_of):
        low, mid, high = planes_of
        for side in range(2):
            product = v32[0, low, side, inner] * v32[0, high, side, inner]
            product = product + v32[1, low, side, inner] * v32[1, high, side, inner]
            total = weight[low, side] + weight[mid, side] + weight[high, side]
            value = (4.0 * KINETIC * KINETIC) * total * product
            count(2, side, value)
            pair_out[target, :, side * lanes : (side + 1) * lanes] = (coef_ref[2] * value).astype(BF16)

    def hop_one(plane):
        return remote(ybuf.at[plane, 1 - core], rone.at[plane], (one_s, one_r), plane, sibling)

    fourth = rows // 4
    per = fourth // layer
    depth = planes * slabs
    size = 2 * planes * per

    def quarter(low, high):
        return pl.ds(pl.multiple_of((2 * low + high) * fourth, fourth), fourth)

    def hop_two(plane):
        return remote(
            ybuf.at[plane, core, quarter(1 - zlow, zhigh)], rtwo.at[plane, 0], (two_s.at[0], two_r.at[0]), plane, partner
        )

    def hop_pass(plane):
        return remote(
            ybuf.at[plane, core, quarter(zlow, 1 - zhigh)], rtwo.at[plane, 1], (two_s.at[1], two_r.at[1]), plane, partner
        )

    def transform(group):
        count = len(group)
        value = jnp.concatenate([dbuf[plane] for plane in group], axis=0)
        value = times_table(value, tab.at[0:2])
        value = jnp.concatenate([value[index * rows : (index + 1) * rows] for index in range(count)], axis=1)
        value = table_times(tab.at[2:4], value)
        for index, plane in enumerate(group):
            ybuf[plane, 0] = value[:, index * cols : index * cols + lanes]
            ybuf[plane, 1] = value[:, index * cols + lanes : (index + 1) * cols]
            hop_one(plane).start()

    def merge(plane):
        hop_one(plane).wait_recv()
        ybuf[plane, core] = ybuf[plane, core] + rone[plane]
        hop_pass(plane).start()
        hop_two(plane).start()

    inside = list(range(3, planes - 1))
    outside = [1, 2, planes - 1, planes]

    def spread(plane, side, value):
        group = inside if plane in inside else outside
        first_row = (0 if plane in inside else size // 4) + group.index(plane) * per
        for row in range(per):
            abuf[side, pl.ds(first_row + row, layer, stride=size // 2), :] = value[row * layer : (row + 1) * layer]

    def relay(plane):
        hop_pass(plane).wait_recv()
        spread(plane, 1, ybuf[plane, core, quarter(1 - zlow, 1 - zhigh)] + rtwo[plane, 1])

    def settle(plane):
        hop_two(plane).wait_recv()
        spread(plane, 0, ybuf[plane, core, quarter(zlow, zhigh)] + rtwo[plane, 0])

    def in_from(place_of, piece):
        return pl.ds(pl.multiple_of(place_of * (size // 2) + piece * (size // 4), size // 4), size // 4)

    def in_rows(place_of, piece, which):
        start = place_of * size + piece * (size // 2) + which * (size // 4)
        return pl.ds(pl.multiple_of(start, size // 4), size // 4)

    def in_copy(step, piece, side, here):
        source = abuf.at[side, in_from(spot_after(step), piece)]
        peer = layer_peer(step) if side == 0 else other_peer(step)
        return remote(source, rin.at[here], (in_s.at[piece, side], in_r.at[piece, side]), step, peer)

    def in_start(piece, side):
        def start(step, carry):
            in_copy(step, piece, side, in_rows(spot, piece, zhigh)).start()
            return carry

        lax.fori_loop(1 - side, layer, start, 0)
        if side == 0:
            rin[in_rows(spot, piece, zhigh)] = abuf[0, in_from(spot, piece)]

    def in_sent(piece, side):
        def finish(step, carry):
            in_copy(step, piece, side, in_rows(spot, piece, zhigh)).wait_send()
            return carry

        lax.fori_loop(1 - side, layer, finish, 0)

    def in_finish(piece):
        for side in range(2):
            def finish(step, carry):
                place_of = lax.rem(spot + layer - step, layer)
                which = zhigh if side == 0 else 1 - zhigh
                in_copy(step, piece, side, in_rows(place_of, piece, which)).wait_recv()
                return carry

            lax.fori_loop(1 - side, layer, finish, 0)

    def loop(low, high, body):
        def step(index, carry):
            body(index)
            return carry

        lax.fori_loop(low, high, step, 0)

    def both(body, low, high):
        def step(index, carry):
            body(jnp.where(index == 0, low, high))
            return carry

        lax.fori_loop(0, 2, step, 0)

    loop(1, planes + 1, widen)
    loop(2, planes, first)
    loop(3, planes - 1, last)
    transform(inside)
    loop(3, planes - 1, merge)
    for copy in copies[2:]:
        copy.wait()
    fwd = (fwd_s, fwd_r)
    forwards = [
        remote(ghost_in.at[index, mine], ghost_in.at[index, mine], fwd, index, sibling) for index in range(4)
    ]
    for copy in forwards:
        copy.start()
    pl.semaphore_wait(ready.at[0], 3)
    pl.semaphore_signal(ready.at[1], inc=1, device_id=across, device_id_type=MESH)
    for copy in copies[:2]:
        copy.wait()
    for copy in forwards:
        copy.wait()
    widen(0, 0)
    widen(planes + 1, 1)
    pairs(0, (0, 1, 2))
    pairs(1, (planes - 1, planes, planes + 1))
    trades = [
        remote(pair_out.at[0], pair_in.at[1], (pair_s, pair_r), 0, below),
        remote(pair_out.at[1], pair_in.at[0], (pair_s, pair_r), 1, above),
    ]
    for copy in trades:
        copy.start()
    both(first, 1, planes)
    both(last, 2, planes - 1)
    transform([2, planes - 1])
    for plane in inside:
        relay(plane)
    pl.semaphore_wait(ready.at[1], 1)
    in_start(0, 1)
    both(merge, 2, planes - 1)
    for plane in inside:
        settle(plane)
    in_start(0, 0)
    first(0, (1,))
    first(planes + 1, (-1,))
    both(last, 1, planes)
    for copy in trades:
        copy.wait()
    dbuf[1] += pair_in[0].astype(F32)
    dbuf[planes] += pair_in[1].astype(F32)
    transform([1, planes])

    mom = (mom_s, mom_r)
    for order in range(3):
        strip = jnp.sum(mbuf[0, pl.ds(8 * order, 8)], axis=0, keepdims=True)
        total = jnp.sum(strip, axis=1, keepdims=True)
        mbuf[1, pl.ds(order, 1)] = jnp.broadcast_to(total, (1, cols))
    swap = remote(mbuf.at[1, 0:8], mbuf.at[2, 0:8], mom, 0, sibling)
    swap.start()
    for plane in (2, planes - 1):
        relay(plane)
        settle(plane)
    both(merge, 1, planes)
    swap.wait()
    mbuf[3, 0:8] = mbuf[1, 0:8] + mbuf[2, 0:8]
    swap = remote(mbuf.at[3, 0:8], mbuf.at[4, 0:8], mom, 1, partner)
    swap.start()
    relay(1)
    relay(planes)
    in_start(1, 1)
    settle(1)
    settle(planes)
    in_start(1, 0)
    swap.wait()
    mbuf[5, 0:8] = mbuf[3, 0:8] + mbuf[4, 0:8]
    swap = remote(mbuf.at[5, 0:8], mbuf.at[6, 0:8], mom, 2, across)
    swap.start()

    wave_z = signed(lax.broadcasted_iota(jnp.int32, (depth, lanes), 0), depth)
    wave_x = signed(lax.broadcasted_iota(jnp.int32, (depth, lanes), 1) + core * lanes, cols)
    base = wave_z * wave_z + wave_x * wave_x
    for row in range(per):
        number = (2 * zlow + zhigh) * fourth + row * layer + spot
        wave_y = signed(jnp.full((depth, lanes), number, jnp.int32), rows)
        summed = base + wave_y * wave_y
        value = (4.0 * math.pi / (8.0 * depth * rows * cols)) / (summed + SCREEN * SCREEN)
        kern[:, row * lanes : (row + 1) * lanes] = jnp.where(summed == 0.0, 0.0, value)
    loads[4].wait()

    def moment_round(number, stride):
        where = lax.rem(slab // stride, 4)
        copies, waits = [], []
        for step in range(1, 4):
            peer = {"probe": probe, "slab": slab + (lax.rem(where + step, 4) - where) * stride}
            source = lax.rem(where + 4 - step, 4)
            sems = (mslot_s.at[number], mslot_r.at[number])
            copies.append(remote(mslots.at[number, where], mslots.at[number, where], sems, step, peer))
            waits.append(remote(mslots.at[number, source], mslots.at[number, source], sems, step, peer))
        return where, copies, waits

    def moment_start(number, stride, value):
        where, copies, waits = moment_round(number, stride)
        mslots[number, where] = value
        for copy in copies:
            copy.start()

    def moment_finish(number, stride):
        where, copies, waits = moment_round(number, stride)
        for copy in waits:
            copy.wait_recv()
        for copy in copies:
            copy.wait_send()
        return (mslots[number, 0] + mslots[number, 1]) + (mslots[number, 2] + mslots[number, 3])

    in_finish(0)
    swap.wait()
    moment_start(0, 1, (mbuf[5, 0:8] + mbuf[6, 0:8])[:, :128])
    in_finish(1)
    columns = jnp.concatenate([rin[pl.ds(row, depth, stride=per), :] for row in range(per)], axis=1)
    here = lax.broadcasted_iota(jnp.int32, (1, per * lanes), 1) + (probe + slab) * (per * lanes)
    mean = jnp.sum(columns, axis=0, keepdims=True) * (1.0 / depth)
    columns = columns - jnp.where(here == 0, mean, 0.0)
    columns = table_times(ztab.at[0:2], columns) * kern[...]
    columns = table_times(ztab.at[2:4], columns)
    for row in range(per):
        rout[pl.ds(row, depth, stride=per), :] = columns[:, row * lanes : (row + 1) * lanes]

    piece = planes // 2 * per
    own_quarter = 2 * zlow + zhigh
    far_quarter = 2 * (1 - zlow) + (1 - zhigh)

    def out_rows(place_of, side, part):
        which = zhigh if side == 0 else 1 - zhigh
        return pl.ds(pl.multiple_of(place_of * size + which * (size // 2) + part * piece, piece), piece)

    def landing(side, part, place_of):
        rows_at = pl.ds(pl.multiple_of(place_of * piece, piece), piece)
        return quads.at[own_quarter, part, rows_at] if side == 0 else hold.at[part, rows_at]

    def out_copy(step, side, part, place_of):
        source = rout.at[out_rows(spot_after(step), side, part)]
        sems = (out_s.at[side, part], out_r.at[side, part])
        return remote(source, landing(side, part, place_of), sems, step, layer_peer(step))

    def out_start(side, part):
        def start(step, carry):
            out_copy(step, side, part, spot).start()
            return carry

        lax.fori_loop(1, layer, start, 0)
        target = landing(side, part, spot)
        target[...] = rout[out_rows(spot, side, part)]

    def out_finish(side, part):
        def finish(step, carry):
            out_copy(step, side, part, spot_after(layer - step)).wait_recv()
            return carry

        lax.fori_loop(1, layer, finish, 0)

    def out_sent():
        def finish(step, carry):
            for side in range(2):
                for part in range(2):
                    out_copy(step, side, part, spot).wait_send()
            return carry

        lax.fori_loop(1, layer, finish, 0)

    def to_partner(part):
        return remote(quads.at[own_quarter, part], quads.at[own_quarter, part], (near_s, near_r), part, partner)

    def to_across(part):
        return remote(hold.at[part], quads.at[own_quarter, part], (far_s, far_r), part, across)

    def pass_on(part):
        return remote(quads.at[far_quarter, part], quads.at[far_quarter, part], (relay_s, relay_r), part, partner)

    for part in range(2):
        out_start(0, part)
        out_start(1, part)
    moments = moment_finish(0, 1)
    moment_start(1, 8, moments)

    def drain(plane):
        hop_one(plane).wait_send()
        hop_two(plane).wait_send()
        hop_pass(plane).wait_send()

    loop(1, planes + 1, drain)
    for piece_number in range(2):
        for side in range(2):
            in_sent(piece_number, side)
    for part in range(2):
        out_finish(0, part)
        to_partner(part).start()
        out_finish(1, part)
        to_across(part).start()
    moment_ref[...] = moment_finish(1, 8)
    for part in range(2):
        to_across(part).wait_recv()
        pass_on(part).start()

    def share(part):
        slot = pl.ds(4 * core + 2 * part, 2)
        return remote(pot.at[slot], pot.at[slot], (e_s, e_r), part, sibling)

    def invert(part):
        to_partner(part).wait_recv()
        pass_on(part).wait_recv()
        columns = []
        for plane in range(planes // 2):
            blocks = [
                quads[which, part, pl.ds(plane * per + row, layer, stride=piece), :]
                for which in range(4)
                for row in range(per)
            ]
            columns.append(jnp.concatenate(blocks, axis=0))
        value = table_times(tab.at[0:2], jnp.concatenate(columns, axis=1))
        for pair in range(2):
            pot[4 * core + 2 * part + pair] = value[:, pair * cols : (pair + 1) * cols]
        share(part).start()

    def finish(part):
        share(part).wait_recv()
        value = [
            jnp.concatenate(
                [pot[4 * side + 2 * part + plane // 2, :, plane % 2 * lanes : (plane % 2 + 1) * lanes] for side in range(2)],
                axis=1,
            )
            for plane in range(planes // 2)
        ]
        value = times_table(jnp.concatenate(value, axis=0), tab.at[0:2])
        for plane in range(planes // 2):
            out_ref[part * (planes // 2) + plane] = value[plane * rows : (plane + 1) * rows]

    invert(0)
    finish(0)
    out_sent()
    invert(1)
    finish(1)
    for part in range(2):
        to_partner(part).wait_send()
        to_across(part).wait_send()
        pass_on(part).wait_send()
        share(part).wait_send()


def per_device(probes, potential, potential_change, coefficients):
    panel, planes, rows, cols = probes.shape
    slabs = lax.axis_size("slab")
    layer = slabs // 2
    depth = planes * slabs
    fourth = rows // 4
    size = 2 * planes * (fourth // layer)
    vmem = pl.BlockSpec(memory_space=pltpu.VMEM)
    anywhere = pl.BlockSpec(memory_space=pl.ANY)
    dma = pltpu.SemaphoreType.DMA
    high, low = cas_split(rows)
    order = shuffle(rows)
    forward = tables((high, low), (high[:, order], low[:, order]))
    high, low = cas_split(depth)
    spots = np.arange(layer)[:, None, None, None] // 4 * 8 + np.arange(layer)[:, None, None, None] % 4
    halves = np.arange(2)[None, None, :, None] * 4
    inner = np.array([list(range(2, planes - 2)), [0, 1, planes - 2, planes - 1]])[None, :, None, :]
    came = ((spots + halves) * planes + inner).reshape(-1)
    goes = ((spots[:, 0] + halves[:, 0]) * planes + np.arange(planes)).reshape(-1)
    deep = tables((high[:, came], low[:, came]), (high[goes], low[goes]))
    tall = rows + 2 * PAD
    hartree_change, total = pl.pallas_call(
        functools.partial(response_kernel, slabs, layer),
        out_shape=(
            pltpu.VMEM((planes, rows, cols), F32),
            jax.ShapeDtypeStruct((8, 128), F32),
        ),
        in_specs=[pl.BlockSpec(memory_space=pltpu.SMEM)] + [anywhere] * 5,
        out_specs=(vmem, vmem),
        scratch_shapes=[
            pltpu.VMEM((4, rows, cols), BF16),
            pltpu.VMEM((panel, planes + 2, rows, cols), BF16),
            pltpu.VMEM((planes, rows, cols), F32),
            pltpu.VMEM((planes, rows, cols), F32),
            pltpu.VMEM((4, rows, cols), F32),
            pltpu.VMEM((planes + 2, 2, rows, 128), F32),
            pltpu.VMEM((planes + 2, 2, rows, 128), F32),
            pltpu.VMEM((panel, planes + 2, 2, tall, 128), F32),
            pltpu.VMEM((panel, planes + 2, 2, tall, 128), F32),
            pltpu.VMEM((panel, planes + 2, 2, tall, 128), F32),
            pltpu.VMEM((panel, planes + 2, 2, tall, 128), F32),
            pltpu.VMEM((planes + 1, rows, cols), F32),
            pltpu.VMEM((2, rows, cols), BF16),
            pltpu.VMEM((2, rows, cols), BF16),
            pltpu.VMEM((planes + 1, 2, rows, 128), F32),
            pltpu.VMEM((planes + 1, rows, 128), F32),
            pltpu.VMEM((planes + 1, 2, fourth, 128), F32),
            pltpu.VMEM((7, 24, cols), F32),
            pltpu.VMEM((4, depth, depth), BF16),
            pltpu.VMEM((2, layer * size // 2, 128), F32),
            pltpu.VMEM((layer * size, 128), F32),
            pltpu.VMEM((depth, 4 * 128), F32),
            pltpu.VMEM((layer * size, 128), F32),
            pltpu.VMEM((2, layer * size // 4, 128), F32),
            pltpu.VMEM((4, 2, layer * size // 4, 128), F32),
            pltpu.VMEM((2, 4, 8, 128), F32),
            dma((5,)),
            dma((6,)), dma((6,)),
            dma((4,)), dma((4,)),
            dma((2,)), dma((2,)),
            dma((planes + 1,)), dma((planes + 1,)),
            dma((2, planes + 1)), dma((2, planes + 1)),
            dma((3,)), dma((3,)),
            dma((2, 2, layer)), dma((2, 2, layer)),
            dma((2, 2, layer)), dma((2, 2, layer)),
            dma((2,)), dma((2,)),
            dma((2,)), dma((2,)),
            dma((2,)), dma((2,)),
            dma((2,)), dma((2,)),
            dma((2, 4)), dma((2, 4)),
            pltpu.SemaphoreType.REGULAR((2,)),
        ],
        compiler_params=pltpu.CompilerParams(
            collective_id=0, has_side_effects=True, vmem_limit_bytes=56 * 1024 * 1024
        ),
        name="response",
    )(coefficients, forward, deep, probes, potential, potential_change)
    weights = jnp.array([1.0, 2.0, 1.0], F32) / (panel * lax.axis_size("probe") * depth * rows * cols)
    return hartree_change, total[:3, 0] * weights


def solution(mesh):
    return jax.shard_map(
        per_device,
        mesh=mesh,
        in_specs=(
            P("probe", "slab", None, None),
            P("slab", None, None),
            P("slab", None, None),
            P(),
        ),
        out_specs=(P("slab", None, None), P()),
        check_vma=False,
    )
```

```python
import functools
import math

import jax
import jax.numpy as jnp
import ml_dtypes
import numpy as np
from jax import lax
from jax.experimental import pallas as pl
from jax.experimental.pallas import tpu as pltpu
from jax.sharding import PartitionSpec as P

MESH = pl.DeviceIdType.MESH
F32 = jnp.float32
BF16 = jnp.bfloat16
KINETIC = 1.0 / 12.0
SCREEN = 0.05
PAD = 8
STEP = 16


def cas_split(size):
    index = np.arange(size)
    angle = (index[:, None] * index[None, :] % size) * (2.0 * np.pi / size)
    table = np.cos(angle) + np.sin(angle)
    high = table.astype(ml_dtypes.bfloat16)
    low = (table - high.astype(np.float64)).astype(ml_dtypes.bfloat16)
    return high, low


def shuffle(size):
    index = np.arange(size)
    return index % 8 * (size // 8) + index // 8


def tables(*pairs):
    return jnp.asarray(np.stack([part for pair in pairs for part in pair]))


def split(value):
    high = value.astype(BF16)
    low = (value - high.astype(F32)).astype(BF16)
    return high, low


def times_table(value, table):
    high, low = split(value)
    total = jnp.dot(high, table[0], preferred_element_type=F32)
    total = total + jnp.dot(high, table[1], preferred_element_type=F32)
    return total + jnp.dot(low, table[0], preferred_element_type=F32)


def table_times(table, value):
    high, low = split(value)
    total = jnp.dot(table[0], high, preferred_element_type=F32)
    total = total + jnp.dot(table[1], high, preferred_element_type=F32)
    return total + jnp.dot(table[0], low, preferred_element_type=F32)


def place():
    probe = lax.axis_index("probe")
    slab = lax.axis_index("slab")
    return probe, slab


def sibling_of(probe, slab):
    return {"probe": probe + 1 - 2 * lax.rem(probe, 2), "slab": slab}


def partner_of(probe, slab):
    return {"probe": lax.rem(probe + 2, 4), "slab": slab}


def greet(peers):
    barrier = pltpu.get_barrier_semaphore()
    for peer in peers:
        pl.semaphore_signal(barrier, inc=1, device_id=peer, device_id_type=MESH)
    pl.semaphore_wait(barrier, len(peers))


def remote(source, target, sems, index, peer):
    return pltpu.make_async_remote_copy(
        src_ref=source,
        dst_ref=target,
        send_sem=sems[0].at[index],
        recv_sem=sems[1].at[index],
        device_id=peer,
        device_id_type=MESH,
    )


def signed(index, size):
    return jnp.where(index <= size // 2, index, index - size).astype(F32) * (2.0 * math.pi / size)


def response_kernel(
    slabs, layer,
    coef_ref, table_ref, ztable_ref, probes_ref, pot_ref, change_ref,
    out_ref, moment_ref,
    tab, v16, pot, change, ghost_in, level_out, level_in, near, weight, v32, qbuf, tbuf, ubuf, dbuf,
    ybuf, rone, rtwo, mbuf,
    ztab, abuf, rin, kern, rout, hold, quads, mslots,
    load_sems, halo_s, halo_r, fwd_s, fwd_r, one_s, one_r, two_s, two_r, mom_s, mom_r,
    in_s, in_r, out_s, out_r, near_s, near_r, far_s, far_r, relay_s, relay_r, e_s, e_r, mslot_s, mslot_r, ready,
):
    probe, slab = place()
    core = lax.rem(probe, 2)
    zlow = probe // 2
    above = {"probe": probe, "slab": lax.rem(slab + 1, slabs)}
    below = {"probe": probe, "slab": lax.rem(slab + slabs - 1, slabs)}
    sibling = sibling_of(probe, slab)
    partner = partner_of(probe, slab)
    zhigh = lax.rem(slab // 4, 2)
    spot = slab // 8 * 4 + lax.rem(slab, 4)
    across = {"probe": lax.rem(probe + 2, 4), "slab": slab + 4 - 8 * zhigh}

    def spot_after(step):
        return lax.rem(spot + step, layer)

    def layer_peer(step):
        other = spot_after(step)
        return {"probe": probe, "slab": other // 4 * 8 + zhigh * 4 + lax.rem(other, 4)}

    def other_peer(step):
        other = spot_after(step)
        return {
            "probe": lax.rem(probe + 2, 4),
            "slab": other // 4 * 8 + (1 - zhigh) * 4 + lax.rem(other, 4),
        }

    planes = probes_ref.shape[1]
    rows, cols = probes_ref.shape[2], probes_ref.shape[3]
    half = rows // 2
    mine = pl.ds(pl.multiple_of(core * half, half), half)

    loads = [
        pltpu.make_async_copy(change_ref, change, load_sems.at[0]),
        pltpu.make_async_copy(pot_ref, pot, load_sems.at[1]),
        pltpu.make_async_copy(probes_ref, v16.at[:, 1 : planes + 1], load_sems.at[2]),
        pltpu.make_async_copy(table_ref, tab, load_sems.at[3]),
        pltpu.make_async_copy(ztable_ref, ztab, load_sems.at[4]),
    ]
    for load in loads:
        load.start()
    column = [{"probe": probe, "slab": slab - lax.rem(slab, 4) + lax.rem(slab + step, 4)} for step in range(1, 4)]
    row_peers = [{"probe": probe, "slab": lax.rem(slab + 8 * step, slabs)} for step in range(1, 4)]
    greet([above, below, sibling, partner, across] + column + row_peers)
    for peer in row_peers:
        pl.semaphore_signal(ready.at[0], inc=1, device_id=peer, device_id_type=MESH)
    halo = (halo_s, halo_r)
    copies = [
        remote(probes_ref.at[:, planes - 1 : planes], v16.at[:, 0:1], halo, 0, above),
        remote(probes_ref.at[:, 0:1], v16.at[:, planes + 1 : planes + 2], halo, 1, below),
    ]
    for copy in copies:
        copy.start()
    for index, (plane, peer) in enumerate(((planes - 1, above), (0, below))):
        copies.append(remote(change_ref.at[plane, mine], ghost_in.at[index, mine], halo, 2 + index, peer))
        copies[-1].start()
    for load in loads[:4]:
        load.wait()
    for index, (plane, peer) in enumerate(((planes - 1, above), (0, below))):
        level_out[index] = pot[plane, mine].astype(BF16)
        copies.append(remote(level_out.at[index], level_in.at[index, mine], halo, 4 + index, peer))
        copies[-1].start()

    lanes = cols // 2
    lane = lax.broadcasted_iota(jnp.int32, (STEP, lanes), 1)
    at_low, at_high = lane == 0, lane == lanes - 1
    inner = pl.ds(PAD, rows)

    def seal(buffer, *lead):
        for side in range(2):
            buffer[(*lead, side, pl.ds(0, PAD))] = pltpu.roll(buffer[(*lead, side, pl.ds(rows, PAD))], 1, 0)
            buffer[(*lead, side, pl.ds(rows + PAD, PAD))] = pltpu.roll(buffer[(*lead, side, pl.ds(PAD, PAD))], PAD - 1, 0)

    stretch = rows // 8

    def widen(plane, ghost=None):
        for step in range(8):
            here = pl.ds(step * stretch, stretch)
            spread = pl.ds(step, stretch, stride=8)
            wide = pl.ds(PAD + step, stretch, stride=8)
            local = change[plane - 1, here] if ghost is None else ghost_in[ghost, here]
            for side in range(2):
                part = slice(side * lanes, (side + 1) * lanes)
                weight[plane, side, spread, :] = local[:, part]
                if ghost is None:
                    near[plane, side, spread, :] = pot[plane - 1, here, part]
            for which in range(2):
                value = v16[which, plane, here].astype(F32)
                tangent = value * local
                for side in range(2):
                    part = slice(side * lanes, (side + 1) * lanes)
                    v32[which, plane, side, wide, :] = value[:, part]
                    qbuf[which, plane, side, wide, :] = tangent[:, part]
        for which in range(2):
            seal(v32, which, plane)
            seal(qbuf, which, plane)

    def level(plane, ghost):
        for step in range(8):
            for side in range(2):
                part = slice(side * lanes, (side + 1) * lanes)
                value = level_in[ghost, step * stretch : (step + 1) * stretch, part].astype(F32)
                near[plane, side, pl.ds(step, stretch, stride=8), :] = value

    def beside(buffer, which, plane, row, steps):
        middle, total = [], []
        for side in range(2):
            tall = buffer[which, plane, side, row : row + STEP + 2 * PAD]
            middle.append(tall[PAD : PAD + STEP])
            around = tall[:STEP] + tall[2 * PAD :]
            for step in steps:
                around = around + buffer[which, plane + step, side, row + PAD : row + PAD + STEP]
            total.append(around)
        left = [pltpu.roll(value, 1, 1) for value in middle]
        right = [pltpu.roll(value, lanes - 1, 1) for value in middle]
        for side in range(2):
            beyond = jnp.where(at_low, left[1 - side], left[side])
            beyond = beyond + jnp.where(at_high, right[1 - side], right[side])
            total[side] = total[side] + beyond
        return middle, total

    def first(plane, steps=(-1, 1)):
        for row in range(0, rows, STEP):
            here = slice(row, row + STEP)
            there = slice(row + PAD, row + PAD + STEP)
            for which in range(2):
                terms, around = beside(v32, which, plane, row, steps)
                tangents, beyond = beside(qbuf, which, plane, row, steps)
                for side in range(2):
                    local = near[plane, side, here]
                    term = local * terms[side] - KINETIC * around[side]
                    tbuf[which, plane, side, there] = term
                    ubuf[which, plane, side, there] = (
                        local * tangents[side] - KINETIC * beyond[side] + weight[plane, side, here] * term
                    )
        for which in range(2):
            seal(tbuf, which, plane)
            seal(ubuf, which, plane)

    mbuf[0:2] = jnp.zeros((2, 24, cols), F32)

    def fold(value):
        total = value[0:8]
        for index in range(1, value.shape[0] // 8):
            total = total + value[8 * index : 8 * index + 8]
        return total

    def count(order, side, value):
        mbuf[0, pl.ds(8 * order, 8), side * lanes : (side + 1) * lanes] += fold(value)

    def last(plane):
        tallies = [[0.0] * 3, [0.0] * 3]
        for row in range(0, rows, STEP):
            here = slice(row, row + STEP)
            there = slice(row + PAD, row + PAD + STEP)
            sums = [None, None]
            for which in range(2):
                terms, around = beside(tbuf, which, plane, row, (-1, 1))
                mixes, beyond = beside(ubuf, which, plane, row, (-1, 1))
                for side in range(2):
                    local = near[plane, side, here]
                    vector = v32[which, plane, side, there]
                    tangent = qbuf[which, plane, side, there]
                    image = local * terms[side] - KINETIC * around[side]
                    third = local * mixes[side] - KINETIC * beyond[side] + weight[plane, side, here] * image
                    parts = (vector * tangent, vector * mixes[side], vector * (4.0 * third - 3.0 * tangent))
                    sums[side] = parts if sums[side] is None else tuple(a + b for a, b in zip(sums[side], parts))
            for side in range(2):
                for order in range(3):
                    tallies[side][order] = tallies[side][order] + fold(sums[side][order])
                dbuf[plane, here, side * lanes : (side + 1) * lanes] = (
                    coef_ref[0] * sums[side][0] + (2.0 * coef_ref[1]) * sums[side][1] + coef_ref[2] * sums[side][2]
                )
        for side in range(2):
            for order in range(3):
                mbuf[0, pl.ds(8 * order, 8), side * lanes : (side + 1) * lanes] += tallies[side][order]

    def pairs(target, planes_of):
        low, mid, high = planes_of
        for side in range(2):
            product = v32[0, low, side, inner] * v32[0, high, side, inner]
            product = product + v32[1, low, side, inner] * v32[1, high, side, inner]
            total = weight[low, side] + weight[mid, side] + weight[high, side]
            value = (4.0 * KINETIC * KINETIC) * total * product
            count(2, side, value)
            dbuf[target, :, side * lanes : (side + 1) * lanes] = coef_ref[2] * value

    def hop_one(plane):
        return remote(ybuf.at[plane, 1 - core], rone.at[plane], (one_s, one_r), plane, sibling)

    fourth = rows // 4
    per = fourth // layer
    depth = planes * slabs
    size = 2 * planes * per

    def quarter(low, high):
        return pl.ds(pl.multiple_of((2 * low + high) * fourth, fourth), fourth)

    def hop_two(plane):
        return remote(
            ybuf.at[plane, core, quarter(1 - zlow, zhigh)], rtwo.at[plane, 0], (two_s.at[0], two_r.at[0]), plane, partner
        )

    def hop_pass(plane):
        return remote(
            ybuf.at[plane, core, quarter(zlow, 1 - zhigh)], rtwo.at[plane, 1], (two_s.at[1], two_r.at[1]), plane, partner
        )

    def transform(group):
        count = len(group)
        value = jnp.concatenate([dbuf[plane] for plane in group], axis=0)
        value = times_table(value, tab.at[0:2])
        value = jnp.concatenate([value[index * rows : (index + 1) * rows] for index in range(count)], axis=1)
        value = table_times(tab.at[2:4], value)
        for index, plane in enumerate(group):
            ybuf[plane, 0] = value[:, index * cols : index * cols + lanes]
            ybuf[plane, 1] = value[:, index * cols + lanes : (index + 1) * cols]
            hop_one(plane).start()

    def merge(plane):
        hop_one(plane).wait_recv()
        ybuf[plane, core] = ybuf[plane, core] + rone[plane]
        hop_pass(plane).start()
        hop_two(plane).start()

    inside = list(range(3, planes - 1))
    outside = [0, planes + 1, 1, 2, planes - 1, planes]
    pieces = ((0, len(inside) * per), (len(inside) * per, len(outside) * per))
    sent_rows = (planes + 2) * per

    def spread(plane, side, value):
        group = inside if plane in inside else outside
        first_row = (0 if plane in inside else pieces[1][0]) + group.index(plane) * per
        for row in range(per):
            abuf[side, pl.ds(first_row + row, layer, stride=sent_rows), :] = value[row * layer : (row + 1) * layer]

    def relay(plane):
        hop_pass(plane).wait_recv()
        spread(plane, 1, ybuf[plane, core, quarter(1 - zlow, 1 - zhigh)] + rtwo[plane, 1])

    def settle(plane):
        hop_two(plane).wait_recv()
        spread(plane, 0, ybuf[plane, core, quarter(zlow, zhigh)] + rtwo[plane, 0])

    def in_from(place_of, piece):
        start, length = pieces[piece]
        return pl.ds(pl.multiple_of(place_of * sent_rows + start, 8), length)

    def in_rows(place_of, piece, which):
        start, length = pieces[piece]
        return pl.ds(pl.multiple_of(place_of * (2 * sent_rows) + 2 * start + which * length, 8), length)

    def in_copy(step, piece, side, here):
        source = abuf.at[side, in_from(spot_after(step), piece)]
        peer = layer_peer(step) if side == 0 else other_peer(step)
        return remote(source, rin.at[here], (in_s.at[piece, side], in_r.at[piece, side]), step, peer)

    def in_start(piece, side):
        def start(step, carry):
            in_copy(step, piece, side, in_rows(spot, piece, zhigh)).start()
            return carry

        lax.fori_loop(1 - side, layer, start, 0)
        if side == 0:
            rin[in_rows(spot, piece, zhigh)] = abuf[0, in_from(spot, piece)]

    def in_sent(piece, side):
        def finish(step, carry):
            in_copy(step, piece, side, in_rows(spot, piece, zhigh)).wait_send()
            return carry

        lax.fori_loop(1 - side, layer, finish, 0)

    def in_finish(piece):
        for side in range(2):
            def finish(step, carry):
                place_of = lax.rem(spot + layer - step, layer)
                which = zhigh if side == 0 else 1 - zhigh
                in_copy(step, piece, side, in_rows(place_of, piece, which)).wait_recv()
                return carry

            lax.fori_loop(1 - side, layer, finish, 0)

    def loop(low, high, body):
        def step(index, carry):
            body(index)
            return carry

        lax.fori_loop(low, high, step, 0)

    def both(body, low, high):
        def step(index, carry):
            body(jnp.where(index == 0, low, high))
            return carry

        lax.fori_loop(0, 2, step, 0)

    fwd = (fwd_s, fwd_r)
    forwards = [
        remote(ghosts.at[index, mine], ghosts.at[index, mine], fwd, number * 2 + index, sibling)
        for number, ghosts in enumerate((ghost_in, level_in))
        for index in range(2)
    ]
    loop(1, planes + 1, widen)
    loop(2, planes, first)
    loop(3, planes - 1, last)
    for copy in copies[2:]:
        copy.wait()
    for copy in forwards:
        copy.start()
    transform(inside)
    pl.semaphore_wait(ready.at[0], 3)
    pl.semaphore_signal(ready.at[1], inc=1, device_id=across, device_id_type=MESH)
    for copy in copies[:2]:
        copy.wait()
    for copy in forwards:
        copy.wait()
    widen(0, 0)
    widen(planes + 1, 1)
    pairs(0, (0, 1, 2))
    pairs(planes + 1, (planes - 1, planes, planes + 1))
    loop(3, planes - 1, merge)
    transform([0, planes + 1])
    both(first, 1, planes)
    both(merge, 0, planes + 1)
    both(last, 2, planes - 1)
    transform([2, planes - 1])
    for plane in inside:
        relay(plane)
    pl.semaphore_wait(ready.at[1], 1)
    in_start(0, 1)
    both(merge, 2, planes - 1)
    for plane in inside:
        settle(plane)
    in_start(0, 0)
    level(0, 0)
    level(planes + 1, 1)
    first(0, (1,))
    first(planes + 1, (-1,))
    both(last, 1, planes)
    transform([1, planes])

    mom = (mom_s, mom_r)
    for order in range(3):
        strip = jnp.sum(mbuf[0, pl.ds(8 * order, 8)], axis=0, keepdims=True)
        total = jnp.sum(strip, axis=1, keepdims=True)
        mbuf[1, pl.ds(order, 1)] = jnp.broadcast_to(total, (1, cols))
    swap = remote(mbuf.at[1, 0:8], mbuf.at[2, 0:8], mom, 0, sibling)
    swap.start()
    for plane in (0, planes + 1, 2, planes - 1):
        relay(plane)
        settle(plane)
    both(merge, 1, planes)
    swap.wait()
    mbuf[3, 0:8] = mbuf[1, 0:8] + mbuf[2, 0:8]
    swap = remote(mbuf.at[3, 0:8], mbuf.at[4, 0:8], mom, 1, partner)
    swap.start()
    relay(1)
    relay(planes)
    in_start(1, 1)
    settle(1)
    settle(planes)
    in_start(1, 0)
    swap.wait()
    mbuf[5, 0:8] = mbuf[3, 0:8] + mbuf[4, 0:8]
    swap = remote(mbuf.at[5, 0:8], mbuf.at[6, 0:8], mom, 2, across)
    swap.start()

    wave_z = signed(lax.broadcasted_iota(jnp.int32, (depth, lanes), 0), depth)
    wave_x = signed(lax.broadcasted_iota(jnp.int32, (depth, lanes), 1) + core * lanes, cols)
    base = wave_z * wave_z + wave_x * wave_x
    for row in range(per):
        number = (2 * zlow + zhigh) * fourth + row * layer + spot
        wave_y = signed(jnp.full((depth, lanes), number, jnp.int32), rows)
        summed = base + wave_y * wave_y
        value = (4.0 * math.pi / (8.0 * depth * rows * cols)) / (summed + SCREEN * SCREEN)
        kern[:, row * lanes : (row + 1) * lanes] = jnp.where(summed == 0.0, 0.0, value)
    loads[4].wait()

    def moment_round(number, stride):
        where = lax.rem(slab // stride, 4)
        copies, waits = [], []
        for step in range(1, 4):
            peer = {"probe": probe, "slab": slab + (lax.rem(where + step, 4) - where) * stride}
            source = lax.rem(where + 4 - step, 4)
            sems = (mslot_s.at[number], mslot_r.at[number])
            copies.append(remote(mslots.at[number, where], mslots.at[number, where], sems, step, peer))
            waits.append(remote(mslots.at[number, source], mslots.at[number, source], sems, step, peer))
        return where, copies, waits

    def moment_start(number, stride, value):
        where, copies, waits = moment_round(number, stride)
        mslots[number, where] = value
        for copy in copies:
            copy.start()

    def moment_finish(number, stride):
        where, copies, waits = moment_round(number, stride)
        for copy in waits:
            copy.wait_recv()
        for copy in copies:
            copy.wait_send()
        return (mslots[number, 0] + mslots[number, 1]) + (mslots[number, 2] + mslots[number, 3])

    in_finish(0)
    swap.wait()
    moment_start(0, 1, (mbuf[5, 0:8] + mbuf[6, 0:8])[:, :128])
    in_finish(1)
    came = 2 * (planes + 2) * layer
    columns = jnp.concatenate([rin[pl.ds(row, came, stride=per), :] for row in range(per)], axis=1)
    here = lax.broadcasted_iota(jnp.int32, (1, per * lanes), 1) + (probe + slab) * (per * lanes)
    mean = jnp.where(here == 0, jnp.sum(columns, axis=0, keepdims=True) * (1.0 / depth), 0.0)
    number = lax.rem(lax.broadcasted_iota(jnp.int32, (came, per * lanes), 0), 2 * (planes + 2))
    count = len(inside)
    number = number - 2 * count
    number = jnp.where(number >= len(outside), number - len(outside), number)
    columns = jnp.where((number == 0) | (number == 1), columns, columns - mean)
    columns = table_times((ztab[0, :, :came], ztab[1, :, :came]), columns) * kern[...]
    columns = table_times((ztab[2, :, :depth], ztab[3, :, :depth]), columns)
    for row in range(per):
        rout[pl.ds(row, depth, stride=per), :] = columns[:, row * lanes : (row + 1) * lanes]

    piece = planes // 2 * per
    own_quarter = 2 * zlow + zhigh
    far_quarter = 2 * (1 - zlow) + (1 - zhigh)

    def out_rows(place_of, side, part):
        which = zhigh if side == 0 else 1 - zhigh
        return pl.ds(pl.multiple_of(place_of * size + which * (size // 2) + part * piece, piece), piece)

    def landing(side, part, place_of):
        rows_at = pl.ds(pl.multiple_of(place_of * piece, piece), piece)
        return quads.at[own_quarter, part, rows_at] if side == 0 else hold.at[part, rows_at]

    def out_copy(step, side, part, place_of):
        source = rout.at[out_rows(spot_after(step), side, part)]
        sems = (out_s.at[side, part], out_r.at[side, part])
        return remote(source, landing(side, part, place_of), sems, step, layer_peer(step))

    def out_start(side, part):
        def start(step, carry):
            out_copy(step, side, part, spot).start()
            return carry

        lax.fori_loop(1, layer, start, 0)
        target = landing(side, part, spot)
        target[...] = rout[out_rows(spot, side, part)]

    def out_finish(side, part):
        def finish(step, carry):
            out_copy(step, side, part, spot_after(layer - step)).wait_recv()
            return carry

        lax.fori_loop(1, layer, finish, 0)

    def out_sent():
        def finish(step, carry):
            for side in range(2):
                for part in range(2):
                    out_copy(step, side, part, spot).wait_send()
            return carry

        lax.fori_loop(1, layer, finish, 0)

    def to_partner(part):
        return remote(quads.at[own_quarter, part], quads.at[own_quarter, part], (near_s, near_r), part, partner)

    def to_across(part):
        return remote(hold.at[part], quads.at[own_quarter, part], (far_s, far_r), part, across)

    def pass_on(part):
        return remote(quads.at[far_quarter, part], quads.at[far_quarter, part], (relay_s, relay_r), part, partner)

    for part in range(2):
        out_start(0, part)
        out_start(1, part)
    moments = moment_finish(0, 1)
    moment_start(1, 8, moments)

    def drain(plane):
        hop_one(plane).wait_send()
        hop_two(plane).wait_send()
        hop_pass(plane).wait_send()

    loop(0, planes + 2, drain)
    for piece_number in range(2):
        for side in range(2):
            in_sent(piece_number, side)
    for part in range(2):
        out_finish(0, part)
        to_partner(part).start()
        out_finish(1, part)
        to_across(part).start()
    moment_ref[...] = moment_finish(1, 8)
    for part in range(2):
        to_across(part).wait_recv()
        pass_on(part).start()

    def share(part, pair):
        slot = 4 * core + 2 * part + pair
        return remote(pot.at[slot], pot.at[slot], (e_s, e_r), 2 * part + pair, sibling)

    def invert(part):
        to_partner(part).wait_recv()
        pass_on(part).wait_recv()
        for pair in range(2):
            columns = []
            for plane in (2 * pair, 2 * pair + 1):
                blocks = [
                    quads[which, part, pl.ds(plane * per + row, layer, stride=piece), :]
                    for which in range(4)
                    for row in range(per)
                ]
                columns.append(jnp.concatenate(blocks, axis=0))
            pot[4 * core + 2 * part + pair] = table_times(tab.at[0:2], jnp.concatenate(columns, axis=1))
            share(part, pair).start()

    def finish(part):
        for pair in range(2):
            share(part, pair).wait_recv()
            sides = [pot[4 * side + 2 * part + pair] for side in range(2)]
            value = [
                jnp.concatenate([side[:, plane * lanes : (plane + 1) * lanes] for side in sides], axis=1)
                for plane in range(2)
            ]
            value = times_table(jnp.concatenate(value, axis=0), tab.at[0:2])
            for plane in range(2):
                out_ref[part * (planes // 2) + 2 * pair + plane] = value[plane * rows : (plane + 1) * rows]

    invert(0)
    finish(0)
    out_sent()
    invert(1)
    finish(1)
    for part in range(2):
        to_partner(part).wait_send()
        to_across(part).wait_send()
        pass_on(part).wait_send()
        for pair in range(2):
            share(part, pair).wait_send()


def per_device(probes, potential, potential_change, coefficients):
    panel, planes, rows, cols = probes.shape
    slabs = lax.axis_size("slab")
    layer = slabs // 2
    depth = planes * slabs
    half = rows // 2
    fourth = rows // 4
    size = 2 * planes * (fourth // layer)
    vmem = pl.BlockSpec(memory_space=pltpu.VMEM)
    anywhere = pl.BlockSpec(memory_space=pl.ANY)
    dma = pltpu.SemaphoreType.DMA
    high, low = cas_split(rows)
    order = shuffle(rows)
    forward = tables((high, low), (high[:, order], low[:, order]))
    high, low = cas_split(depth)
    spots = np.arange(layer)[:, None, None, None] // 4 * 8 + np.arange(layer)[:, None, None, None] % 4
    halves = np.arange(2)[None, None, :, None] * 4
    inner = [list(range(2, planes - 2)), [-1, planes, 0, 1, planes - 2, planes - 1]]
    came = [
        (np.arange(layer)[:, None, None] // 4 * 8 + np.arange(layer)[:, None, None] % 4 + halves[0, 0]) * planes
        + np.array(group)
        for group in inner
    ]
    came = np.concatenate([part.reshape(layer, -1) for part in came], axis=1).reshape(-1) % depth
    goes = ((spots[:, 0] + halves[:, 0]) * planes + np.arange(planes)).reshape(-1)
    extra = np.zeros((depth, len(came) - depth), high.dtype)
    back = [np.concatenate([part[goes], extra], axis=1) for part in (high, low)]
    deep = tables((high[:, came], low[:, came]), back)
    tall = rows + 2 * PAD
    hartree_change, total = pl.pallas_call(
        functools.partial(response_kernel, slabs, layer),
        out_shape=(
            pltpu.VMEM((planes, rows, cols), F32),
            jax.ShapeDtypeStruct((8, 128), F32),
        ),
        in_specs=[pl.BlockSpec(memory_space=pltpu.SMEM)] + [anywhere] * 5,
        out_specs=(vmem, vmem),
        scratch_shapes=[
            pltpu.VMEM((4, rows, cols), BF16),
            pltpu.VMEM((panel, planes + 2, rows, cols), BF16),
            pltpu.VMEM((planes, rows, cols), F32),
            pltpu.VMEM((planes, rows, cols), F32),
            pltpu.VMEM((2, rows, cols), F32),
            pltpu.VMEM((2, half, cols), BF16),
            pltpu.VMEM((2, rows, cols), BF16),
            pltpu.VMEM((planes + 2, 2, rows, 128), F32),
            pltpu.VMEM((planes + 2, 2, rows, 128), F32),
            pltpu.VMEM((panel, planes + 2, 2, tall, 128), F32),
            pltpu.VMEM((panel, planes + 2, 2, tall, 128), F32),
            pltpu.VMEM((panel, planes + 2, 2, tall, 128), F32),
            pltpu.VMEM((panel, planes + 2, 2, tall, 128), F32),
            pltpu.VMEM((planes + 2, rows, cols), F32),
            pltpu.VMEM((planes + 2, 2, rows, 128), F32),
            pltpu.VMEM((planes + 2, rows, 128), F32),
            pltpu.VMEM((planes + 2, 2, fourth, 128), F32),
            pltpu.VMEM((7, 24, cols), F32),
            pltpu.VMEM((4, depth, len(came)), BF16),
            pltpu.VMEM((2, len(came) // 2 * 4, 128), F32),
            pltpu.VMEM((len(came) * 4, 128), F32),
            pltpu.VMEM((depth, 4 * 128), F32),
            pltpu.VMEM((layer * size, 128), F32),
            pltpu.VMEM((2, layer * size // 4, 128), F32),
            pltpu.VMEM((4, 2, layer * size // 4, 128), F32),
            pltpu.VMEM((2, 4, 8, 128), F32),
            dma((5,)),
            dma((6,)), dma((6,)),
            dma((4,)), dma((4,)),
            dma((planes + 2,)), dma((planes + 2,)),
            dma((2, planes + 2)), dma((2, planes + 2)),
            dma((3,)), dma((3,)),
            dma((2, 2, layer)), dma((2, 2, layer)),
            dma((2, 2, layer)), dma((2, 2, layer)),
            dma((2,)), dma((2,)),
            dma((2,)), dma((2,)),
            dma((2,)), dma((2,)),
            dma((4,)), dma((4,)),
            dma((2, 4)), dma((2, 4)),
            pltpu.SemaphoreType.REGULAR((2,)),
        ],
        compiler_params=pltpu.CompilerParams(
            collective_id=0, has_side_effects=True, vmem_limit_bytes=56 * 1024 * 1024
        ),
        name="response",
    )(coefficients, forward, deep, probes, potential, potential_change)
    weights = jnp.array([1.0, 2.0, 1.0], F32) / (panel * lax.axis_size("probe") * depth * rows * cols)
    return hartree_change, total[:3, 0] * weights


def solution(mesh):
    return jax.shard_map(
        per_device,
        mesh=mesh,
        in_specs=(
            P("probe", "slab", None, None),
            P("slab", None, None),
            P("slab", None, None),
            P(),
        ),
        out_specs=(P("slab", None, None), P()),
        check_vma=False,
    )
```

```python
import functools
import math

import jax
import jax.numpy as jnp
import ml_dtypes
import numpy as np
from jax import lax
from jax.experimental import pallas as pl
from jax.experimental.pallas import tpu as pltpu
from jax.sharding import PartitionSpec as P

MESH = pl.DeviceIdType.MESH
F32 = jnp.float32
BF16 = jnp.bfloat16
KINETIC = 1.0 / 12.0
SCREEN = 0.05
PAD = 8
STEP = 16


def cas_split(size):
    index = np.arange(size)
    angle = (index[:, None] * index[None, :] % size) * (2.0 * np.pi / size)
    table = np.cos(angle) + np.sin(angle)
    high = table.astype(ml_dtypes.bfloat16)
    low = (table - high.astype(np.float64)).astype(ml_dtypes.bfloat16)
    return high, low


def shuffle(size):
    index = np.arange(size)
    return index % 8 * (size // 8) + index // 8


def tables(*pairs):
    return jnp.asarray(np.stack([part for pair in pairs for part in pair]))


def split(value):
    high = value.astype(BF16)
    low = (value - high.astype(F32)).astype(BF16)
    return high, low


def times_table(value, table):
    high, low = split(value)
    total = jnp.dot(high, table[0], preferred_element_type=F32)
    total = total + jnp.dot(high, table[1], preferred_element_type=F32)
    return total + jnp.dot(low, table[0], preferred_element_type=F32)


def table_times(table, value):
    high, low = split(value)
    total = jnp.dot(table[0], high, preferred_element_type=F32)
    total = total + jnp.dot(table[1], high, preferred_element_type=F32)
    return total + jnp.dot(table[0], low, preferred_element_type=F32)


def place():
    probe = lax.axis_index("probe")
    slab = lax.axis_index("slab")
    return probe, slab


def sibling_of(probe, slab):
    return {"probe": probe + 1 - 2 * lax.rem(probe, 2), "slab": slab}


def partner_of(probe, slab):
    return {"probe": lax.rem(probe + 2, 4), "slab": slab}


def greet(peers):
    barrier = pltpu.get_barrier_semaphore()
    for peer in peers:
        pl.semaphore_signal(barrier, inc=1, device_id=peer, device_id_type=MESH)
    pl.semaphore_wait(barrier, len(peers))


def remote(source, target, sems, index, peer):
    return pltpu.make_async_remote_copy(
        src_ref=source,
        dst_ref=target,
        send_sem=sems[0].at[index],
        recv_sem=sems[1].at[index],
        device_id=peer,
        device_id_type=MESH,
    )


def signed(index, size):
    return jnp.where(index <= size // 2, index, index - size).astype(F32) * (2.0 * math.pi / size)


def response_kernel(
    slabs, layer,
    coef_ref, table_ref, ztable_ref, probes_ref, pot_ref, change_ref,
    out_ref, moment_ref,
    tab, v16, pot, change, ghost_in, level_out, level_in, near, weight, v32, qbuf, tbuf, ubuf, dbuf,
    ybuf, rone, rtwo, mbuf,
    ztab, abuf, rin, kern, rout, hold, quads, mslots,
    load_sems, halo_s, halo_r, fwd_s, fwd_r, one_s, one_r, two_s, two_r, mom_s, mom_r,
    in_s, in_r, out_s, out_r, near_s, near_r, far_s, far_r, relay_s, relay_r, e_s, e_r, mslot_s, mslot_r, ready,
):
    probe, slab = place()
    core = lax.rem(probe, 2)
    zlow = probe // 2
    above = {"probe": probe, "slab": lax.rem(slab + 1, slabs)}
    below = {"probe": probe, "slab": lax.rem(slab + slabs - 1, slabs)}
    sibling = sibling_of(probe, slab)
    partner = partner_of(probe, slab)
    zhigh = lax.rem(slab // 4, 2)
    spot = slab // 8 * 4 + lax.rem(slab, 4)
    across = {"probe": lax.rem(probe + 2, 4), "slab": slab + 4 - 8 * zhigh}

    def spot_after(step):
        return lax.rem(spot + step, layer)

    def layer_peer(step):
        other = spot_after(step)
        return {"probe": probe, "slab": other // 4 * 8 + zhigh * 4 + lax.rem(other, 4)}

    def other_peer(step):
        other = spot_after(step)
        return {
            "probe": lax.rem(probe + 2, 4),
            "slab": other // 4 * 8 + (1 - zhigh) * 4 + lax.rem(other, 4),
        }

    planes = probes_ref.shape[1]
    rows, cols = probes_ref.shape[2], probes_ref.shape[3]
    half = rows // 2
    mine = pl.ds(pl.multiple_of(core * half, half), half)

    loads = [
        pltpu.make_async_copy(change_ref, change, load_sems.at[0]),
        pltpu.make_async_copy(pot_ref, pot, load_sems.at[1]),
        pltpu.make_async_copy(probes_ref, v16.at[:, 1 : planes + 1], load_sems.at[2]),
        pltpu.make_async_copy(table_ref, tab, load_sems.at[3]),
        pltpu.make_async_copy(ztable_ref, ztab, load_sems.at[4]),
    ]
    for load in loads:
        load.start()
    column = [{"probe": probe, "slab": slab - lax.rem(slab, 4) + lax.rem(slab + step, 4)} for step in range(1, 4)]
    row_peers = [{"probe": probe, "slab": lax.rem(slab + 8 * step, slabs)} for step in range(1, 4)]
    greet([above, below, sibling, partner, across] + column + row_peers)
    for peer in row_peers:
        pl.semaphore_signal(ready.at[0], inc=1, device_id=peer, device_id_type=MESH)
    halo = (halo_s, halo_r)
    copies = [
        remote(probes_ref.at[:, planes - 1 : planes], v16.at[:, 0:1], halo, 0, above),
        remote(probes_ref.at[:, 0:1], v16.at[:, planes + 1 : planes + 2], halo, 1, below),
    ]
    for copy in copies:
        copy.start()
    for index, (plane, peer) in enumerate(((planes - 1, above), (0, below))):
        copies.append(remote(change_ref.at[plane, mine], ghost_in.at[index, mine], halo, 2 + index, peer))
        copies[-1].start()
    for load in loads[:4]:
        load.wait()
    for index, (plane, peer) in enumerate(((planes - 1, above), (0, below))):
        level_out[index] = pot[plane, mine].astype(BF16)
        copies.append(remote(level_out.at[index], level_in.at[index, mine], halo, 4 + index, peer))
        copies[-1].start()

    lanes = cols // 2
    lane = lax.broadcasted_iota(jnp.int32, (STEP, lanes), 1)
    at_low, at_high = lane == 0, lane == lanes - 1
    inner = pl.ds(PAD, rows)

    def seal(buffer, *lead):
        for side in range(2):
            buffer[(*lead, side, pl.ds(0, PAD))] = pltpu.roll(buffer[(*lead, side, pl.ds(rows, PAD))], 1, 0)
            buffer[(*lead, side, pl.ds(rows + PAD, PAD))] = pltpu.roll(buffer[(*lead, side, pl.ds(PAD, PAD))], PAD - 1, 0)

    stretch = rows // 8

    def widen(plane, ghost=None):
        for step in range(8):
            here = pl.ds(step * stretch, stretch)
            spread = pl.ds(step, stretch, stride=8)
            wide = pl.ds(PAD + step, stretch, stride=8)
            local = change[plane - 1, here] if ghost is None else ghost_in[ghost, here]
            for side in range(2):
                part = slice(side * lanes, (side + 1) * lanes)
                weight[plane, side, spread, :] = local[:, part]
                if ghost is None:
                    near[plane, side, spread, :] = pot[plane - 1, here, part]
            for which in range(2):
                value = v16[which, plane, here].astype(F32)
                tangent = value * local
                for side in range(2):
                    part = slice(side * lanes, (side + 1) * lanes)
                    v32[which, plane, side, wide, :] = value[:, part]
                    qbuf[which, plane, side, wide, :] = tangent[:, part]
        for which in range(2):
            seal(v32, which, plane)
            seal(qbuf, which, plane)

    def level(plane, ghost):
        for step in range(8):
            for side in range(2):
                part = slice(side * lanes, (side + 1) * lanes)
                value = level_in[ghost, step * stretch : (step + 1) * stretch, part].astype(F32)
                near[plane, side, pl.ds(step, stretch, stride=8), :] = value

    def beside(buffer, which, plane, row, steps):
        middle, total = [], []
        for side in range(2):
            tall = buffer[which, plane, side, row : row + STEP + 2 * PAD]
            middle.append(tall[PAD : PAD + STEP])
            around = tall[:STEP] + tall[2 * PAD :]
            for step in steps:
                around = around + buffer[which, plane + step, side, row + PAD : row + PAD + STEP]
            total.append(around)
        left = [pltpu.roll(value, 1, 1) for value in middle]
        right = [pltpu.roll(value, lanes - 1, 1) for value in middle]
        for side in range(2):
            beyond = jnp.where(at_low, left[1 - side], left[side])
            beyond = beyond + jnp.where(at_high, right[1 - side], right[side])
            total[side] = total[side] + beyond
        return middle, total

    def first(plane, steps=(-1, 1)):
        for row in range(0, rows, STEP):
            here = slice(row, row + STEP)
            there = slice(row + PAD, row + PAD + STEP)
            for which in range(2):
                terms, around = beside(v32, which, plane, row, steps)
                tangents, beyond = beside(qbuf, which, plane, row, steps)
                for side in range(2):
                    local = near[plane, side, here]
                    term = local * terms[side] - KINETIC * around[side]
                    tbuf[which, plane, side, there] = term
                    ubuf[which, plane, side, there] = (
                        local * tangents[side] - KINETIC * beyond[side] + weight[plane, side, here] * term
                    )
        for which in range(2):
            seal(tbuf, which, plane)
            seal(ubuf, which, plane)

    mbuf[0:2] = jnp.zeros((2, 24, cols), F32)

    def fold(value):
        total = value[0:8]
        for index in range(1, value.shape[0] // 8):
            total = total + value[8 * index : 8 * index + 8]
        return total

    def count(order, side, value):
        mbuf[0, pl.ds(8 * order, 8), side * lanes : (side + 1) * lanes] += fold(value)

    def last(plane):
        tallies = [[0.0] * 3, [0.0] * 3]
        for row in range(0, rows, STEP):
            here = slice(row, row + STEP)
            there = slice(row + PAD, row + PAD + STEP)
            sums = [None, None]
            for which in range(2):
                terms, around = beside(tbuf, which, plane, row, (-1, 1))
                mixes, beyond = beside(ubuf, which, plane, row, (-1, 1))
                for side in range(2):
                    local = near[plane, side, here]
                    vector = v32[which, plane, side, there]
                    tangent = qbuf[which, plane, side, there]
                    image = local * terms[side] - KINETIC * around[side]
                    third = local * mixes[side] - KINETIC * beyond[side] + weight[plane, side, here] * image
                    parts = (vector * tangent, vector * mixes[side], vector * (4.0 * third - 3.0 * tangent))
                    sums[side] = parts if sums[side] is None else tuple(a + b for a, b in zip(sums[side], parts))
            for side in range(2):
                for order in range(3):
                    tallies[side][order] = tallies[side][order] + fold(sums[side][order])
                dbuf[plane, here, side * lanes : (side + 1) * lanes] = (
                    coef_ref[0] * sums[side][0] + (2.0 * coef_ref[1]) * sums[side][1] + coef_ref[2] * sums[side][2]
                )
        for side in range(2):
            for order in range(3):
                mbuf[0, pl.ds(8 * order, 8), side * lanes : (side + 1) * lanes] += tallies[side][order]

    def pairs(target, planes_of):
        low, mid, high = planes_of
        for side in range(2):
            product = v32[0, low, side, inner] * v32[0, high, side, inner]
            product = product + v32[1, low, side, inner] * v32[1, high, side, inner]
            total = weight[low, side] + weight[mid, side] + weight[high, side]
            value = (4.0 * KINETIC * KINETIC) * total * product
            count(2, side, value)
            dbuf[target, :, side * lanes : (side + 1) * lanes] = coef_ref[2] * value

    def hop_one(plane):
        return remote(ybuf.at[plane, 1 - core], rone.at[plane], (one_s, one_r), plane, sibling)

    fourth = rows // 4
    per = fourth // layer
    depth = planes * slabs
    size = 2 * planes * per

    def quarter(low, high):
        return pl.ds(pl.multiple_of((2 * low + high) * fourth, fourth), fourth)

    def hop_two(plane):
        return remote(
            ybuf.at[plane, core, quarter(1 - zlow, zhigh)], rtwo.at[plane, 0], (two_s.at[0], two_r.at[0]), plane, partner
        )

    def hop_pass(plane):
        return remote(
            ybuf.at[plane, core, quarter(zlow, 1 - zhigh)], rtwo.at[plane, 1], (two_s.at[1], two_r.at[1]), plane, partner
        )

    def transform(group):
        count = len(group)
        value = jnp.concatenate([dbuf[plane] for plane in group], axis=0)
        value = times_table(value, tab.at[0:2])
        value = jnp.concatenate([value[index * rows : (index + 1) * rows] for index in range(count)], axis=1)
        value = table_times(tab.at[2:4], value)
        for index, plane in enumerate(group):
            ybuf[plane, 0] = value[:, index * cols : index * cols + lanes]
            ybuf[plane, 1] = value[:, index * cols + lanes : (index + 1) * cols]
            hop_one(plane).start()

    def merge(plane):
        hop_one(plane).wait_recv()
        ybuf[plane, core] = ybuf[plane, core] + rone[plane]
        hop_pass(plane).start()
        hop_two(plane).start()

    inside = list(range(3, planes - 1))
    outside = [0, planes + 1, 1, 2, planes - 1, planes]
    pieces = ((0, len(inside) * per), (len(inside) * per, len(outside) * per))
    sent_rows = (planes + 2) * per

    def spread(plane, side, value):
        group = inside if plane in inside else outside
        first_row = (0 if plane in inside else pieces[1][0]) + group.index(plane) * per
        for row in range(per):
            abuf[side, pl.ds(first_row + row, layer, stride=sent_rows), :] = value[row * layer : (row + 1) * layer]

    def relay(plane):
        hop_pass(plane).wait_recv()
        spread(plane, 1, ybuf[plane, core, quarter(1 - zlow, 1 - zhigh)] + rtwo[plane, 1])

    def settle(plane):
        hop_two(plane).wait_recv()
        spread(plane, 0, ybuf[plane, core, quarter(zlow, zhigh)] + rtwo[plane, 0])

    def in_from(place_of, piece):
        start, length = pieces[piece]
        return pl.ds(pl.multiple_of(place_of * sent_rows + start, 8), length)

    def in_rows(place_of, piece, which):
        start, length = pieces[piece]
        return pl.ds(pl.multiple_of(place_of * (2 * sent_rows) + 2 * start + which * length, 8), length)

    def in_copy(step, piece, side, here):
        source = abuf.at[side, in_from(spot_after(step), piece)]
        peer = layer_peer(step) if side == 0 else other_peer(step)
        return remote(source, rin.at[here], (in_s.at[piece, side], in_r.at[piece, side]), step, peer)

    def in_start(piece, side):
        def start(step, carry):
            in_copy(step, piece, side, in_rows(spot, piece, zhigh)).start()
            return carry

        lax.fori_loop(1 - side, layer, start, 0)
        if side == 0:
            rin[in_rows(spot, piece, zhigh)] = abuf[0, in_from(spot, piece)]

    def in_sent(piece, side):
        def finish(step, carry):
            in_copy(step, piece, side, in_rows(spot, piece, zhigh)).wait_send()
            return carry

        lax.fori_loop(1 - side, layer, finish, 0)

    def in_finish(piece):
        for side in range(2):
            def finish(step, carry):
                place_of = lax.rem(spot + layer - step, layer)
                which = zhigh if side == 0 else 1 - zhigh
                in_copy(step, piece, side, in_rows(place_of, piece, which)).wait_recv()
                return carry

            lax.fori_loop(1 - side, layer, finish, 0)

    def loop(low, high, body):
        def step(index, carry):
            body(index)
            return carry

        lax.fori_loop(low, high, step, 0)

    def both(body, low, high):
        def step(index, carry):
            body(jnp.where(index == 0, low, high))
            return carry

        lax.fori_loop(0, 2, step, 0)

    fwd = (fwd_s, fwd_r)
    forwards = [
        remote(ghosts.at[index, mine], ghosts.at[index, mine], fwd, number * 2 + index, sibling)
        for number, ghosts in enumerate((ghost_in, level_in))
        for index in range(2)
    ]
    loop(1, planes + 1, widen)
    loop(2, planes, first)
    loop(3, planes - 1, last)
    for copy in copies[2:]:
        copy.wait()
    for copy in forwards:
        copy.start()
    transform(inside)
    pl.semaphore_wait(ready.at[0], 3)
    pl.semaphore_signal(ready.at[1], inc=1, device_id=across, device_id_type=MESH)
    for copy in copies[:2]:
        copy.wait()
    for copy in forwards:
        copy.wait()
    widen(0, 0)
    widen(planes + 1, 1)
    pairs(0, (0, 1, 2))
    pairs(planes + 1, (planes - 1, planes, planes + 1))
    loop(3, planes - 1, merge)
    transform([0, planes + 1])
    both(first, 1, planes)
    both(merge, 0, planes + 1)
    both(last, 2, planes - 1)
    transform([2, planes - 1])
    both(merge, 2, planes - 1)
    level(0, 0)
    level(planes + 1, 1)
    first(0, (1,))
    first(planes + 1, (-1,))
    both(last, 1, planes)
    transform([1, planes])
    for plane in inside:
        relay(plane)
    pl.semaphore_wait(ready.at[1], 1)
    in_start(0, 1)
    for plane in inside:
        settle(plane)
    in_start(0, 0)

    mom = (mom_s, mom_r)
    for order in range(3):
        strip = jnp.sum(mbuf[0, pl.ds(8 * order, 8)], axis=0, keepdims=True)
        total = jnp.sum(strip, axis=1, keepdims=True)
        mbuf[1, pl.ds(order, 1)] = jnp.broadcast_to(total, (1, cols))
    swap = remote(mbuf.at[1, 0:8], mbuf.at[2, 0:8], mom, 0, sibling)
    swap.start()
    for plane in (0, planes + 1, 2, planes - 1):
        relay(plane)
        settle(plane)
    both(merge, 1, planes)
    swap.wait()
    mbuf[3, 0:8] = mbuf[1, 0:8] + mbuf[2, 0:8]
    swap = remote(mbuf.at[3, 0:8], mbuf.at[4, 0:8], mom, 1, partner)
    swap.start()
    relay(1)
    relay(planes)
    in_start(1, 1)
    settle(1)
    settle(planes)
    in_start(1, 0)
    swap.wait()
    mbuf[5, 0:8] = mbuf[3, 0:8] + mbuf[4, 0:8]
    swap = remote(mbuf.at[5, 0:8], mbuf.at[6, 0:8], mom, 2, across)
    swap.start()

    wave_z = signed(lax.broadcasted_iota(jnp.int32, (depth, lanes), 0), depth)
    wave_x = signed(lax.broadcasted_iota(jnp.int32, (depth, lanes), 1) + core * lanes, cols)
    base = wave_z * wave_z + wave_x * wave_x
    for row in range(per):
        number = (2 * zlow + zhigh) * fourth + row * layer + spot
        wave_y = signed(jnp.full((depth, lanes), number, jnp.int32), rows)
        summed = base + wave_y * wave_y
        value = (4.0 * math.pi / (8.0 * depth * rows * cols)) / (summed + SCREEN * SCREEN)
        kern[:, row * lanes : (row + 1) * lanes] = jnp.where(summed == 0.0, 0.0, value)
    loads[4].wait()

    def moment_round(number, stride):
        where = lax.rem(slab // stride, 4)
        copies, waits = [], []
        for step in range(1, 4):
            peer = {"probe": probe, "slab": slab + (lax.rem(where + step, 4) - where) * stride}
            source = lax.rem(where + 4 - step, 4)
            sems = (mslot_s.at[number], mslot_r.at[number])
            copies.append(remote(mslots.at[number, where], mslots.at[number, where], sems, step, peer))
            waits.append(remote(mslots.at[number, source], mslots.at[number, source], sems, step, peer))
        return where, copies, waits

    def moment_start(number, stride, value):
        where, copies, waits = moment_round(number, stride)
        mslots[number, where] = value
        for copy in copies:
            copy.start()

    def moment_finish(number, stride):
        where, copies, waits = moment_round(number, stride)
        for copy in waits:
            copy.wait_recv()
        for copy in copies:
            copy.wait_send()
        return (mslots[number, 0] + mslots[number, 1]) + (mslots[number, 2] + mslots[number, 3])

    in_finish(0)
    swap.wait()
    moment_start(0, 1, (mbuf[5, 0:8] + mbuf[6, 0:8])[:, :128])
    in_finish(1)
    came = 2 * (planes + 2) * layer
    columns = jnp.concatenate([rin[pl.ds(row, came, stride=per), :] for row in range(per)], axis=1)
    here = lax.broadcasted_iota(jnp.int32, (1, per * lanes), 1) + (probe + slab) * (per * lanes)
    mean = jnp.where(here == 0, jnp.sum(columns, axis=0, keepdims=True) * (1.0 / depth), 0.0)
    number = lax.rem(lax.broadcasted_iota(jnp.int32, (came, per * lanes), 0), 2 * (planes + 2))
    count = len(inside)
    number = number - 2 * count
    number = jnp.where(number >= len(outside), number - len(outside), number)
    columns = jnp.where((number == 0) | (number == 1), columns, columns - mean)
    columns = table_times((ztab[0, :, :came], ztab[1, :, :came]), columns) * kern[...]
    columns = table_times((ztab[2, :, :depth], ztab[3, :, :depth]), columns)
    for row in range(per):
        rout[pl.ds(row, depth, stride=per), :] = columns[:, row * lanes : (row + 1) * lanes]

    piece = planes // 2 * per
    own_quarter = 2 * zlow + zhigh
    far_quarter = 2 * (1 - zlow) + (1 - zhigh)

    def out_rows(place_of, side, part):
        which = zhigh if side == 0 else 1 - zhigh
        return pl.ds(pl.multiple_of(place_of * size + which * (size // 2) + part * piece, piece), piece)

    def landing(side, part, place_of):
        rows_at = pl.ds(pl.multiple_of(place_of * piece, piece), piece)
        return quads.at[own_quarter, part, rows_at] if side == 0 else hold.at[part, rows_at]

    def out_copy(step, side, part, place_of):
        source = rout.at[out_rows(spot_after(step), side, part)]
        sems = (out_s.at[side, part], out_r.at[side, part])
        return remote(source, landing(side, part, place_of), sems, step, layer_peer(step))

    def out_start(side, part):
        def start(step, carry):
            out_copy(step, side, part, spot).start()
            return carry

        lax.fori_loop(1, layer, start, 0)
        target = landing(side, part, spot)
        target[...] = rout[out_rows(spot, side, part)]

    def out_finish(side, part):
        def finish(step, carry):
            out_copy(step, side, part, spot_after(layer - step)).wait_recv()
            return carry

        lax.fori_loop(1, layer, finish, 0)

    def out_sent():
        def finish(step, carry):
            for side in range(2):
                for part in range(2):
                    out_copy(step, side, part, spot).wait_send()
            return carry

        lax.fori_loop(1, layer, finish, 0)

    def to_partner(part):
        return remote(quads.at[own_quarter, part], quads.at[own_quarter, part], (near_s, near_r), part, partner)

    def to_across(part):
        return remote(hold.at[part], quads.at[own_quarter, part], (far_s, far_r), part, across)

    def pass_on(part):
        return remote(quads.at[far_quarter, part], quads.at[far_quarter, part], (relay_s, relay_r), part, partner)

    for part in range(2):
        out_start(0, part)
        out_start(1, part)
    moments = moment_finish(0, 1)
    moment_start(1, 8, moments)

    def drain(plane):
        hop_one(plane).wait_send()
        hop_two(plane).wait_send()
        hop_pass(plane).wait_send()

    loop(0, planes + 2, drain)
    for piece_number in range(2):
        for side in range(2):
            in_sent(piece_number, side)
    for part in range(2):
        out_finish(0, part)
        to_partner(part).start()
        out_finish(1, part)
        to_across(part).start()
    moment_ref[...] = moment_finish(1, 8)
    for part in range(2):
        to_across(part).wait_recv()
        pass_on(part).start()

    def share(part, pair):
        slot = 4 * core + 2 * part + pair
        return remote(pot.at[slot], pot.at[slot], (e_s, e_r), 2 * part + pair, sibling)

    def invert(part):
        to_partner(part).wait_recv()
        pass_on(part).wait_recv()
        for pair in range(2):
            columns = []
            for plane in (2 * pair, 2 * pair + 1):
                blocks = [
                    quads[which, part, pl.ds(plane * per + row, layer, stride=piece), :]
                    for which in range(4)
                    for row in range(per)
                ]
                columns.append(jnp.concatenate(blocks, axis=0))
            pot[4 * core + 2 * part + pair] = table_times(tab.at[0:2], jnp.concatenate(columns, axis=1))
            share(part, pair).start()

    def finish(part):
        for pair in range(2):
            share(part, pair).wait_recv()
            sides = [pot[4 * side + 2 * part + pair] for side in range(2)]
            value = [
                jnp.concatenate([side[:, plane * lanes : (plane + 1) * lanes] for side in sides], axis=1)
                for plane in range(2)
            ]
            value = times_table(jnp.concatenate(value, axis=0), tab.at[0:2])
            for plane in range(2):
                out_ref[part * (planes // 2) + 2 * pair + plane] = value[plane * rows : (plane + 1) * rows]

    invert(0)
    finish(0)
    out_sent()
    invert(1)
    finish(1)
    for part in range(2):
        to_partner(part).wait_send()
        to_across(part).wait_send()
        pass_on(part).wait_send()
        for pair in range(2):
            share(part, pair).wait_send()


def per_device(probes, potential, potential_change, coefficients):
    panel, planes, rows, cols = probes.shape
    slabs = lax.axis_size("slab")
    layer = slabs // 2
    depth = planes * slabs
    half = rows // 2
    fourth = rows // 4
    size = 2 * planes * (fourth // layer)
    vmem = pl.BlockSpec(memory_space=pltpu.VMEM)
    anywhere = pl.BlockSpec(memory_space=pl.ANY)
    dma = pltpu.SemaphoreType.DMA
    high, low = cas_split(rows)
    order = shuffle(rows)
    forward = tables((high, low), (high[:, order], low[:, order]))
    high, low = cas_split(depth)
    spots = np.arange(layer)[:, None, None, None] // 4 * 8 + np.arange(layer)[:, None, None, None] % 4
    halves = np.arange(2)[None, None, :, None] * 4
    inner = [list(range(2, planes - 2)), [-1, planes, 0, 1, planes - 2, planes - 1]]
    came = [
        (np.arange(layer)[:, None, None] // 4 * 8 + np.arange(layer)[:, None, None] % 4 + halves[0, 0]) * planes
        + np.array(group)
        for group in inner
    ]
    came = np.concatenate([part.reshape(layer, -1) for part in came], axis=1).reshape(-1) % depth
    goes = ((spots[:, 0] + halves[:, 0]) * planes + np.arange(planes)).reshape(-1)
    extra = np.zeros((depth, len(came) - depth), high.dtype)
    back = [np.concatenate([part[goes], extra], axis=1) for part in (high, low)]
    deep = tables((high[:, came], low[:, came]), back)
    tall = rows + 2 * PAD
    hartree_change, total = pl.pallas_call(
        functools.partial(response_kernel, slabs, layer),
        out_shape=(
            pltpu.VMEM((planes, rows, cols), F32),
            jax.ShapeDtypeStruct((8, 128), F32),
        ),
        in_specs=[pl.BlockSpec(memory_space=pltpu.SMEM)] + [anywhere] * 5,
        out_specs=(vmem, vmem),
        scratch_shapes=[
            pltpu.VMEM((4, rows, cols), BF16),
            pltpu.VMEM((panel, planes + 2, rows, cols), BF16),
            pltpu.VMEM((planes, rows, cols), F32),
            pltpu.VMEM((planes, rows, cols), F32),
            pltpu.VMEM((2, rows, cols), F32),
            pltpu.VMEM((2, half, cols), BF16),
            pltpu.VMEM((2, rows, cols), BF16),
            pltpu.VMEM((planes + 2, 2, rows, 128), F32),
            pltpu.VMEM((planes + 2, 2, rows, 128), F32),
            pltpu.VMEM((panel, planes + 2, 2, tall, 128), F32),
            pltpu.VMEM((panel, planes + 2, 2, tall, 128), F32),
            pltpu.VMEM((panel, planes + 2, 2, tall, 128), F32),
            pltpu.VMEM((panel, planes + 2, 2, tall, 128), F32),
            pltpu.VMEM((planes + 2, rows, cols), F32),
            pltpu.VMEM((planes + 2, 2, rows, 128), F32),
            pltpu.VMEM((planes + 2, rows, 128), F32),
            pltpu.VMEM((planes + 2, 2, fourth, 128), F32),
            pltpu.VMEM((7, 24, cols), F32),
            pltpu.VMEM((4, depth, len(came)), BF16),
            pltpu.VMEM((2, len(came) // 2 * 4, 128), F32),
            pltpu.VMEM((len(came) * 4, 128), F32),
            pltpu.VMEM((depth, 4 * 128), F32),
            pltpu.VMEM((layer * size, 128), F32),
            pltpu.VMEM((2, layer * size // 4, 128), F32),
            pltpu.VMEM((4, 2, layer * size // 4, 128), F32),
            pltpu.VMEM((2, 4, 8, 128), F32),
            dma((5,)),
            dma((6,)), dma((6,)),
            dma((4,)), dma((4,)),
            dma((planes + 2,)), dma((planes + 2,)),
            dma((2, planes + 2)), dma((2, planes + 2)),
            dma((3,)), dma((3,)),
            dma((2, 2, layer)), dma((2, 2, layer)),
            dma((2, 2, layer)), dma((2, 2, layer)),
            dma((2,)), dma((2,)),
            dma((2,)), dma((2,)),
            dma((2,)), dma((2,)),
            dma((4,)), dma((4,)),
            dma((2, 4)), dma((2, 4)),
            pltpu.SemaphoreType.REGULAR((2,)),
        ],
        compiler_params=pltpu.CompilerParams(
            collective_id=0, has_side_effects=True, vmem_limit_bytes=56 * 1024 * 1024
        ),
        name="response",
    )(coefficients, forward, deep, probes, potential, potential_change)
    weights = jnp.array([1.0, 2.0, 1.0], F32) / (panel * lax.axis_size("probe") * depth * rows * cols)
    return hartree_change, total[:3, 0] * weights


def solution(mesh):
    return jax.shard_map(
        per_device,
        mesh=mesh,
        in_specs=(
            P("probe", "slab", None, None),
            P("slab", None, None),
            P("slab", None, None),
            P(),
        ),
        out_specs=(P("slab", None, None), P()),
        check_vma=False,
    )
```
